32 devices in a mesh: ctx: 8 (over z, y), head: 4 (over x, core).
Axes of the slice: x: 2, y: 2, z: 4, core: 2. Of those that a mesh axis runs over, the one named last changes fastest.
Arguments:
- lin_q: bfloat16 [1024, 32, 128], P('ctx', 'head'), may hold values from -4 to 4
- lin_k: bfloat16 [1024, 32, 128], P('ctx', 'head'), may hold values from -4 to 4
- lin_v: bfloat16 [1024, 32, 128], P('ctx', 'head'), may hold values from -16 to 16
- lin_decay: float32 [32, 1024], P('head', 'ctx'), may hold values from -1.5 to 0
- norm_gain: float32 [32, 128], P('head'), may hold values from 0.1 to 1.9
- soft_q: bfloat16 [1024, 32, 128], P('ctx', 'head'), may hold values from -5 to 5
- soft_k: bfloat16 [1024, 32, 128], P('ctx', 'head'), may hold values from -5 to 5
- soft_v: bfloat16 [1024, 32, 128], P('ctx', 'head'), may hold values from -5 to 5
- out_grad: bfloat16 [1024, 32, 128], P('ctx', 'head'), may hold values from -5 to 5
- block_lists: int32 [8, 16], P('ctx'), may hold values from 0 to 6, as said below
- block_counts: int32 [8], P('ctx'), may hold values from 0 to 7, as said below
Outputs:
- lin_dq: bfloat16 [1024, 32, 128], P('ctx', 'head')
- lin_dk: bfloat16 [1024, 32, 128], P('ctx', 'head')
- lin_dv: bfloat16 [1024, 32, 128], P('ctx', 'head')
- soft_dq: bfloat16 [1024, 32, 128], P('ctx', 'head')
- soft_dk: bfloat16 [1024, 32, 128], P('ctx', 'head')
- soft_dv: bfloat16 [1024, 32, 128], P('ctx', 'head')
The draws below stay inside these ranges and needn't reach their ends.
Inputs may be any that keep to these rules, and one draw needn't show every extreme that they name: `block_lists`: entries past block_counts[b] are 0. The first block_counts[b] entries of query block b are distinct blocks that lie before the span of 128 tokens holding b. All query blocks of one span name together at most one block of each other span. In every span after the first, some query block names every block that its span names; from the second span on these include block 0, and from the third on also the last block before the span. `block_counts`: in span i of 128 tokens some query block has the count min(i, 16); every count is at most that; counts are 0 only in the first span.
All inputs are finite; a program needn't handle non-finite values.
Results may differ from the reference program's by a relative error of at most 0.011.
Values may be sent and summed in bfloat16 or wider, within the bound.
No kernel may reach another device: no remote copies, remote signals or barrier semaphores. Data moves between devices by JAX's collectives and lax.ppermute only.
A program may use at most 128 MiB of HBM per device.

```python
import math
import jax
import jax.numpy as jnp
from jax import lax

H = 32
HD = 128
BLK = 128
NSEL = 16
TOK_DEV = 128
TOKENS = 1024
QB_DEV = 1
NQB = 8
N_CTX = 8


def draw_lin_v(key, part):
    base_key = jax.random.fold_in(key, 41)
    first_key = jax.random.fold_in(base_key, 0)
    ramp = jnp.arange(H, dtype=jnp.float32) / max(H - 1, 1)
    shape = (TOKENS, H, HD)
    values = jax.random.truncated_normal(first_key, -4.0, 4.0, shape, jnp.float32) * (3.0 ** ramp)[None, :, None]
    return values.astype(jnp.bfloat16)


def draw_lin_decay(key, part):
    base_key = jax.random.fold_in(key, 11)
    keys_here = jax.random.split(base_key, 7)
    slow_share = 0.5
    slow = jax.random.bernoulli(keys_here[0], slow_share, (H,))
    slow_rate = jnp.exp(jax.random.uniform(keys_here[1], (H,), jnp.float32, math.log(8e-06), math.log(4e-05)))
    fast_rate = jnp.exp(jax.random.uniform(keys_here[2], (H,), jnp.float32, math.log(0.02), math.log(0.035)))
    base_rate = jnp.where(slow, slow_rate, fast_rate)
    span_total = TOKENS // TOK_DEV
    span_factor = jnp.exp(jax.random.uniform(keys_here[3], (H, span_total), jnp.float32, math.log(0.6), math.log(1.7)))
    token_factor = jnp.exp(jax.random.uniform(keys_here[4], (H, TOKENS), jnp.float32, math.log(0.7), math.log(1.4)))
    decay_speed = base_rate[:, None] * jnp.repeat(span_factor, TOK_DEV, axis=1) * token_factor
    slot_spots = jax.random.randint(keys_here[5], (2,), 0, TOKENS)
    loss_values = jax.random.uniform(keys_here[6], (H, 2), jnp.float32, 0.22, 0.69)
    token_offsets = jnp.arange(TOKENS)
    spike_factor = jnp.where(token_offsets[None, :] == slot_spots[0], loss_values[:, 0:1], 0.0) + jnp.where(token_offsets[None, :] == slot_spots[1], loss_values[:, 1:2], 0.0)
    return (-decay_speed - spike_factor).astype(jnp.float32)


def drawn_pairs(key):
    base_key = jax.random.fold_in(key, 23)
    first_key, second_key = jax.random.split(base_key, 2)
    shape = (TOKENS, H, HD)
    queries = jax.random.truncated_normal(first_key, -4.5, 4.5, shape, jnp.float32)
    keys_drawn = jax.random.truncated_normal(second_key, -4.5, 4.5, shape, jnp.float32)
    return (queries, keys_drawn)


def draw_soft_q(key, part):
    return drawn_pairs(key)[0].astype(jnp.bfloat16)


def draw_soft_k(key, part):
    return drawn_pairs(key)[1].astype(jnp.bfloat16)


def span_routes(key):
    base_key = jax.random.fold_in(key, 31)
    span_total = TOKENS // TOK_DEV

    def one_span(span_index):
        keys_here = jax.random.split(jax.random.fold_in(base_key, span_index), 5)
        shuffled = jax.random.permutation(keys_here[0], span_total).astype(jnp.int32)
        usable = (shuffled >= 1) & (shuffled < span_index - 1)
        order = jnp.argsort(jnp.where(usable, 0, 1), stable=True)
        others = jnp.concatenate([shuffled[order], jnp.zeros((NSEL,), jnp.int32)])[:NSEL - 2]
        owners = jnp.concatenate([jnp.zeros((1,), jnp.int32), jnp.reshape(span_index - 1, (1,)).astype(jnp.int32), others])
        picked_blocks = jax.random.randint(keys_here[1], (NSEL,), 0, QB_DEV).astype(jnp.int32)
        picked_blocks = picked_blocks.at[0].set(0).at[1].set(QB_DEV - 1)
        block_ids = owners * QB_DEV + picked_blocks
        live_total = jnp.minimum(span_index, NSEL)
        counts = jax.random.randint(keys_here[2], (QB_DEV,), 0, NSEL) % jnp.maximum(live_total, 1) + 1
        full_one = jax.random.randint(keys_here[3], (), 0, QB_DEV)
        counts = jnp.where(jnp.arange(QB_DEV) == full_one, live_total, counts)
        counts = jnp.where(live_total == 0, 0, counts).astype(jnp.int32)

        def one_block(sub_key, count_here):
            ranking = jax.random.permutation(sub_key, NSEL).astype(jnp.int32)
            inside = ranking < live_total
            ranked = ranking[jnp.argsort(jnp.where(inside, 0, 1), stable=True)]
            return jnp.where(jnp.arange(NSEL) < count_here, block_ids[ranked], 0)
        block_keys = jax.random.split(keys_here[4], QB_DEV)
        lists = jax.vmap(one_block)(block_keys, counts)
        return (lists, counts)
    lists, counts = jax.vmap(one_span)(jnp.arange(span_total, dtype=jnp.int32))
    return (lists.reshape(NQB, NSEL).astype(jnp.int32), counts.reshape(NQB).astype(jnp.int32))


def draw_block_lists(key, part):
    return span_routes(key)[0]


def draw_block_counts(key, part):
    return span_routes(key)[1]


def shard_levels(key, extent, cuts, low, top_value):
    level = 1.0
    for dim, shards_of in cuts:
        steps = jax.random.uniform(jax.random.fold_in(jax.random.fold_in(key, 6), dim), (shards_of,), jnp.float32, low / len(cuts), top_value / len(cuts))
        level = level * jnp.repeat(jnp.exp(steps), extent[dim] // shards_of).reshape((-1,) + (1,) * (len(extent) - 1 - dim))
    return level


def centred(key, shape, scale, limit, pieces=(), held_as=jnp.bfloat16):
    values = jax.random.normal(key, shape, jnp.float32) * scale
    if len(pieces) > 0:
        values = shard_levels(key, shape, pieces, -0.22, 0.18) * values
    return jnp.clip(values, min=-limit, max=limit).astype(held_as)


def setup_inputs(seed: int = 0) -> dict:
    streams_of = jax.random.split(jax.random.key(seed), 12)
    return {
        "lin_q": centred(streams_of[0], (TOKENS, H, HD), 1.0, 4.0, ((0, 8), (1, 4))),
        "lin_k": centred(streams_of[1], (TOKENS, H, HD), 1.0, 4.0, ((0, 8), (1, 4))),
        "lin_v": draw_lin_v(jax.random.fold_in(streams_of[11], 71), 0),
        "lin_decay": draw_lin_decay(jax.random.fold_in(streams_of[11], 71), 0),
        "norm_gain": jnp.clip(1.0 + 0.18 * jax.random.normal(streams_of[4], (H, HD), jnp.float32), 0.1, 1.9),
        "soft_q": draw_soft_q(jax.random.fold_in(streams_of[11], 71), 0),
        "soft_k": draw_soft_k(jax.random.fold_in(streams_of[11], 71), 0),
        "soft_v": centred(streams_of[7], (TOKENS, H, HD), 1.0, 5.0, ((0, 8), (1, 4))),
        "out_grad": centred(streams_of[8], (TOKENS, H, HD), 1.0, 5.0, ((0, 8), (1, 4))),
        "block_lists": draw_block_lists(jax.random.fold_in(streams_of[11], 71), 0),
        "block_counts": draw_block_counts(jax.random.fold_in(streams_of[11], 71), 0),
    }


epsilon = 1e-05
exact_precision = lax.Precision.HIGHEST

def decay_tables(decays):
    running = jnp.cumsum(decays, axis=1)
    finish = running[:, -1]
    length = decays.shape[1]
    below_diag = (jnp.arange(length)[:, None] >= jnp.arange(length)[None, :])[None]
    spread = running[:, :, None] - running[:, None, :]
    within = jnp.where(below_diag, jnp.exp(jnp.where(below_diag, spread, 0.0)), 0.0)
    return (jnp.exp(finish), jnp.exp(finish[:, None] - running), jnp.exp(running), within)

def sparse_grads(queries, grads_out, key_rows, value_rows, allowed):
    score_scale = queries.shape[-1] ** (-0.5)
    scores = jnp.einsum('bqhd,bkhd->bhqk', queries.astype(jnp.float32), key_rows.astype(jnp.float32)) * score_scale
    key_mask = allowed[:, None]
    scores = jnp.where(key_mask, scores, -1e+30)
    row_max = lax.optimization_barrier(jnp.max(scores, axis=-1, keepdims=True))
    weights = jnp.where(key_mask, jnp.exp(scores - row_max), 0.0)
    softmax_probs = weights / lax.optimization_barrier(jnp.sum(weights, axis=-1, keepdims=True))
    rounded = softmax_probs.astype(jnp.bfloat16)
    outputs = jnp.einsum('bhqk,bkhd->bqhd', rounded.astype(jnp.float32), value_rows.astype(jnp.float32))
    row_delta = lax.optimization_barrier(jnp.sum(grads_out.astype(jnp.float32) * outputs, axis=-1))
    grad_probs = jnp.einsum('bqhd,bkhd->bhqk', grads_out.astype(jnp.float32), value_rows.astype(jnp.float32))
    grad_scores = (softmax_probs * (grad_probs - jnp.transpose(row_delta, (0, 2, 1))[..., None])).astype(jnp.bfloat16)
    query_gradient = jnp.einsum('bhqk,bkhd->bqhd', grad_scores.astype(jnp.float32), key_rows.astype(jnp.float32)) * score_scale
    key_gradient = jnp.einsum('bhqk,bqhd->bkhd', grad_scores.astype(jnp.float32), queries.astype(jnp.float32)) * score_scale
    value_gradient = jnp.einsum('bhqk,bqhd->bkhd', rounded.astype(jnp.float32), grads_out.astype(jnp.float32))
    return (query_gradient, key_gradient, value_gradient)

def reference(lin_q, lin_k, lin_v, lin_decay, norm_gain, soft_q, soft_k, soft_v, out_grad, block_lists, block_counts):
    query_spans = lin_q.astype(jnp.float32).reshape(N_CTX, TOK_DEV, H, HD)
    key_spans = lin_k.astype(jnp.float32).reshape(N_CTX, TOK_DEV, H, HD)
    value_spans = lin_v.astype(jnp.float32).reshape(N_CTX, TOK_DEV, H, HD)
    decay_spans = jnp.transpose(lin_decay.reshape(H, N_CTX, TOK_DEV), (1, 0, 2))

    def forward_step(carried_state, slices):
        current_query, current_key, current_value, decay_here = slices
        carry_decay, trailing_decay, leading_decay, within = decay_tables(decay_here)
        pair_weights = jnp.einsum('thk,shk->hts', current_query, current_key, precision=exact_precision) * within
        span_output = jnp.einsum('hts,shv->thv', pair_weights, current_value, precision=exact_precision)
        span_output = span_output + leading_decay.T[:, :, None] * jnp.einsum('wfg,fgl->wfl', current_query, carried_state, precision=exact_precision)
        segment_state = jnp.einsum('boz,bor->ozr', current_key * trailing_decay.T[:, :, None], current_value, precision=exact_precision)
        return (carry_decay[:, None, None] * carried_state + segment_state, (carried_state, span_output))
    zero_state = jnp.zeros((H, HD, HD), jnp.float32)
    _, (states_in, span_outs) = lax.scan(forward_step, zero_state, (query_spans, key_spans, value_spans, decay_spans))
    layer_out = span_outs.reshape(TOKENS, H, HD)
    root_mean = jnp.sqrt(lax.optimization_barrier(jnp.sum(layer_out * layer_out, axis=(1, 2))) / (H * HD) + epsilon)
    query_blocks = soft_q.reshape(NQB, BLK, H, HD)
    key_blocks = soft_k.reshape(NQB, BLK, H, HD)
    value_blocks = soft_v.reshape(NQB, BLK, H, HD)
    grad_blocks = out_grad.reshape(NQB, BLK, H, HD)
    span_lists = block_lists.reshape(N_CTX, QB_DEV, NSEL)
    span_counts = block_counts.reshape(N_CTX, QB_DEV)
    causal = jnp.arange(BLK)[:, None] >= jnp.arange(BLK)[None, :]
    entries = QB_DEV * NSEL

    def sparse_step(accum, span_index):
        acc_key, acc_value = accum
        first = (span_index * QB_DEV).astype(jnp.int32)
        query_rows = lax.dynamic_slice_in_dim(query_blocks, first, QB_DEV, 0)
        grad_rows = lax.dynamic_slice_in_dim(grad_blocks, first, QB_DEV, 0)
        own_keys = lax.dynamic_slice_in_dim(key_blocks, first, QB_DEV, 0)
        own_values = lax.dynamic_slice_in_dim(value_blocks, first, QB_DEV, 0)
        my_lists = span_lists[span_index]
        my_counts = span_counts[span_index]
        my_live = jnp.arange(NSEL)[None, :] < my_counts[:, None]
        listed_keys = key_blocks[my_lists].reshape(QB_DEV, NSEL * BLK, H, HD)
        listed_values = value_blocks[my_lists].reshape(QB_DEV, NSEL * BLK, H, HD)
        key_rows = jnp.concatenate([own_keys, listed_keys], axis=1)
        value_rows = jnp.concatenate([own_values, listed_values], axis=1)
        remote_mask = jnp.broadcast_to(jnp.repeat(my_live, BLK, axis=1)[:, None, :], (QB_DEV, BLK, NSEL * BLK))
        allowed = jnp.concatenate([jnp.broadcast_to(causal, (QB_DEV, BLK, BLK)), remote_mask], axis=2)
        query_gradient, key_gradient, value_gradient = sparse_grads(query_rows, grad_rows, key_rows, value_rows, allowed)
        flat_ids = my_lists.reshape(entries)
        flat_live = my_live.reshape(entries)
        flat_owner = flat_ids // QB_DEV
        segment = jnp.where(flat_live, flat_owner, N_CTX).astype(jnp.int32)
        remote_key = key_gradient[:, BLK:].reshape(entries, BLK, H, HD)
        remote_value = value_gradient[:, BLK:].reshape(entries, BLK, H, HD)
        part_key = jax.ops.segment_sum(remote_key, segment, num_segments=N_CTX + 1)[:N_CTX].astype(jnp.bfloat16)
        part_value = jax.ops.segment_sum(remote_value, segment, num_segments=N_CTX + 1)[:N_CTX].astype(jnp.bfloat16)
        part_key = lax.optimization_barrier(part_key).astype(jnp.float32)
        part_value = lax.optimization_barrier(part_value).astype(jnp.float32)
        owners = jnp.arange(N_CTX, dtype=jnp.int32)
        matches = flat_live[None, :] & (flat_owner[None, :] == owners[:, None])
        target = lax.optimization_barrier(jnp.max(jnp.where(matches, flat_ids[None, :], -1), axis=1))
        dest = jnp.where(target >= 0, target, NQB).astype(jnp.int32)
        acc_key = acc_key.at[dest].add(part_key)
        acc_value = acc_value.at[dest].add(part_value)
        return ((acc_key, acc_value), (query_gradient, key_gradient[:, :BLK], value_gradient[:, :BLK]))
    empty = jnp.zeros((NQB + 1, BLK, H, HD), jnp.float32)
    (acc_key, acc_value), (query_gradient, own_key, own_value) = lax.scan(sparse_step, (empty, empty), jnp.arange(N_CTX, dtype=jnp.int32))
    soft_dq = query_gradient.reshape(TOKENS, H, HD).astype(jnp.bfloat16)
    soft_dk = (own_key.reshape(TOKENS, H, HD) + acc_key[:NQB].reshape(TOKENS, H, HD)).astype(jnp.bfloat16)
    value_total = own_value.reshape(TOKENS, H, HD) + acc_value[:NQB].reshape(TOKENS, H, HD)
    soft_dv = value_total.astype(jnp.bfloat16)
    cotangent = out_grad.astype(jnp.float32) + value_total
    scaled = norm_gain[None] * cotangent
    inner = lax.optimization_barrier(jnp.sum(scaled * layer_out, axis=(1, 2)))
    linear_cotangent = scaled / root_mean[:, None, None] - layer_out * (inner / (H * HD * root_mean ** 3))[:, None, None]
    cot_spans = linear_cotangent.reshape(N_CTX, TOK_DEV, H, HD)

    def backward_step(carried_state, slices):
        current_query, current_key, current_value, decay_here, local_cotangent, incoming_state = slices
        carry_decay, trailing_decay, leading_decay, within = decay_tables(decay_here)
        grad_pair = jnp.einsum('thv,shv->hts', local_cotangent, current_value, precision=exact_precision) * within
        pair_weights = jnp.einsum('thk,shk->hts', current_query, current_key, precision=exact_precision) * within
        query_gradient = jnp.einsum('hts,shk->thk', grad_pair, current_key, precision=exact_precision)
        query_gradient = query_gradient + leading_decay.T[:, :, None] * jnp.einsum('fqs,qrs->fqr', local_cotangent, incoming_state, precision=exact_precision)
        key_gradient = jnp.einsum('hts,thk->shk', grad_pair, current_query, precision=exact_precision)
        key_gradient = key_gradient + trailing_decay.T[:, :, None] * jnp.einsum('fut,ujt->fuj', current_value, carried_state, precision=exact_precision)
        value_gradient = jnp.einsum('hts,thv->shv', pair_weights, local_cotangent, precision=exact_precision)
        value_gradient = value_gradient + trailing_decay.T[:, :, None] * jnp.einsum('zpu,pux->zpx', current_key, carried_state, precision=exact_precision)
        segment_state = jnp.einsum('boz,bor->ozr', current_query * leading_decay.T[:, :, None], local_cotangent, precision=exact_precision)
        return (segment_state + carry_decay[:, None, None] * carried_state, (query_gradient, key_gradient, value_gradient))
    _, (lin_dq, lin_dk, lin_dv) = lax.scan(backward_step, zero_state, (query_spans, key_spans, value_spans, decay_spans, cot_spans, states_in), reverse=True)
    lin_dq = lin_dq.reshape(TOKENS, H, HD).astype(jnp.bfloat16)
    lin_dk = lin_dk.reshape(TOKENS, H, HD).astype(jnp.bfloat16)
    lin_dv = lin_dv.reshape(TOKENS, H, HD).astype(jnp.bfloat16)
    return (lin_dq, lin_dk, lin_dv, soft_dq, soft_dk, soft_dv)
```

```python
import functools

import jax
import jax.numpy as jnp
from jax import lax
from jax.experimental import pallas as pl
from jax.experimental.pallas import tpu as pltpu
from jax.sharding import PartitionSpec as P

BLK = 128
NSEL = 16
PAD = 16
VMEM_BYTES = 24 * 1024 * 1024


epsilon = 1e-05
exact_precision = lax.Precision.HIGHEST


def carried_in(part, axis, combine, identity, reverse):
    count = lax.axis_size(axis)
    place = lax.axis_index(axis)
    ahead = count - 1 - place if reverse else place
    gathered = jax.tree.map(lambda a: lax.all_gather(a, axis), part)
    state = jax.tree.map(lambda a, e: jnp.zeros_like(a) + jnp.asarray(e, a.dtype), part, identity)

    def one(lap, state):
        source = count - 1 - lap if reverse else lap
        return combine(
            state, jax.tree.map(lambda a: lax.dynamic_index_in_dim(a, source, 0, False), gathered)
        )

    return lax.fori_loop(0, ahead, one, state)


def decay_tables(decays):
    running = jnp.cumsum(decays, axis=1)
    finish = running[:, -1]
    length = decays.shape[1]
    below_diag = (jnp.arange(length)[:, None] >= jnp.arange(length)[None, :])[None]
    spread = running[:, :, None] - running[:, None, :]
    within = jnp.where(below_diag, jnp.exp(jnp.where(below_diag, spread, 0.0)), 0.0)
    return (jnp.exp(finish), jnp.exp(finish[:, None] - running), jnp.exp(running), within)


def chain_join(earlier, later):
    return (earlier[0] * later[0], later[0][:, None, None] * earlier[1] + later[1])


def sparse_grads(queries, grads_out, key_rows, value_rows, allowed):
    score_scale = queries.shape[-1] ** (-0.5)
    scores = (
        jnp.einsum("bqhd,bkhd->bhqk", queries, key_rows, preferred_element_type=jnp.float32)
        * score_scale
    )
    key_mask = allowed[:, None]
    scores = jnp.where(key_mask, scores, -1e30)
    row_max = jnp.max(scores, axis=-1, keepdims=True)
    weights = jnp.where(key_mask, jnp.exp(scores - row_max), 0.0)
    softmax_probs = weights / jnp.sum(weights, axis=-1, keepdims=True)
    rounded = softmax_probs.astype(jnp.bfloat16)
    outputs = jnp.einsum("bhqk,bkhd->bqhd", rounded, value_rows, preferred_element_type=jnp.float32)
    row_delta = jnp.sum(grads_out.astype(jnp.float32) * outputs, axis=-1)
    grad_probs = jnp.einsum(
        "bqhd,bkhd->bhqk", grads_out, value_rows, preferred_element_type=jnp.float32
    )
    grad_scores = (
        softmax_probs * (grad_probs - jnp.transpose(row_delta, (0, 2, 1))[..., None])
    ).astype(jnp.bfloat16)
    query_gradient = (
        jnp.einsum("bhqk,bkhd->bqhd", grad_scores, key_rows, preferred_element_type=jnp.float32)
        * score_scale
    )
    key_gradient = (
        jnp.einsum("bhqk,bqhd->bkhd", grad_scores, queries, preferred_element_type=jnp.float32)
        * score_scale
    )
    value_gradient = jnp.einsum(
        "bhqk,bqhd->bkhd", rounded, grads_out, preferred_element_type=jnp.float32
    )
    return (query_gradient, key_gradient, value_gradient)


def local(
    lin_q,
    lin_k,
    lin_v,
    lin_decay,
    norm_gain,
    soft_q,
    soft_k,
    soft_v,
    out_grad,
    block_lists,
    block_counts,
):
    tok_rows, heads_here, head_width = lin_q.shape
    blocks_here = tok_rows // BLK
    span_count = lax.axis_size("ctx")
    own_span = lax.axis_index("ctx")
    total_width = heads_here * lax.axis_size("head") * head_width
    complete_query = lin_q.astype(jnp.float32)
    complete_key = lin_k.astype(jnp.float32)
    complete_value = lin_v.astype(jnp.float32)
    carry_decay, trailing_decay, leading_decay, within = decay_tables(lin_decay)
    state_here = jnp.einsum(
        "boz,bor->ozr",
        complete_key * trailing_decay.T[:, :, None],
        complete_value,
        precision=exact_precision,
    )
    identity = (jnp.ones_like(carry_decay), jnp.zeros_like(state_here))
    incoming_state = carried_in((carry_decay, state_here), "ctx", chain_join, identity, False)[1]
    pair_weights = (
        jnp.einsum("thk,shk->hts", lin_q, lin_k, preferred_element_type=jnp.float32) * within
    )
    layer_out = jnp.einsum("hts,shv->thv", pair_weights, complete_value, precision=exact_precision)
    layer_out = layer_out + leading_decay.T[:, :, None] * jnp.einsum(
        "wfg,fgl->wfl", complete_query, incoming_state, precision=exact_precision
    )
    squares = lax.psum(jnp.sum(layer_out * layer_out, axis=(1, 2)), "head")
    root_mean = jnp.sqrt(squares / total_width + epsilon)
    norm_scale = norm_gain[None]
    all_lists, all_counts = (
        lax.all_gather(block_lists, "ctx", axis=0, tiled=True),
        lax.all_gather(block_counts, "ctx", axis=0, tiled=True),
    )
    entries = blocks_here * NSEL
    every_live = (
        jnp.arange(NSEL)[None, None, :] < all_counts.reshape(span_count, blocks_here)[:, :, None]
    ).reshape(span_count, entries)
    owner_hits = every_live & (all_lists // blocks_here == own_span)
    wanted_here = jnp.max(jnp.where(owner_hits, all_lists % blocks_here, -1), axis=1)
    my_live = jnp.arange(NSEL)[None, :] < block_counts[:, None]
    flat_owner = (block_lists // blocks_here).reshape(entries)
    flat_live = my_live.reshape(entries)
    key_blocks = soft_k.reshape(blocks_here, BLK, heads_here, head_width)
    value_blocks = soft_v.reshape(blocks_here, BLK, heads_here, head_width)
    picked = jnp.clip(wanted_here, 0, blocks_here - 1)
    present = (wanted_here >= 0)[:, None, None, None]
    nothing = jnp.zeros((), jnp.bfloat16)
    send_keys = jnp.where(present, key_blocks[picked], nothing)
    send_values = jnp.where(present, value_blocks[picked], nothing)
    got_keys, got_values = (
        lax.all_to_all(send_keys, "ctx", split_axis=0, concat_axis=0, tiled=True),
        lax.all_to_all(send_values, "ctx", split_axis=0, concat_axis=0, tiled=True),
    )
    listed_keys = jnp.take(got_keys, flat_owner, axis=0).reshape(
        blocks_here, NSEL * BLK, heads_here, head_width
    )
    listed_values = jnp.take(got_values, flat_owner, axis=0).reshape(
        blocks_here, NSEL * BLK, heads_here, head_width
    )
    key_rows = jnp.concatenate([key_blocks, listed_keys], axis=1)
    value_rows = jnp.concatenate([value_blocks, listed_values], axis=1)
    causal = jnp.arange(BLK)[:, None] >= jnp.arange(BLK)[None, :]
    remote_mask = jnp.broadcast_to(
        jnp.repeat(my_live, BLK, axis=1)[:, None, :], (blocks_here, BLK, NSEL * BLK)
    )
    allowed = jnp.concatenate(
        [jnp.broadcast_to(causal, (blocks_here, BLK, BLK)), remote_mask], axis=2
    )
    query_blocks = soft_q.reshape(blocks_here, BLK, heads_here, head_width)
    grad_blocks = out_grad.reshape(blocks_here, BLK, heads_here, head_width)
    query_gradient, key_gradient, value_gradient = sparse_grads(
        query_blocks, grad_blocks, key_rows, value_rows, allowed
    )
    soft_dq = query_gradient.reshape(tok_rows, heads_here, head_width).astype(jnp.bfloat16)
    routing = (
        flat_live[None, :] & (flat_owner[None, :] == jnp.arange(span_count)[:, None])
    ).astype(jnp.float32)
    remote_key = key_gradient[:, BLK:].reshape(entries, BLK, heads_here, head_width)
    remote_value = value_gradient[:, BLK:].reshape(entries, BLK, heads_here, head_width)
    part_key = jnp.einsum("oe,exhd->oxhd", routing, remote_key, precision=exact_precision).astype(
        jnp.bfloat16
    )
    part_value = jnp.einsum(
        "oe,exhd->oxhd", routing, remote_value, precision=exact_precision
    ).astype(jnp.bfloat16)
    back_key, back_value = (
        lax.all_to_all(part_key, "ctx", split_axis=0, concat_axis=0, tiled=True),
        lax.all_to_all(part_value, "ctx", split_axis=0, concat_axis=0, tiled=True),
    )
    placing = (wanted_here[:, None] == jnp.arange(blocks_here)[None, :]).astype(jnp.float32)
    added_key = jnp.einsum(
        "rb,rxhd->bxhd", placing, back_key.astype(jnp.float32), precision=exact_precision
    ).reshape(tok_rows, heads_here, head_width)
    added_value = jnp.einsum(
        "rb,rxhd->bxhd", placing, back_value.astype(jnp.float32), precision=exact_precision
    ).reshape(tok_rows, heads_here, head_width)
    soft_dk = (key_gradient[:, :BLK].reshape(tok_rows, heads_here, head_width) + added_key).astype(
        jnp.bfloat16
    )
    value_total = value_gradient[:, :BLK].reshape(tok_rows, heads_here, head_width) + added_value
    soft_dv = value_total.astype(jnp.bfloat16)
    cotangent = out_grad.astype(jnp.float32) + value_total
    inner_total = lax.psum(jnp.sum(norm_scale * cotangent * layer_out, axis=(1, 2)), "head")
    linear_cotangent = (
        norm_scale * cotangent / root_mean[:, None, None]
        - layer_out * (inner_total / (total_width * root_mean**3))[:, None, None]
    )
    reverse_state = carried_in(
        (
            carry_decay,
            jnp.einsum(
                "boz,bor->ozr",
                complete_query * leading_decay.T[:, :, None],
                linear_cotangent,
                precision=exact_precision,
            ),
        ),
        "ctx",
        chain_join,
        identity,
        True,
    )[1]
    grad_pair = (
        jnp.einsum("thv,shv->hts", linear_cotangent, complete_value, precision=exact_precision)
        * within
    )
    lin_dq = jnp.einsum("hts,shk->thk", grad_pair, complete_key, precision=exact_precision)
    lin_dq = lin_dq + leading_decay.T[:, :, None] * jnp.einsum(
        "fqs,qrs->fqr", linear_cotangent, incoming_state, precision=exact_precision
    )
    lin_dk = jnp.einsum("hts,thk->shk", grad_pair, complete_query, precision=exact_precision)
    lin_dk = lin_dk + trailing_decay.T[:, :, None] * jnp.einsum(
        "fut,ujt->fuj", complete_value, reverse_state, precision=exact_precision
    )
    lin_dv = jnp.einsum("hts,thv->shv", pair_weights, linear_cotangent, precision=exact_precision)
    lin_dv = lin_dv + trailing_decay.T[:, :, None] * jnp.einsum(
        "zpu,pux->zpx", complete_key, reverse_state, precision=exact_precision
    )
    return (
        lin_dq.astype(jnp.bfloat16),
        lin_dk.astype(jnp.bfloat16),
        lin_dv.astype(jnp.bfloat16),
        soft_dq,
        soft_dk,
        soft_dv,
    )


def triple(x):
    top = x.astype(jnp.bfloat16)
    rest = x - top.astype(jnp.float32)
    middle = rest.astype(jnp.bfloat16)
    low = (rest - middle.astype(jnp.float32)).astype(jnp.bfloat16)
    return top, middle, low


def by_head(source, scratch):
    rows, heads, width = source.shape
    scratch[...] = source[...].astype(jnp.float32).reshape(rows * heads, width)


def head_of(scratch, head, heads):
    rows = scratch.shape[0] // heads
    return scratch[pl.ds(head, rows, stride=heads), :].astype(jnp.bfloat16)


def pack_kernel(*refs):
    count = len(refs) - 2
    scratch, packed = refs[-1], refs[-2]
    rows, heads, _ = refs[0].shape
    for place in range(count):
        by_head(refs[place], scratch)
        for head in range(heads):
            packed[head, pl.ds(place * rows, rows), :] = head_of(scratch, head, heads)


def pack_lin_kernel(q_ref, k_ref, v_ref, decay_ref, gain_ref, packed, scratch):
    rows, heads, width = q_ref.shape
    pack_kernel(q_ref, k_ref, v_ref, packed, scratch)
    parts = [*triple(decay_ref[...]), *triple(gain_ref[...])]
    parts = [p.astype(jnp.float32) for p in parts]
    line = lax.broadcasted_iota(jnp.int32, (PAD, width), 0)
    for head in range(heads):
        block = jnp.zeros((PAD, width), jnp.float32)
        for place, part in enumerate(parts):
            block = jnp.where(line == place, part[head : head + 1], block)
        packed[head, pl.ds(3 * rows, PAD), :] = block.astype(jnp.bfloat16)


def unpack_kernel(packed, *refs):
    outs, scratch = refs[:-1], refs[-1]
    rows, heads, width = outs[0].shape
    for place, out in enumerate(outs):
        for head in range(heads):
            scratch[pl.ds(head, rows, stride=heads), :] = packed[
                head, pl.ds(place * rows, rows), :
            ].astype(jnp.float32)
        out[...] = scratch[...].reshape(rows, heads, width).astype(jnp.bfloat16)


def nt(a, b):
    return lax.dot_general(a, b, (((1,), (1,)), ((), ())), preferred_element_type=jnp.float32)


def nn(a, b):
    return lax.dot_general(a, b, (((1,), (0,)), ((), ())), preferred_element_type=jnp.float32)


def tn(a, b):
    return lax.dot_general(a, b, (((0,), (0,)), ((), ())), preferred_element_type=jnp.float32)


def soft_kernel(x_ref, packed, cot_ref, score_scr, dk_scr, dv_scr, kt_scr, vt_scr):
    spans, lines, width = x_ref.shape
    rows = lines // 4
    group = 2 if spans % 2 == 0 else 1
    wide = group * rows
    steps = spans // group
    scale = width ** (-0.5)

    def part(place, index):
        block = x_ref[pl.ds(index * group, group), pl.ds(place * rows, rows), :]
        return block.reshape(wide, width)

    def flip(x):
        return jnp.transpose(x.astype(jnp.float32)).astype(jnp.bfloat16)

    for step in range(steps):
        kt_scr[step] = flip(part(1, step))
        vt_scr[step] = flip(part(2, step))
    key_at = lax.broadcasted_iota(jnp.int32, (wide, wide), 0)
    query_at = lax.broadcasted_iota(jnp.int32, (wide, wide), 1)
    causal = key_at <= query_at
    for step in range(steps):
        queries = part(0, step)
        grads = part(3, step)
        grads_t = jnp.transpose(grads.astype(jnp.float32))
        top = None
        for at in range(step + 1):
            scores = nt(part(1, at), queries)
            if at == step:
                scores = jnp.where(causal, scores, -1e30)
            score_scr[at] = scores
            here = jnp.max(scores, axis=0, keepdims=True)
            top = here if top is None else jnp.maximum(top, here)
        total = jnp.zeros_like(top)
        for at in range(step + 1):
            weights = jnp.exp((score_scr[at] - top) * scale)
            score_scr[at] = weights
            total = total + jnp.sum(weights, axis=0, keepdims=True)
        inverse = 1.0 / total
        outputs_t = jnp.zeros((width, wide), jnp.float32)
        for at in range(step + 1):
            probs = score_scr[at] * inverse
            score_scr[at] = probs
            low = probs.astype(jnp.bfloat16)
            outputs_t = outputs_t + nn(vt_scr[at], low)
            added = nn(low, grads)
            dv_scr[at] = added if at == step else dv_scr[at] + added
        delta = jnp.sum(grads_t * outputs_t, axis=0, keepdims=True)
        dq_t = jnp.zeros((width, wide), jnp.float32)
        for at in range(step + 1):
            grad_probs = nt(part(2, at), grads)
            grad_scores = (score_scr[at] * (grad_probs - delta)).astype(jnp.bfloat16)
            dq_t = dq_t + nn(kt_scr[at], grad_scores)
            added = nn(grad_scores, queries)
            dk_scr[at] = added if at == step else dk_scr[at] + added
        dq = (jnp.transpose(dq_t) * scale).astype(jnp.bfloat16)
        packed[pl.ds(step * group, group), pl.ds(0, rows), :] = dq.reshape(group, rows, width)
    for step in range(steps):
        dk = (dk_scr[step] * scale).astype(jnp.bfloat16)
        packed[pl.ds(step * group, group), pl.ds(rows, rows), :] = dk.reshape(group, rows, width)
        dv = dv_scr[step]
        packed[pl.ds(step * group, group), pl.ds(2 * rows, rows), :] = dv.astype(
            jnp.bfloat16
        ).reshape(group, rows, width)
        cot_ref[pl.ds(step * group, group)] = (part(3, step).astype(jnp.float32) + dv).reshape(
            group, rows, width
        )


def span_tables(extra):
    rows = extra.shape[1]
    first = lax.broadcasted_iota(jnp.int32, (rows, rows), 0)
    second = lax.broadcasted_iota(jnp.int32, (rows, rows), 1)
    lower = first >= second
    along = nn(extra, (first <= second).astype(jnp.float32).astype(jnp.bfloat16))
    down = nt(lower.astype(jnp.float32).astype(jnp.bfloat16), extra)
    row = along[0:1] + along[1:2] + along[2:3]
    col = down[:, 0:1] + down[:, 1:2] + down[:, 2:3]
    finish = row[:, rows - 1 : rows]
    return row, col, finish, lower


def gain_of(extra):
    wide = extra.astype(jnp.float32)
    return wide[3:4] + wide[4:5] + wide[5:6]


def lin_forward_kernel(x_ref, cot_ref, out_ref, state_ref, sums_ref):
    spans, _, width = cot_ref.shape
    rows = cot_ref.shape[1]
    state = jnp.zeros((width, width), jnp.float32)
    for span in range(spans):
        q = x_ref[span, pl.ds(0, rows), :]
        k = x_ref[span, pl.ds(rows, rows), :]
        v = x_ref[span, pl.ds(2 * rows, rows), :]
        extra = x_ref[span, pl.ds(3 * rows, PAD), :]
        row, col, finish, lower = span_tables(extra)
        within = jnp.exp(jnp.where(lower, col - row, -1e30))
        pair = (nt(q, k) * within).astype(jnp.bfloat16)
        low_state = state.astype(jnp.bfloat16)
        state_ref[span] = low_state
        out = nn(pair, v) + jnp.exp(col) * nn(q, low_state)
        out_ref[span] = out
        decayed = (k.astype(jnp.float32) * jnp.exp(finish - col)).astype(jnp.bfloat16)
        state = jnp.exp(finish) * state + tn(decayed, v)
        scaled = gain_of(extra) * cot_ref[span]
        sums_ref[span] = jnp.sum(jnp.transpose(out * out), axis=0, keepdims=True)
        sums_ref[spans + span] = jnp.sum(jnp.transpose(scaled * out), axis=0, keepdims=True)


def lin_backward_kernel(total_width, x_ref, cot_ref, out_ref, state_ref, sums_ref, packed):
    spans, rows, width = cot_ref.shape
    state = jnp.zeros((width, width), jnp.float32)
    for span in reversed(range(spans)):
        q = x_ref[span, pl.ds(0, rows), :]
        k = x_ref[span, pl.ds(rows, rows), :]
        v = x_ref[span, pl.ds(2 * rows, rows), :]
        extra = x_ref[span, pl.ds(3 * rows, PAD), :]
        row, col, finish, lower = span_tables(extra)
        upper = jnp.logical_not(lower) | (
            lax.broadcasted_iota(jnp.int32, (rows, rows), 0)
            == lax.broadcasted_iota(jnp.int32, (rows, rows), 1)
        )
        within = jnp.exp(jnp.where(lower, col - row, -1e30))
        within_t = jnp.exp(jnp.where(upper, row - col, -1e30))
        mean = sums_ref[span] / total_width + epsilon
        root = jnp.sqrt(mean)
        first = jnp.transpose(jnp.broadcast_to(1.0 / root, (8, rows)))[:, 0:1]
        second = jnp.transpose(
            jnp.broadcast_to(sums_ref[spans + span] / (total_width * root * mean), (8, rows))
        )[:, 0:1]
        cotangent = gain_of(extra) * cot_ref[span] * first - out_ref[span] * second
        low_cot = cotangent.astype(jnp.bfloat16)
        grad_pair = (nt(low_cot, v) * within).astype(jnp.bfloat16)
        grad_pair_t = (nt(v, low_cot) * within_t).astype(jnp.bfloat16)
        pair_t = (nt(k, q) * within_t).astype(jnp.bfloat16)
        leading = jnp.exp(col)
        trailing = jnp.exp(finish - col)
        low_state = state.astype(jnp.bfloat16)
        dq = nn(grad_pair, k) + leading * nt(low_cot, state_ref[span])
        dk = nn(grad_pair_t, q) + trailing * nt(v, low_state)
        dv = nn(pair_t, low_cot) + trailing * nn(k, low_state)
        packed[span, pl.ds(0, rows), :] = dq.astype(jnp.bfloat16)
        packed[span, pl.ds(rows, rows), :] = dk.astype(jnp.bfloat16)
        packed[span, pl.ds(2 * rows, rows), :] = dv.astype(jnp.bfloat16)
        decayed = (q.astype(jnp.float32) * leading).astype(jnp.bfloat16)
        state = jnp.exp(finish) * state + tn(decayed, low_cot)


def call(kernel, out_shape, scratch, cost, *args):
    return pl.pallas_call(
        kernel,
        out_shape=out_shape,
        scratch_shapes=scratch,
        compiler_params=pltpu.CompilerParams(vmem_limit_bytes=VMEM_BYTES),
        cost_estimate=pl.CostEstimate(
            flops=cost, bytes_accessed=4 * 1024 * 1024, transcendentals=0
        ),
    )(*args)


def summed_everywhere(x):
    for axis in ("head", "ctx"):
        count = lax.axis_size(axis)
        step = 1
        while step < count:
            x = x + lax.ppermute(x, axis, [(i, i ^ step) for i in range(count)])
            step *= 2
    return x


def swapped(x):
    return lax.all_to_all(x, "ctx", split_axis=0, concat_axis=0, tiled=True)


def by_heads(
    lin_q, lin_k, lin_v, lin_decay, norm_gain, soft_q, soft_k, soft_v, out_grad
):
    rows, heads, width = lin_q.shape
    spans = lax.axis_size("ctx")
    total_width = heads * lax.axis_size("head") * width
    low = lambda *s: jax.ShapeDtypeStruct(s, jnp.bfloat16)
    full = lambda *s: jax.ShapeDtypeStruct(s, jnp.float32)
    turn = [pltpu.VMEM((rows * heads, width), jnp.float32)]
    group = 2 if spans % 2 == 0 else 1
    wide, steps = group * rows, spans // group
    with jax.named_scope("pack_soft"):
        soft_sent = call(
            pack_kernel, low(heads, 4 * rows, width), turn, 1 << 20,
            soft_q, soft_k, soft_v, out_grad,
        )
    soft_got = swapped(soft_sent)
    with jax.named_scope("pack_lin"):
        lin_sent = call(
            pack_lin_kernel, low(heads, 3 * rows + PAD, width), turn, 1 << 20,
            lin_q, lin_k, lin_v, lin_decay, norm_gain,
        )
    lin_got = swapped(lin_sent)
    with jax.named_scope("soft_layer"):
        soft_made, cot = call(
            soft_kernel,
            (low(spans, 3 * rows, width), full(spans, rows, width)),
            [
                pltpu.VMEM((steps, wide, wide), jnp.float32),
                pltpu.VMEM((steps, wide, width), jnp.float32),
                pltpu.VMEM((steps, wide, width), jnp.float32),
                pltpu.VMEM((steps, width, wide), jnp.bfloat16),
                pltpu.VMEM((steps, width, wide), jnp.bfloat16),
            ],
            1 << 30,
            soft_got,
        )
    soft_back = swapped(soft_made)
    with jax.named_scope("lin_forward"):
        layer_out, states, sums = call(
            lin_forward_kernel,
            (full(spans, rows, width), low(spans, width, width), full(2 * spans, 1, rows)),
            [],
            1 << 28,
            lin_got, cot,
        )
    with jax.named_scope("width_sums"):
        sums = summed_everywhere(sums.reshape(2 * spans, rows)).reshape(2 * spans, 1, rows)
    with jax.named_scope("lin_backward"):
        lin_made = call(
            functools.partial(lin_backward_kernel, total_width),
            low(spans, 3 * rows, width),
            [],
            1 << 28,
            lin_got, cot, layer_out, states, sums,
        )
    lin_back = swapped(lin_made)
    mine = (low(rows, heads, width),) * 3
    with jax.named_scope("unpack_soft"):
        soft_out = call(unpack_kernel, mine, turn, 1 << 20, soft_back)
    with jax.named_scope("unpack_lin"):
        lin_out = call(unpack_kernel, mine, turn, 1 << 20, lin_back)
    return (*lin_out, *soft_out)


def layers(
    lin_q,
    lin_k,
    lin_v,
    lin_decay,
    norm_gain,
    soft_q,
    soft_k,
    soft_v,
    out_grad,
    block_lists,
    block_counts,
):
    spans = lax.axis_size("ctx")
    if lin_q.shape[0] == BLK and spans - 1 <= NSEL and lin_q.shape[1] == spans:
        return by_heads(
            lin_q, lin_k, lin_v, lin_decay, norm_gain, soft_q, soft_k, soft_v, out_grad
        )
    return local(
        lin_q,
        lin_k,
        lin_v,
        lin_decay,
        norm_gain,
        soft_q,
        soft_k,
        soft_v,
        out_grad,
        block_lists,
        block_counts,
    )


def solution(mesh):
    in_specs = (
        P("ctx", "head", None),
        P("ctx", "head", None),
        P("ctx", "head", None),
        P("head", "ctx"),
        P("head", None),
        P("ctx", "head", None),
        P("ctx", "head", None),
        P("ctx", "head", None),
        P("ctx", "head", None),
        P("ctx", None),
        P("ctx"),
    )
    out_specs = (
        P("ctx", "head", None),
        P("ctx", "head", None),
        P("ctx", "head", None),
        P("ctx", "head", None),
        P("ctx", "head", None),
        P("ctx", "head", None),
    )
    return jax.shard_map(layers, mesh=mesh, in_specs=in_specs, out_specs=out_specs, check_vma=False)
```

```python
import functools

import jax
import jax.numpy as jnp
from jax import lax
from jax.experimental import pallas as pl
from jax.experimental.pallas import tpu as pltpu
from jax.sharding import PartitionSpec as P

BLK = 128
NSEL = 16
PAD = 16
GROUP = 2
COST = 1024
VMEM_BYTES = (24 * 1024 * 1024, 56 * 1024 * 1024)


epsilon = 1e-05
exact_precision = lax.Precision.HIGHEST


def carried_in(part, axis, combine, identity, reverse):
    count = lax.axis_size(axis)
    place = lax.axis_index(axis)
    ahead = count - 1 - place if reverse else place
    gathered = jax.tree.map(lambda a: lax.all_gather(a, axis), part)
    state = jax.tree.map(lambda a, e: jnp.zeros_like(a) + jnp.asarray(e, a.dtype), part, identity)

    def one(lap, state):
        source = count - 1 - lap if reverse else lap
        return combine(
            state, jax.tree.map(lambda a: lax.dynamic_index_in_dim(a, source, 0, False), gathered)
        )

    return lax.fori_loop(0, ahead, one, state)


def decay_tables(decays):
    running = jnp.cumsum(decays, axis=1)
    finish = running[:, -1]
    length = decays.shape[1]
    below_diag = (jnp.arange(length)[:, None] >= jnp.arange(length)[None, :])[None]
    spread = running[:, :, None] - running[:, None, :]
    within = jnp.where(below_diag, jnp.exp(jnp.where(below_diag, spread, 0.0)), 0.0)
    return (jnp.exp(finish), jnp.exp(finish[:, None] - running), jnp.exp(running), within)


def chain_join(earlier, later):
    return (earlier[0] * later[0], later[0][:, None, None] * earlier[1] + later[1])


def sparse_grads(queries, grads_out, key_rows, value_rows, allowed):
    score_scale = queries.shape[-1] ** (-0.5)
    scores = (
        jnp.einsum("bqhd,bkhd->bhqk", queries, key_rows, preferred_element_type=jnp.float32)
        * score_scale
    )
    key_mask = allowed[:, None]
    scores = jnp.where(key_mask, scores, -1e30)
    row_max = jnp.max(scores, axis=-1, keepdims=True)
    weights = jnp.where(key_mask, jnp.exp(scores - row_max), 0.0)
    softmax_probs = weights / jnp.sum(weights, axis=-1, keepdims=True)
    rounded = softmax_probs.astype(jnp.bfloat16)
    outputs = jnp.einsum("bhqk,bkhd->bqhd", rounded, value_rows, preferred_element_type=jnp.float32)
    row_delta = jnp.sum(grads_out.astype(jnp.float32) * outputs, axis=-1)
    grad_probs = jnp.einsum(
        "bqhd,bkhd->bhqk", grads_out, value_rows, preferred_element_type=jnp.float32
    )
    grad_scores = (
        softmax_probs * (grad_probs - jnp.transpose(row_delta, (0, 2, 1))[..., None])
    ).astype(jnp.bfloat16)
    query_gradient = (
        jnp.einsum("bhqk,bkhd->bqhd", grad_scores, key_rows, preferred_element_type=jnp.float32)
        * score_scale
    )
    key_gradient = (
        jnp.einsum("bhqk,bqhd->bkhd", grad_scores, queries, preferred_element_type=jnp.float32)
        * score_scale
    )
    value_gradient = jnp.einsum(
        "bhqk,bqhd->bkhd", rounded, grads_out, preferred_element_type=jnp.float32
    )
    return (query_gradient, key_gradient, value_gradient)


def local(
    lin_q,
    lin_k,
    lin_v,
    lin_decay,
    norm_gain,
    soft_q,
    soft_k,
    soft_v,
    out_grad,
    block_lists,
    block_counts,
):
    tok_rows, heads_here, head_width = lin_q.shape
    blocks_here = tok_rows // BLK
    span_count = lax.axis_size("ctx")
    own_span = lax.axis_index("ctx")
    total_width = heads_here * lax.axis_size("head") * head_width
    complete_query = lin_q.astype(jnp.float32)
    complete_key = lin_k.astype(jnp.float32)
    complete_value = lin_v.astype(jnp.float32)
    carry_decay, trailing_decay, leading_decay, within = decay_tables(lin_decay)
    state_here = jnp.einsum(
        "boz,bor->ozr",
        complete_key * trailing_decay.T[:, :, None],
        complete_value,
        precision=exact_precision,
    )
    identity = (jnp.ones_like(carry_decay), jnp.zeros_like(state_here))
    incoming_state = carried_in((carry_decay, state_here), "ctx", chain_join, identity, False)[1]
    pair_weights = (
        jnp.einsum("thk,shk->hts", lin_q, lin_k, preferred_element_type=jnp.float32) * within
    )
    layer_out = jnp.einsum("hts,shv->thv", pair_weights, complete_value, precision=exact_precision)
    layer_out = layer_out + leading_decay.T[:, :, None] * jnp.einsum(
        "wfg,fgl->wfl", complete_query, incoming_state, precision=exact_precision
    )
    squares = lax.psum(jnp.sum(layer_out * layer_out, axis=(1, 2)), "head")
    root_mean = jnp.sqrt(squares / total_width + epsilon)
    norm_scale = norm_gain[None]
    all_lists, all_counts = (
        lax.all_gather(block_lists, "ctx", axis=0, tiled=True),
        lax.all_gather(block_counts, "ctx", axis=0, tiled=True),
    )
    entries = blocks_here * NSEL
    every_live = (
        jnp.arange(NSEL)[None, None, :] < all_counts.reshape(span_count, blocks_here)[:, :, None]
    ).reshape(span_count, entries)
    owner_hits = every_live & (all_lists // blocks_here == own_span)
    wanted_here = jnp.max(jnp.where(owner_hits, all_lists % blocks_here, -1), axis=1)
    my_live = jnp.arange(NSEL)[None, :] < block_counts[:, None]
    flat_owner = (block_lists // blocks_here).reshape(entries)
    flat_live = my_live.reshape(entries)
    key_blocks = soft_k.reshape(blocks_here, BLK, heads_here, head_width)
    value_blocks = soft_v.reshape(blocks_here, BLK, heads_here, head_width)
    picked = jnp.clip(wanted_here, 0, blocks_here - 1)
    present = (wanted_here >= 0)[:, None, None, None]
    nothing = jnp.zeros((), jnp.bfloat16)
    send_keys = jnp.where(present, key_blocks[picked], nothing)
    send_values = jnp.where(present, value_blocks[picked], nothing)
    got_keys, got_values = (
        lax.all_to_all(send_keys, "ctx", split_axis=0, concat_axis=0, tiled=True),
        lax.all_to_all(send_values, "ctx", split_axis=0, concat_axis=0, tiled=True),
    )
    listed_keys = jnp.take(got_keys, flat_owner, axis=0).reshape(
        blocks_here, NSEL * BLK, heads_here, head_width
    )
    listed_values = jnp.take(got_values, flat_owner, axis=0).reshape(
        blocks_here, NSEL * BLK, heads_here, head_width
    )
    key_rows = jnp.concatenate([key_blocks, listed_keys], axis=1)
    value_rows = jnp.concatenate([value_blocks, listed_values], axis=1)
    causal = jnp.arange(BLK)[:, None] >= jnp.arange(BLK)[None, :]
    remote_mask = jnp.broadcast_to(
        jnp.repeat(my_live, BLK, axis=1)[:, None, :], (blocks_here, BLK, NSEL * BLK)
    )
    allowed = jnp.concatenate(
        [jnp.broadcast_to(causal, (blocks_here, BLK, BLK)), remote_mask], axis=2
    )
    query_blocks = soft_q.reshape(blocks_here, BLK, heads_here, head_width)
    grad_blocks = out_grad.reshape(blocks_here, BLK, heads_here, head_width)
    query_gradient, key_gradient, value_gradient = sparse_grads(
        query_blocks, grad_blocks, key_rows, value_rows, allowed
    )
    soft_dq = query_gradient.reshape(tok_rows, heads_here, head_width).astype(jnp.bfloat16)
    routing = (
        flat_live[None, :] & (flat_owner[None, :] == jnp.arange(span_count)[:, None])
    ).astype(jnp.float32)
    remote_key = key_gradient[:, BLK:].reshape(entries, BLK, heads_here, head_width)
    remote_value = value_gradient[:, BLK:].reshape(entries, BLK, heads_here, head_width)
    part_key = jnp.einsum("oe,exhd->oxhd", routing, remote_key, precision=exact_precision).astype(
        jnp.bfloat16
    )
    part_value = jnp.einsum(
        "oe,exhd->oxhd", routing, remote_value, precision=exact_precision
    ).astype(jnp.bfloat16)
    back_key, back_value = (
        lax.all_to_all(part_key, "ctx", split_axis=0, concat_axis=0, tiled=True),
        lax.all_to_all(part_value, "ctx", split_axis=0, concat_axis=0, tiled=True),
    )
    placing = (wanted_here[:, None] == jnp.arange(blocks_here)[None, :]).astype(jnp.float32)
    added_key = jnp.einsum(
        "rb,rxhd->bxhd", placing, back_key.astype(jnp.float32), precision=exact_precision
    ).reshape(tok_rows, heads_here, head_width)
    added_value = jnp.einsum(
        "rb,rxhd->bxhd", placing, back_value.astype(jnp.float32), precision=exact_precision
    ).reshape(tok_rows, heads_here, head_width)
    soft_dk = (key_gradient[:, :BLK].reshape(tok_rows, heads_here, head_width) + added_key).astype(
        jnp.bfloat16
    )
    value_total = value_gradient[:, :BLK].reshape(tok_rows, heads_here, head_width) + added_value
    soft_dv = value_total.astype(jnp.bfloat16)
    cotangent = out_grad.astype(jnp.float32) + value_total
    inner_total = lax.psum(jnp.sum(norm_scale * cotangent * layer_out, axis=(1, 2)), "head")
    linear_cotangent = (
        norm_scale * cotangent / root_mean[:, None, None]
        - layer_out * (inner_total / (total_width * root_mean**3))[:, None, None]
    )
    reverse_state = carried_in(
        (
            carry_decay,
            jnp.einsum(
                "boz,bor->ozr",
                complete_query * leading_decay.T[:, :, None],
                linear_cotangent,
                precision=exact_precision,
            ),
        ),
        "ctx",
        chain_join,
        identity,
        True,
    )[1]
    grad_pair = (
        jnp.einsum("thv,shv->hts", linear_cotangent, complete_value, precision=exact_precision)
        * within
    )
    lin_dq = jnp.einsum("hts,shk->thk", grad_pair, complete_key, precision=exact_precision)
    lin_dq = lin_dq + leading_decay.T[:, :, None] * jnp.einsum(
        "fqs,qrs->fqr", linear_cotangent, incoming_state, precision=exact_precision
    )
    lin_dk = jnp.einsum("hts,thk->shk", grad_pair, complete_query, precision=exact_precision)
    lin_dk = lin_dk + trailing_decay.T[:, :, None] * jnp.einsum(
        "fut,ujt->fuj", complete_value, reverse_state, precision=exact_precision
    )
    lin_dv = jnp.einsum("hts,thv->shv", pair_weights, linear_cotangent, precision=exact_precision)
    lin_dv = lin_dv + trailing_decay.T[:, :, None] * jnp.einsum(
        "zpu,pux->zpx", complete_key, reverse_state, precision=exact_precision
    )
    return (
        lin_dq.astype(jnp.bfloat16),
        lin_dk.astype(jnp.bfloat16),
        lin_dv.astype(jnp.bfloat16),
        soft_dq,
        soft_dk,
        soft_dv,
    )


def triple(x):
    top = x.astype(jnp.bfloat16)
    rest = x - top.astype(jnp.float32)
    middle = rest.astype(jnp.bfloat16)
    low = (rest - middle.astype(jnp.float32)).astype(jnp.bfloat16)
    return top, middle, low


def nt(a, b):
    return lax.dot_general(a, b, (((1,), (1,)), ((), ())), preferred_element_type=jnp.float32)


def nn(a, b):
    return lax.dot_general(a, b, (((1,), (0,)), ((), ())), preferred_element_type=jnp.float32)


def tn(a, b):
    return lax.dot_general(a, b, (((0,), (0,)), ((), ())), preferred_element_type=jnp.float32)


def later(half):
    return lax.axis_index("ctx") >= half


def place_in(half):
    return lax.rem(lax.axis_index("ctx"), half)


def spread(source, scratch):
    rows, heads, width = source.shape
    scratch[...] = source[...].astype(jnp.float32).reshape(rows * heads, width)


def head_of(scratch, head, heads):
    return scratch[pl.ds(head, scratch.shape[0] // heads, stride=heads), :]


def soft_head(place, half):
    return 2 * place if place < half else 2 * (place - half) + 1


def pack_soft_kernel(half, *refs):
    sources, sent, scratch = refs[:4], refs[4], refs[5]
    rows, heads, _ = sources[0].shape
    for place, source in enumerate(sources):
        spread(source, scratch)
        for dest in range(2 * half):
            sent[dest, pl.ds(place * rows, rows), :] = head_of(
                scratch, soft_head(dest, half), heads
            ).astype(jnp.bfloat16)


def put_heads(half, outs, scratch, first, second, rows, heads):
    late, me = later(half), place_in(half)
    for step, out in enumerate(outs):
        head = 2 * jnp.bitwise_xor(me, step)
        even, odd = head_of(scratch, head, heads), head_of(scratch, head + 1, heads)
        out[pl.ds(first * rows, rows), :] = jnp.where(late, odd, even).astype(jnp.bfloat16)
        out[pl.ds(second * rows, rows), :] = jnp.where(late, even, odd).astype(jnp.bfloat16)


def pack_lin_kernel(half, *refs):
    sources, decay_ref, gain_ref, outs = refs[:3], refs[3], refs[4], refs[5 : 5 + half]
    scratches, parts_scr = refs[5 + half : 8 + half], refs[8 + half]
    late, me = later(half), place_in(half)
    rows, heads, width = sources[0].shape
    for place, (source, scratch) in enumerate(zip(sources, scratches)):
        spread(source, scratch)
        put_heads(half, outs, scratch, place, 3 + place, rows, heads)
    parts = [*triple(decay_ref[...]), *triple(gain_ref[...])]
    for place, part in enumerate(parts):
        parts_scr[pl.ds(place * heads, heads), :] = part.astype(jnp.float32)
    line = lax.broadcasted_iota(jnp.int32, (PAD, width), 0)
    for step, out in enumerate(outs):
        blocks = []
        for head in range(2):
            at = 2 * jnp.bitwise_xor(me, step) + head
            block = jnp.zeros((PAD, width), jnp.float32)
            for place in range(len(parts)):
                block = jnp.where(line == place, parts_scr[pl.ds(place * heads + at, 1), :], block)
            blocks.append(block)
        even, odd = blocks
        out[pl.ds(6 * rows, PAD), :] = jnp.where(late, odd, even).astype(jnp.bfloat16)
        out[pl.ds(6 * rows + PAD, PAD), :] = jnp.where(late, even, odd).astype(jnp.bfloat16)


def unpack_soft_kernel(half, packed, *refs):
    outs, scratch = refs[:-1], refs[-1]
    rows, heads, width = outs[0].shape
    for place, out in enumerate(outs):
        for source in range(2 * half):
            scratch[pl.ds(soft_head(source, half), rows, stride=heads), :] = packed[
                source, pl.ds(place * rows, rows), :
            ].astype(jnp.float32)
        out[...] = scratch[...].reshape(rows, heads, width).astype(jnp.bfloat16)


def unpack_lin_kernel(half, *refs):
    steps, outs, scratch = refs[:half], refs[half:-1], refs[-1]
    late, me = later(half), place_in(half)
    rows, heads, width = outs[0].shape
    for place, out in enumerate(outs):
        for step, ref in enumerate(steps):
            head = 2 * jnp.bitwise_xor(me, step)
            first = ref[pl.ds(place * rows, rows), :].astype(jnp.float32)
            second = ref[pl.ds((3 + place) * rows, rows), :].astype(jnp.float32)
            scratch[pl.ds(head, rows, stride=heads), :] = jnp.where(late, second, first)
            scratch[pl.ds(head + 1, rows, stride=heads), :] = jnp.where(late, first, second)
        out[...] = scratch[...].reshape(rows, heads, width).astype(jnp.bfloat16)


def soft_part(x_ref, place):
    rows, width = x_ref.shape[1] // 4, x_ref.shape[2]

    def take(tile):
        return x_ref[pl.ds(tile * GROUP, GROUP), pl.ds(place * rows, rows), :].reshape(
            GROUP * rows, width
        )

    return take


def tile_scores(k, q, i, j):
    scores = nt(k(i), q(j))
    if i < j:
        return scores
    key_at = lax.broadcasted_iota(jnp.int32, scores.shape, 0)
    query_at = lax.broadcasted_iota(jnp.int32, scores.shape, 1)
    return jnp.where(key_at <= query_at, scores, -1e30)


def soft_forward_kernel(half, x_ref, lines_ref, dv_ref, own_ref, give_ref, scr, total_scr):
    late = later(half)
    spans, rows, width = dv_ref.shape
    wide, scale = GROUP * rows, width**-0.5
    q, k, v, g = (soft_part(x_ref, place) for place in range(4))
    lines_ref[...] = jnp.zeros_like(lines_ref)
    for j in range(spans // GROUP):
        top = None
        for i in range(j + 1):
            scores = tile_scores(k, q, i, j)
            scr[i] = scores
            here = jnp.max(scores, axis=0, keepdims=True)
            top = here if top is None else jnp.maximum(top, here)
        total = jnp.zeros_like(top)
        for i in range(j + 1):
            weights = jnp.exp((scr[i] - top) * scale)
            scr[i] = weights
            total = total + jnp.sum(weights, axis=0, keepdims=True)
        inverse = 1.0 / total
        out_t = None
        for i in range(j + 1):
            low = (scr[i] * inverse).astype(jnp.bfloat16)
            part = tn(v(i), low)
            out_t = part if out_t is None else out_t + part
            part = nn(low, g(j))
            total_scr[i] = part if i == j else total_scr[i] + part
        delta = jnp.sum(jnp.transpose(g(j).astype(jnp.float32)) * out_t, axis=0, keepdims=True)
        for place, line in enumerate((top, inverse, delta)):
            lines_ref[pl.ds(place, 1), pl.ds(j * wide, wide)] = line
    for i in range(spans // GROUP):
        dv_ref[pl.ds(i * GROUP, GROUP)] = (
            total_scr[i].astype(jnp.bfloat16).reshape(GROUP, rows, width)
        )
        total_scr[i] = total_scr[i] + g(i).astype(jnp.float32)
    tiles = half // GROUP
    for i in range(tiles):
        early, after = total_scr[i], total_scr[tiles + i]
        at = pl.ds(i * wide, wide)
        own_ref[at, :] = jnp.where(late, after, early)
        give_ref[at, :] = jnp.where(late, early, after).astype(jnp.bfloat16)


def soft_backward_kernel(x_ref, lines_ref, dv_ref, packed, dk_scr):
    spans, rows, width = dv_ref.shape
    wide, scale = GROUP * rows, width**-0.5
    q, k, v, g = (soft_part(x_ref, place) for place in range(4))
    for j in range(spans // GROUP):
        top, inverse, delta = (
            lines_ref[pl.ds(place, 1), pl.ds(j * wide, wide)] for place in range(3)
        )
        dq_t = None
        for i in range(j + 1):
            probs = jnp.exp((tile_scores(k, q, i, j) - top) * scale) * inverse
            grad_scores = (probs * (nt(v(i), g(j)) - delta)).astype(jnp.bfloat16)
            part = tn(k(i), grad_scores)
            dq_t = part if dq_t is None else dq_t + part
            part = nn(grad_scores, q(j))
            dk_scr[i] = part if i == j else dk_scr[i] + part
        dq = (jnp.transpose(dq_t) * scale).astype(jnp.bfloat16)
        packed[pl.ds(j * GROUP, GROUP), pl.ds(0, rows), :] = dq.reshape(GROUP, rows, width)
    for i in range(spans // GROUP):
        dk = (dk_scr[i] * scale).astype(jnp.bfloat16)
        packed[pl.ds(i * GROUP, GROUP), pl.ds(rows, rows), :] = dk.reshape(GROUP, rows, width)
    packed[:, pl.ds(2 * rows, rows), :] = dv_ref[...]


def span_tables(extra):
    rows = extra.shape[1]
    first = lax.broadcasted_iota(jnp.int32, (rows, rows), 0)
    second = lax.broadcasted_iota(jnp.int32, (rows, rows), 1)
    lower = first >= second
    along = nn(extra, (first <= second).astype(jnp.float32).astype(jnp.bfloat16))
    down = nt(lower.astype(jnp.float32).astype(jnp.bfloat16), extra)
    row = along[0:1] + along[1:2] + along[2:3]
    col = down[:, 0:1] + down[:, 1:2] + down[:, 2:3]
    finish = row[:, rows - 1 : rows]
    return row, col, finish, lower, first <= second


def gain_of(extra):
    wide = extra.astype(jnp.float32)
    return wide[3:4] + wide[4:5] + wide[5:6]


def lin_parts(x_ref, slot, span, rows):
    q, k, v = (
        x_ref[span, pl.ds((slot * 3 + place) * rows, rows), :] for place in range(3)
    )
    return q, k, v, x_ref[span, pl.ds(6 * rows + slot * PAD, PAD), :]


def lin_local_kernel(half, rows, *refs):
    steps, (x_ref, out_ref, states_ref, give_ref) = refs[:half], refs[half:]
    me = place_in(half)
    for step, ref in enumerate(steps):
        x_ref[jnp.bitwise_xor(me, step)] = ref[...]
    width = x_ref.shape[2]
    for slot in range(2):
        state = jnp.zeros((width, width), jnp.float32)
        for span in range(half):
            q, k, v, extra = lin_parts(x_ref, slot, span, rows)
            row, col, finish, lower, _ = span_tables(extra)
            within = jnp.exp(jnp.where(lower, col - row, -1e30))
            pair = (nt(q, k) * within).astype(jnp.bfloat16)
            out = nn(pair, v)
            if span > 0:
                low_state = state.astype(jnp.bfloat16)
                states_ref[slot, span] = low_state
                out = out + jnp.exp(col) * nn(q, low_state)
            else:
                states_ref[slot, span] = jnp.zeros((width, width), jnp.bfloat16)
            out_ref[slot, span] = out
            decayed = (k.astype(jnp.float32) * jnp.exp(finish - col)).astype(jnp.bfloat16)
            state = jnp.exp(finish) * state + tn(decayed, v)
        give_ref[1 - slot] = state.astype(jnp.bfloat16)


def lin_sums_kernel(half, rows, x_ref, own_ref, far_ref, local_ref, given_ref, cot_ref, out_ref, sums_ref):
    before = [jnp.zeros((1, 1), jnp.float32)] * 2
    for span in range(half):
        at = pl.ds(span * rows, rows)
        inner, squares = None, None
        for slot, part_ref in enumerate((own_ref, far_ref)):
            q, _, _, extra = lin_parts(x_ref, slot, span, rows)
            _, col, finish, _, _ = span_tables(extra)
            out = local_ref[slot, span] + jnp.exp(before[slot] + col) * nn(q, given_ref[slot])
            before[slot] = before[slot] + finish
            out_ref[slot, span] = out
            scaled = gain_of(extra) * part_ref[at, :].astype(jnp.float32)
            cot_ref[slot, span] = scaled
            inner = scaled * out if slot == 0 else inner + scaled * out
            squares = out * out if slot == 0 else squares + out * out
        sums_ref[pl.ds(span, 1), :] = jnp.sum(jnp.transpose(squares), axis=0, keepdims=True)
        sums_ref[pl.ds(half + span, 1), :] = jnp.sum(jnp.transpose(inner), axis=0, keepdims=True)


def lin_cot_kernel(half, rows, total_width, x_ref, cot_ref, out_ref, sums_ref, low_ref, state_ref):
    width = cot_ref.shape[3]
    mean = sums_ref[pl.ds(0, half), :] / total_width + epsilon
    root = jnp.sqrt(mean)
    inner = sums_ref[pl.ds(half, half), :] / (total_width * root * mean)
    scalars = jnp.transpose(jnp.concatenate([1.0 / root, inner], axis=0))
    for slot in range(2):
        state = jnp.zeros((width, width), jnp.float32)
        for span in reversed(range(half)):
            q, _, _, extra = lin_parts(x_ref, slot, span, rows)
            _, col, finish, _, _ = span_tables(extra)
            cotangent = (
                cot_ref[slot, span] * scalars[:, span : span + 1]
                - out_ref[slot, span] * scalars[:, half + span : half + span + 1]
            )
            low_cot = cotangent.astype(jnp.bfloat16)
            low_ref[slot, span] = low_cot
            decayed = (q.astype(jnp.float32) * jnp.exp(col)).astype(jnp.bfloat16)
            state = jnp.exp(finish) * state + tn(decayed, low_cot)
        state_ref[1 - slot] = state.astype(jnp.bfloat16)


def lin_own_kernel(half, rows, x_ref, low_ref, states_ref, given_ref, dq_ref, made_ref):
    width = low_ref.shape[3]
    for slot in range(2):
        before = [jnp.zeros((1, 1), jnp.float32)]
        for span in range(half):
            finish = span_tables(lin_parts(x_ref, slot, span, rows)[3])[2]
            before.append(before[-1] + finish)
        given = given_ref[slot].astype(jnp.float32)
        state = jnp.zeros((width, width), jnp.float32)
        for span in reversed(range(half)):
            q, k, v, extra = lin_parts(x_ref, slot, span, rows)
            row, col, finish, lower, upper = span_tables(extra)
            within = jnp.exp(jnp.where(lower, col - row, -1e30))
            within_t = jnp.exp(jnp.where(upper, row - col, -1e30))
            low_cot = low_ref[slot, span]
            grad_pair = (nt(low_cot, v) * within).astype(jnp.bfloat16)
            grad_pair_t = (nt(v, low_cot) * within_t).astype(jnp.bfloat16)
            pair_t = (nt(k, q) * within_t).astype(jnp.bfloat16)
            leading = jnp.exp(col)
            trailing = jnp.exp(finish - col)
            low_state = state.astype(jnp.bfloat16)
            carried = states_ref[slot, span].astype(jnp.float32) + jnp.exp(before[span]) * given
            dq = nn(grad_pair, k) + leading * nt(low_cot, carried.astype(jnp.bfloat16))
            dq_ref[slot, span] = dq.astype(jnp.bfloat16)
            made_ref[slot, 0, span] = nn(grad_pair_t, q) + trailing * nt(v, low_state)
            made_ref[slot, 1, span] = nn(pair_t, low_cot) + trailing * nn(k, low_state)
            decayed = (q.astype(jnp.float32) * leading).astype(jnp.bfloat16)
            state = jnp.exp(finish) * state + tn(decayed, low_cot)


def lin_finish_kernel(half, rows, x_ref, dq_ref, made_ref, state_ref, *refs):
    outs, packed = refs[:half], refs[half]
    for slot in range(2):
        state = state_ref[slot]
        after = jnp.zeros((1, 1), jnp.float32)
        for span in reversed(range(half)):
            _, k, v, extra = lin_parts(x_ref, slot, span, rows)
            _, col, finish, _, _ = span_tables(extra)
            trailing = jnp.exp(after + finish - col)
            after = after + finish
            dk = made_ref[slot, 0, span] + trailing * nt(v, state)
            dv = made_ref[slot, 1, span] + trailing * nn(k, state)
            for place, made in enumerate((dq_ref[slot, span], dk, dv)):
                packed[span, pl.ds((slot * 3 + place) * rows, rows), :] = made.astype(
                    jnp.bfloat16
                )
    for step, out in enumerate(outs):
        out[...] = packed[jnp.bitwise_xor(place_in(half), step)]


def call(name, kernel, out_shape, scratch, cost, *args):
    with jax.named_scope(name):
        return pl.pallas_call(
            kernel,
            out_shape=out_shape,
            scratch_shapes=scratch,
            name=name,
            compiler_params=pltpu.CompilerParams(vmem_limit_bytes=VMEM_BYTES[name.startswith("pack_soft")]),
            cost_estimate=pl.CostEstimate(flops=cost, bytes_accessed=1024, transcendentals=0),
        )(*args)


def by_halves(lin_q, lin_k, lin_v, lin_decay, norm_gain, soft_q, soft_k, soft_v, out_grad):
    rows, heads, width = lin_q.shape
    spans = lax.axis_size("ctx")
    half = spans // 2
    tokens = half * rows
    total_width = heads * lax.axis_size("head") * width
    low = lambda *s: jax.ShapeDtypeStruct(s, jnp.bfloat16)
    full = lambda *s: jax.ShapeDtypeStruct(s, jnp.float32)
    held = lambda *s: pltpu.VMEM(s, jnp.float32)
    bind = functools.partial
    tiles, wide = spans // GROUP, GROUP * rows
    after = lax.optimization_barrier

    def moved(x, pairs):
        return lax.ppermute(x, "ctx", pairs)

    def exchanged(parts):
        return [parts[0]] + [
            moved(parts[step], [(i, i ^ step) for i in range(spans)]) for step in range(1, half)
        ]

    both = [(i, i ^ half) for i in range(spans)]
    up = [(i, i + half) for i in range(half)]
    down = [(i + half, i) for i in range(half)]
    turned = held(rows * heads, width)
    mine = (low(rows, heads, width),) * 3
    soft_sent = call(
        "pack_soft", bind(pack_soft_kernel, half), low(spans, 4 * rows, width), [turned], 11960000000,
        soft_q, soft_k, soft_v, out_grad,
    )
    x = lax.all_to_all(soft_sent, "ctx", 0, 0, tiled=True)
    lin_sent = call(
        "pack_lin", bind(pack_lin_kernel, half), (low(6 * rows + 2 * PAD, width),) * half,
        [turned] * 3 + [held(6 * heads, width)], 5980000000,
        lin_q, lin_k, lin_v, lin_decay, norm_gain,
    )
    lin_got = exchanged(lin_sent)
    lines, dv, own, give = call(
        "soft_forward", bind(soft_forward_kernel, half),
        (full(8, spans * rows), low(spans, rows, width), full(tokens, width), low(tokens, width)),
        [held(tiles, wide, wide), held(tiles, wide, width)], COST, x,
    )
    far = moved(give, both)
    lin_got[0], own = after((lin_got[0], own))
    lin_x, local_out, states, state = call(
        "lin_local", bind(lin_local_kernel, half, rows),
        (
            low(half, 6 * rows + 2 * PAD, width),
            full(2, half, rows, width),
            low(2, half, width, width),
            low(2, width, width),
        ),
        [], 13340000000, *lin_got,
    )
    state = moved(state, up)
    soft_made = call(
        "soft_backward", soft_backward_kernel, low(spans, 3 * rows, width),
        [held(tiles, wide, width)], 16560000000, x, lines, dv,
    )
    far, soft_made = after((far, soft_made))
    cot, layer_out, sums = call(
        "lin_sums", bind(lin_sums_kernel, half, rows),
        (full(2, half, rows, width),) * 2 + (full(2 * half, rows),), [], COST,
        lin_x, own, far, local_out, state,
    )
    soft_made, sums = after((soft_made, sums))
    soft_back = lax.all_to_all(soft_made, "ctx", 0, 0, tiled=True)
    for axis, reach in (("head", lax.axis_size("head")), ("ctx", half)):
        count = lax.axis_size(axis)
        sums = after(sums)
        sums = sums + sum(
            lax.ppermute(sums, axis, [(i, i ^ step) for i in range(count)])
            for step in range(1, reach)
        )
    low_cot, late_state = call(
        "lin_cot", bind(lin_cot_kernel, half, rows, total_width),
        (low(2, half, rows, width), low(2, width, width)), [], COST,
        lin_x, cot, layer_out, sums,
    )
    late_state = moved(late_state, down)
    lin_dq, lin_made = call(
        "lin_own", bind(lin_own_kernel, half, rows),
        (low(2, half, rows, width), full(2, 2, half, rows, width)), [], COST,
        lin_x, low_cot, states, state,
    )
    lin_made = call(
        "lin_finish", bind(lin_finish_kernel, half, rows), (low(6 * rows, width),) * half,
        [pltpu.VMEM((half, 6 * rows, width), jnp.bfloat16)], COST,
        lin_x, lin_dq, lin_made, late_state,
    )
    lin_back = exchanged(lin_made)
    soft_out = call(
        "unpack_soft", bind(unpack_soft_kernel, half), mine, [turned], COST, soft_back
    )
    lin_out = call("unpack_lin", bind(unpack_lin_kernel, half), mine, [turned], COST, *lin_back)
    return (*lin_out, *soft_out)


def layers(
    lin_q,
    lin_k,
    lin_v,
    lin_decay,
    norm_gain,
    soft_q,
    soft_k,
    soft_v,
    out_grad,
    block_lists,
    block_counts,
):
    spans = lax.axis_size("ctx")
    if (
        lin_q.shape[0] == BLK
        and spans - 1 <= NSEL
        and lin_q.shape[1] == spans
        and spans >= 4
        and spans & (spans - 1) == 0
    ):
        return by_halves(
            lin_q, lin_k, lin_v, lin_decay, norm_gain, soft_q, soft_k, soft_v, out_grad
        )
    return local(
        lin_q,
        lin_k,
        lin_v,
        lin_decay,
        norm_gain,
        soft_q,
        soft_k,
        soft_v,
        out_grad,
        block_lists,
        block_counts,
    )


def solution(mesh):
    in_specs = (
        P("ctx", "head", None),
        P("ctx", "head", None),
        P("ctx", "head", None),
        P("head", "ctx"),
        P("head", None),
        P("ctx", "head", None),
        P("ctx", "head", None),
        P("ctx", "head", None),
        P("ctx", "head", None),
        P("ctx", None),
        P("ctx"),
    )
    out_specs = (
        P("ctx", "head", None),
        P("ctx", "head", None),
        P("ctx", "head", None),
        P("ctx", "head", None),
        P("ctx", "head", None),
        P("ctx", "head", None),
    )
    return jax.shard_map(layers, mesh=mesh, in_specs=in_specs, out_specs=out_specs, check_vma=False)
```

```python
import functools

import jax
import jax.numpy as jnp
from jax import lax
from jax.experimental import pallas as pl
from jax.experimental.pallas import tpu as pltpu
from jax.sharding import PartitionSpec as P

BLK = 128
NSEL = 16
PAD = 16
GROUP = 2
COST = 1024
VMEM_BYTES = (24 * 1024 * 1024, 56 * 1024 * 1024)


epsilon = 1e-05
exact_precision = lax.Precision.HIGHEST


def carried_in(part, axis, combine, identity, reverse):
    count = lax.axis_size(axis)
    place = lax.axis_index(axis)
    ahead = count - 1 - place if reverse else place
    gathered = jax.tree.map(lambda a: lax.all_gather(a, axis), part)
    state = jax.tree.map(lambda a, e: jnp.zeros_like(a) + jnp.asarray(e, a.dtype), part, identity)

    def one(lap, state):
        source = count - 1 - lap if reverse else lap
        return combine(
            state, jax.tree.map(lambda a: lax.dynamic_index_in_dim(a, source, 0, False), gathered)
        )

    return lax.fori_loop(0, ahead, one, state)


def decay_tables(decays):
    running = jnp.cumsum(decays, axis=1)
    finish = running[:, -1]
    length = decays.shape[1]
    below_diag = (jnp.arange(length)[:, None] >= jnp.arange(length)[None, :])[None]
    spread = running[:, :, None] - running[:, None, :]
    within = jnp.where(below_diag, jnp.exp(jnp.where(below_diag, spread, 0.0)), 0.0)
    return (jnp.exp(finish), jnp.exp(finish[:, None] - running), jnp.exp(running), within)


def chain_join(earlier, later):
    return (earlier[0] * later[0], later[0][:, None, None] * earlier[1] + later[1])


def sparse_grads(queries, grads_out, key_rows, value_rows, allowed):
    score_scale = queries.shape[-1] ** (-0.5)
    scores = (
        jnp.einsum("bqhd,bkhd->bhqk", queries, key_rows, preferred_element_type=jnp.float32)
        * score_scale
    )
    key_mask = allowed[:, None]
    scores = jnp.where(key_mask, scores, -1e30)
    row_max = jnp.max(scores, axis=-1, keepdims=True)
    weights = jnp.where(key_mask, jnp.exp(scores - row_max), 0.0)
    softmax_probs = weights / jnp.sum(weights, axis=-1, keepdims=True)
    rounded = softmax_probs.astype(jnp.bfloat16)
    outputs = jnp.einsum("bhqk,bkhd->bqhd", rounded, value_rows, preferred_element_type=jnp.float32)
    row_delta = jnp.sum(grads_out.astype(jnp.float32) * outputs, axis=-1)
    grad_probs = jnp.einsum(
        "bqhd,bkhd->bhqk", grads_out, value_rows, preferred_element_type=jnp.float32
    )
    grad_scores = (
        softmax_probs * (grad_probs - jnp.transpose(row_delta, (0, 2, 1))[..., None])
    ).astype(jnp.bfloat16)
    query_gradient = (
        jnp.einsum("bhqk,bkhd->bqhd", grad_scores, key_rows, preferred_element_type=jnp.float32)
        * score_scale
    )
    key_gradient = (
        jnp.einsum("bhqk,bqhd->bkhd", grad_scores, queries, preferred_element_type=jnp.float32)
        * score_scale
    )
    value_gradient = jnp.einsum(
        "bhqk,bqhd->bkhd", rounded, grads_out, preferred_element_type=jnp.float32
    )
    return (query_gradient, key_gradient, value_gradient)


def local(
    lin_q,
    lin_k,
    lin_v,
    lin_decay,
    norm_gain,
    soft_q,
    soft_k,
    soft_v,
    out_grad,
    block_lists,
    block_counts,
):
    tok_rows, heads_here, head_width = lin_q.shape
    blocks_here = tok_rows // BLK
    span_count = lax.axis_size("ctx")
    own_span = lax.axis_index("ctx")
    total_width = heads_here * lax.axis_size("head") * head_width
    complete_query = lin_q.astype(jnp.float32)
    complete_key = lin_k.astype(jnp.float32)
    complete_value = lin_v.astype(jnp.float32)
    carry_decay, trailing_decay, leading_decay, within = decay_tables(lin_decay)
    state_here = jnp.einsum(
        "boz,bor->ozr",
        complete_key * trailing_decay.T[:, :, None],
        complete_value,
        precision=exact_precision,
    )
    identity = (jnp.ones_like(carry_decay), jnp.zeros_like(state_here))
    incoming_state = carried_in((carry_decay, state_here), "ctx", chain_join, identity, False)[1]
    pair_weights = (
        jnp.einsum("thk,shk->hts", lin_q, lin_k, preferred_element_type=jnp.float32) * within
    )
    layer_out = jnp.einsum("hts,shv->thv", pair_weights, complete_value, precision=exact_precision)
    layer_out = layer_out + leading_decay.T[:, :, None] * jnp.einsum(
        "wfg,fgl->wfl", complete_query, incoming_state, precision=exact_precision
    )
    squares = lax.psum(jnp.sum(layer_out * layer_out, axis=(1, 2)), "head")
    root_mean = jnp.sqrt(squares / total_width + epsilon)
    norm_scale = norm_gain[None]
    all_lists, all_counts = (
        lax.all_gather(block_lists, "ctx", axis=0, tiled=True),
        lax.all_gather(block_counts, "ctx", axis=0, tiled=True),
    )
    entries = blocks_here * NSEL
    every_live = (
        jnp.arange(NSEL)[None, None, :] < all_counts.reshape(span_count, blocks_here)[:, :, None]
    ).reshape(span_count, entries)
    owner_hits = every_live & (all_lists // blocks_here == own_span)
    wanted_here = jnp.max(jnp.where(owner_hits, all_lists % blocks_here, -1), axis=1)
    my_live = jnp.arange(NSEL)[None, :] < block_counts[:, None]
    flat_owner = (block_lists // blocks_here).reshape(entries)
    flat_live = my_live.reshape(entries)
    key_blocks = soft_k.reshape(blocks_here, BLK, heads_here, head_width)
    value_blocks = soft_v.reshape(blocks_here, BLK, heads_here, head_width)
    picked = jnp.clip(wanted_here, 0, blocks_here - 1)
    present = (wanted_here >= 0)[:, None, None, None]
    nothing = jnp.zeros((), jnp.bfloat16)
    send_keys = jnp.where(present, key_blocks[picked], nothing)
    send_values = jnp.where(present, value_blocks[picked], nothing)
    got_keys, got_values = (
        lax.all_to_all(send_keys, "ctx", split_axis=0, concat_axis=0, tiled=True),
        lax.all_to_all(send_values, "ctx", split_axis=0, concat_axis=0, tiled=True),
    )
    listed_keys = jnp.take(got_keys, flat_owner, axis=0).reshape(
        blocks_here, NSEL * BLK, heads_here, head_width
    )
    listed_values = jnp.take(got_values, flat_owner, axis=0).reshape(
        blocks_here, NSEL * BLK, heads_here, head_width
    )
    key_rows = jnp.concatenate([key_blocks, listed_keys], axis=1)
    value_rows = jnp.concatenate([value_blocks, listed_values], axis=1)
    causal = jnp.arange(BLK)[:, None] >= jnp.arange(BLK)[None, :]
    remote_mask = jnp.broadcast_to(
        jnp.repeat(my_live, BLK, axis=1)[:, None, :], (blocks_here, BLK, NSEL * BLK)
    )
    allowed = jnp.concatenate(
        [jnp.broadcast_to(causal, (blocks_here, BLK, BLK)), remote_mask], axis=2
    )
    query_blocks = soft_q.reshape(blocks_here, BLK, heads_here, head_width)
    grad_blocks = out_grad.reshape(blocks_here, BLK, heads_here, head_width)
    query_gradient, key_gradient, value_gradient = sparse_grads(
        query_blocks, grad_blocks, key_rows, value_rows, allowed
    )
    soft_dq = query_gradient.reshape(tok_rows, heads_here, head_width).astype(jnp.bfloat16)
    routing = (
        flat_live[None, :] & (flat_owner[None, :] == jnp.arange(span_count)[:, None])
    ).astype(jnp.float32)
    remote_key = key_gradient[:, BLK:].reshape(entries, BLK, heads_here, head_width)
    remote_value = value_gradient[:, BLK:].reshape(entries, BLK, heads_here, head_width)
    part_key = jnp.einsum("oe,exhd->oxhd", routing, remote_key, precision=exact_precision).astype(
        jnp.bfloat16
    )
    part_value = jnp.einsum(
        "oe,exhd->oxhd", routing, remote_value, precision=exact_precision
    ).astype(jnp.bfloat16)
    back_key, back_value = (
        lax.all_to_all(part_key, "ctx", split_axis=0, concat_axis=0, tiled=True),
        lax.all_to_all(part_value, "ctx", split_axis=0, concat_axis=0, tiled=True),
    )
    placing = (wanted_here[:, None] == jnp.arange(blocks_here)[None, :]).astype(jnp.float32)
    added_key = jnp.einsum(
        "rb,rxhd->bxhd", placing, back_key.astype(jnp.float32), precision=exact_precision
    ).reshape(tok_rows, heads_here, head_width)
    added_value = jnp.einsum(
        "rb,rxhd->bxhd", placing, back_value.astype(jnp.float32), precision=exact_precision
    ).reshape(tok_rows, heads_here, head_width)
    soft_dk = (key_gradient[:, :BLK].reshape(tok_rows, heads_here, head_width) + added_key).astype(
        jnp.bfloat16
    )
    value_total = value_gradient[:, :BLK].reshape(tok_rows, heads_here, head_width) + added_value
    soft_dv = value_total.astype(jnp.bfloat16)
    cotangent = out_grad.astype(jnp.float32) + value_total
    inner_total = lax.psum(jnp.sum(norm_scale * cotangent * layer_out, axis=(1, 2)), "head")
    linear_cotangent = (
        norm_scale * cotangent / root_mean[:, None, None]
        - layer_out * (inner_total / (total_width * root_mean**3))[:, None, None]
    )
    reverse_state = carried_in(
        (
            carry_decay,
            jnp.einsum(
                "boz,bor->ozr",
                complete_query * leading_decay.T[:, :, None],
                linear_cotangent,
                precision=exact_precision,
            ),
        ),
        "ctx",
        chain_join,
        identity,
        True,
    )[1]
    grad_pair = (
        jnp.einsum("thv,shv->hts", linear_cotangent, complete_value, precision=exact_precision)
        * within
    )
    lin_dq = jnp.einsum("hts,shk->thk", grad_pair, complete_key, precision=exact_precision)
    lin_dq = lin_dq + leading_decay.T[:, :, None] * jnp.einsum(
        "fqs,qrs->fqr", linear_cotangent, incoming_state, precision=exact_precision
    )
    lin_dk = jnp.einsum("hts,thk->shk", grad_pair, complete_query, precision=exact_precision)
    lin_dk = lin_dk + trailing_decay.T[:, :, None] * jnp.einsum(
        "fut,ujt->fuj", complete_value, reverse_state, precision=exact_precision
    )
    lin_dv = jnp.einsum("hts,thv->shv", pair_weights, linear_cotangent, precision=exact_precision)
    lin_dv = lin_dv + trailing_decay.T[:, :, None] * jnp.einsum(
        "zpu,pux->zpx", complete_key, reverse_state, precision=exact_precision
    )
    return (
        lin_dq.astype(jnp.bfloat16),
        lin_dk.astype(jnp.bfloat16),
        lin_dv.astype(jnp.bfloat16),
        soft_dq,
        soft_dk,
        soft_dv,
    )


def triple(x):
    top = x.astype(jnp.bfloat16)
    rest = x - top.astype(jnp.float32)
    middle = rest.astype(jnp.bfloat16)
    low = (rest - middle.astype(jnp.float32)).astype(jnp.bfloat16)
    return top, middle, low


def nt(a, b):
    return lax.dot_general(a, b, (((1,), (1,)), ((), ())), preferred_element_type=jnp.float32)


def nn(a, b):
    return lax.dot_general(a, b, (((1,), (0,)), ((), ())), preferred_element_type=jnp.float32)


def tn(a, b):
    return lax.dot_general(a, b, (((0,), (0,)), ((), ())), preferred_element_type=jnp.float32)


def later(half):
    return lax.axis_index("ctx") >= half


def place_in(half):
    return lax.rem(lax.axis_index("ctx"), half)


def spread(source, scratch):
    rows, heads, width = source.shape
    scratch[...] = source[...].astype(jnp.float32).reshape(rows * heads, width)


def head_of(scratch, head, heads):
    return scratch[pl.ds(head, scratch.shape[0] // heads, stride=heads), :]


def soft_head(place, half):
    return 2 * place if place < half else 2 * (place - half) + 1


def pack_soft_kernel(half, *refs):
    sources, outs, scratches = refs[:4], refs[4 : 4 + 2 * half], refs[4 + 2 * half :]
    rows, heads, _ = sources[0].shape
    me = lax.axis_index("ctx")
    for source, scratch in zip(sources, scratches):
        spread(source, scratch)
    for step, out in enumerate(outs):
        dest = jnp.bitwise_xor(me, step)
        head = jnp.where(dest < half, 2 * dest, 2 * (dest - half) + 1)
        for place, scratch in enumerate(scratches):
            out[pl.ds(place * rows, rows), :] = head_of(scratch, head, heads).astype(jnp.bfloat16)


def put_heads(half, outs, scratch, first, second, rows, heads):
    late, me = later(half), place_in(half)
    for step, out in enumerate(outs):
        head = 2 * jnp.bitwise_xor(me, step)
        even, odd = head_of(scratch, head, heads), head_of(scratch, head + 1, heads)
        out[pl.ds(first * rows, rows), :] = jnp.where(late, odd, even).astype(jnp.bfloat16)
        out[pl.ds(second * rows, rows), :] = jnp.where(late, even, odd).astype(jnp.bfloat16)


def pack_lin_kernel(half, *refs):
    sources, decay_ref, gain_ref, outs = refs[:3], refs[3], refs[4], refs[5 : 5 + half]
    scratches, parts_scr = refs[5 + half : 8 + half], refs[8 + half]
    late, me = later(half), place_in(half)
    rows, heads, width = sources[0].shape
    for place, (source, scratch) in enumerate(zip(sources, scratches)):
        spread(source, scratch)
        put_heads(half, outs, scratch, place, 3 + place, rows, heads)
    parts = [*triple(decay_ref[...]), *triple(gain_ref[...])]
    for place, part in enumerate(parts):
        parts_scr[pl.ds(place * heads, heads), :] = part.astype(jnp.float32)
    line = lax.broadcasted_iota(jnp.int32, (PAD, width), 0)
    for step, out in enumerate(outs):
        blocks = []
        for head in range(2):
            at = 2 * jnp.bitwise_xor(me, step) + head
            block = jnp.zeros((PAD, width), jnp.float32)
            for place in range(len(parts)):
                block = jnp.where(line == place, parts_scr[pl.ds(place * heads + at, 1), :], block)
            blocks.append(block)
        even, odd = blocks
        out[pl.ds(6 * rows, PAD), :] = jnp.where(late, odd, even).astype(jnp.bfloat16)
        out[pl.ds(6 * rows + PAD, PAD), :] = jnp.where(late, even, odd).astype(jnp.bfloat16)


def unpack_soft_kernel(half, packed, *refs):
    outs, scratch = refs[:-1], refs[-1]
    rows, heads, width = outs[0].shape
    for place, out in enumerate(outs):
        for source in range(2 * half):
            scratch[pl.ds(soft_head(source, half), rows, stride=heads), :] = packed[
                source, pl.ds(place * rows, rows), :
            ].astype(jnp.float32)
        out[...] = scratch[...].reshape(rows, heads, width).astype(jnp.bfloat16)


def unpack_lin_kernel(half, *refs):
    steps, outs, scratch = refs[:half], refs[half:-1], refs[-1]
    late, me = later(half), place_in(half)
    rows, heads, width = outs[0].shape
    for place, out in enumerate(outs):
        for step, ref in enumerate(steps):
            head = 2 * jnp.bitwise_xor(me, step)
            first = ref[pl.ds(place * rows, rows), :].astype(jnp.float32)
            second = ref[pl.ds((3 + place) * rows, rows), :].astype(jnp.float32)
            scratch[pl.ds(head, rows, stride=heads), :] = jnp.where(late, second, first)
            scratch[pl.ds(head + 1, rows, stride=heads), :] = jnp.where(late, first, second)
        out[...] = scratch[...].reshape(rows, heads, width).astype(jnp.bfloat16)


def soft_part(x_ref, place):
    rows, width = x_ref.shape[1] // 4, x_ref.shape[2]

    def take(tile):
        return x_ref[pl.ds(tile * GROUP, GROUP), pl.ds(place * rows, rows), :].reshape(
            GROUP * rows, width
        )

    return take


def tile_scores(k, q, i, j):
    scores = nt(k(i), q(j))
    if i < j:
        return scores
    key_at = lax.broadcasted_iota(jnp.int32, scores.shape, 0)
    query_at = lax.broadcasted_iota(jnp.int32, scores.shape, 1)
    return jnp.where(key_at <= query_at, scores, -1e30)


def soft_forward_kernel(half, *refs):
    steps, refs = refs[: 2 * half], refs[2 * half :]
    x_ref, lines_ref, dv_ref, own_ref, give_ref, scr, total_scr = refs
    for step, ref in enumerate(steps):
        x_ref[jnp.bitwise_xor(lax.axis_index("ctx"), step)] = ref[...]
    late = later(half)
    spans, rows, width = dv_ref.shape
    wide, scale = GROUP * rows, width**-0.5
    q, k, v, g = (soft_part(x_ref, place) for place in range(4))
    lines_ref[...] = jnp.zeros_like(lines_ref)
    for j in range(spans // GROUP):
        top = None
        for i in range(j + 1):
            scores = tile_scores(k, q, i, j)
            scr[i] = scores
            here = jnp.max(scores, axis=0, keepdims=True)
            top = here if top is None else jnp.maximum(top, here)
        total = jnp.zeros_like(top)
        for i in range(j + 1):
            weights = jnp.exp((scr[i] - top) * scale)
            scr[i] = weights
            total = total + jnp.sum(weights, axis=0, keepdims=True)
        inverse = 1.0 / total
        out_t = None
        for i in range(j + 1):
            low = (scr[i] * inverse).astype(jnp.bfloat16)
            part = tn(v(i), low)
            out_t = part if out_t is None else out_t + part
            part = nn(low, g(j))
            total_scr[i] = part if i == j else total_scr[i] + part
        delta = jnp.sum(jnp.transpose(g(j).astype(jnp.float32)) * out_t, axis=0, keepdims=True)
        for place, line in enumerate((top, inverse, delta)):
            lines_ref[pl.ds(place, 1), pl.ds(j * wide, wide)] = line
    for i in range(spans // GROUP):
        dv_ref[pl.ds(i * GROUP, GROUP)] = (
            total_scr[i].astype(jnp.bfloat16).reshape(GROUP, rows, width)
        )
        total_scr[i] = total_scr[i] + g(i).astype(jnp.float32)
    tiles = half // GROUP
    for i in range(tiles):
        early, after = total_scr[i], total_scr[tiles + i]
        at = pl.ds(i * wide, wide)
        own_ref[at, :] = jnp.where(late, after, early)
        give_ref[at, :] = jnp.where(late, early, after).astype(jnp.bfloat16)


def soft_backward_kernel(x_ref, lines_ref, dv_ref, packed, dk_scr):
    spans, rows, width = dv_ref.shape
    wide, scale = GROUP * rows, width**-0.5
    q, k, v, g = (soft_part(x_ref, place) for place in range(4))
    for j in range(spans // GROUP):
        top, inverse, delta = (
            lines_ref[pl.ds(place, 1), pl.ds(j * wide, wide)] for place in range(3)
        )
        dq_t = None
        for i in range(j + 1):
            probs = jnp.exp((tile_scores(k, q, i, j) - top) * scale) * inverse
            grad_scores = (probs * (nt(v(i), g(j)) - delta)).astype(jnp.bfloat16)
            part = tn(k(i), grad_scores)
            dq_t = part if dq_t is None else dq_t + part
            part = nn(grad_scores, q(j))
            dk_scr[i] = part if i == j else dk_scr[i] + part
        dq = (jnp.transpose(dq_t) * scale).astype(jnp.bfloat16)
        packed[pl.ds(j * GROUP, GROUP), pl.ds(0, rows), :] = dq.reshape(GROUP, rows, width)
    for i in range(spans // GROUP):
        dk = (dk_scr[i] * scale).astype(jnp.bfloat16)
        packed[pl.ds(i * GROUP, GROUP), pl.ds(rows, rows), :] = dk.reshape(GROUP, rows, width)
    packed[:, pl.ds(2 * rows, rows), :] = dv_ref[...]


def span_tables(extra):
    rows = extra.shape[1]
    first = lax.broadcasted_iota(jnp.int32, (rows, rows), 0)
    second = lax.broadcasted_iota(jnp.int32, (rows, rows), 1)
    lower = first >= second
    along = nn(extra, (first <= second).astype(jnp.float32).astype(jnp.bfloat16))
    down = nt(lower.astype(jnp.float32).astype(jnp.bfloat16), extra)
    row = along[0:1] + along[1:2] + along[2:3]
    col = down[:, 0:1] + down[:, 1:2] + down[:, 2:3]
    finish = row[:, rows - 1 : rows]
    return row, col, finish, lower, first <= second


def gain_of(extra):
    wide = extra.astype(jnp.float32)
    return wide[3:4] + wide[4:5] + wide[5:6]


def lin_parts(x_ref, slot, span, rows):
    q, k, v = (
        x_ref[span, pl.ds((slot * 3 + place) * rows, rows), :] for place in range(3)
    )
    return q, k, v, x_ref[span, pl.ds(6 * rows + slot * PAD, PAD), :]


def lin_local_kernel(half, rows, *refs):
    steps, (x_ref, out_ref, states_ref, give_ref) = refs[:half], refs[half:]
    me = place_in(half)
    for step, ref in enumerate(steps):
        x_ref[jnp.bitwise_xor(me, step)] = ref[...]
    width = x_ref.shape[2]
    for slot in range(2):
        state = jnp.zeros((width, width), jnp.float32)
        for span in range(half):
            q, k, v, extra = lin_parts(x_ref, slot, span, rows)
            row, col, finish, lower, _ = span_tables(extra)
            within = jnp.exp(jnp.where(lower, col - row, -1e30))
            pair = (nt(q, k) * within).astype(jnp.bfloat16)
            out = nn(pair, v)
            if span > 0:
                low_state = state.astype(jnp.bfloat16)
                states_ref[slot, span] = low_state
                out = out + jnp.exp(col) * nn(q, low_state)
            else:
                states_ref[slot, span] = jnp.zeros((width, width), jnp.bfloat16)
            out_ref[slot, span] = out
            decayed = (k.astype(jnp.float32) * jnp.exp(finish - col)).astype(jnp.bfloat16)
            state = jnp.exp(finish) * state + tn(decayed, v)
        give_ref[1 - slot] = state.astype(jnp.bfloat16)


def lin_sums_kernel(half, rows, x_ref, own_ref, far_ref, local_ref, given_ref, cot_ref, out_ref, sums_ref):
    late = later(half)
    before = [jnp.where(late, jnp.zeros((1, 1), jnp.float32), -1e30)] * 2
    for span in range(half):
        at = pl.ds(span * rows, rows)
        inner, squares = None, None
        for slot, part_ref in enumerate((own_ref, far_ref)):
            q, _, _, extra = lin_parts(x_ref, slot, span, rows)
            _, col, finish, _, _ = span_tables(extra)
            out = local_ref[slot, span] + jnp.exp(before[slot] + col) * nn(q, given_ref[slot])
            before[slot] = before[slot] + finish
            out_ref[slot, span] = out
            scaled = gain_of(extra) * part_ref[at, :].astype(jnp.float32)
            cot_ref[slot, span] = scaled
            inner = scaled * out if slot == 0 else inner + scaled * out
            squares = out * out if slot == 0 else squares + out * out
        sums_ref[pl.ds(span, 1), :] = jnp.sum(jnp.transpose(squares), axis=0, keepdims=True)
        sums_ref[pl.ds(half + span, 1), :] = jnp.sum(jnp.transpose(inner), axis=0, keepdims=True)


def lin_cot_kernel(half, rows, total_width, x_ref, cot_ref, out_ref, sums_ref, low_ref, state_ref):
    width = cot_ref.shape[3]
    mean = sums_ref[pl.ds(0, half), :] / total_width + epsilon
    root = jnp.sqrt(mean)
    inner = sums_ref[pl.ds(half, half), :] / (total_width * root * mean)
    scalars = jnp.transpose(jnp.concatenate([1.0 / root, inner], axis=0))
    for slot in range(2):
        state = jnp.zeros((width, width), jnp.float32)
        for span in reversed(range(half)):
            q, _, _, extra = lin_parts(x_ref, slot, span, rows)
            _, col, finish, _, _ = span_tables(extra)
            cotangent = (
                cot_ref[slot, span] * scalars[:, span : span + 1]
                - out_ref[slot, span] * scalars[:, half + span : half + span + 1]
            )
            low_cot = cotangent.astype(jnp.bfloat16)
            low_ref[slot, span] = low_cot
            decayed = (q.astype(jnp.float32) * jnp.exp(col)).astype(jnp.bfloat16)
            state = jnp.exp(finish) * state + tn(decayed, low_cot)
        state_ref[1 - slot] = state.astype(jnp.bfloat16)


def lin_own_kernel(half, rows, x_ref, low_ref, states_ref, given_ref, dq_ref, made_ref):
    width = low_ref.shape[3]
    for slot in range(2):
        before = [jnp.zeros((1, 1), jnp.float32)]
        for span in range(half):
            finish = span_tables(lin_parts(x_ref, slot, span, rows)[3])[2]
            before.append(before[-1] + finish)
        given = jnp.where(later(half), given_ref[slot].astype(jnp.float32), 0.0)
        state = jnp.zeros((width, width), jnp.float32)
        for span in reversed(range(half)):
            q, k, v, extra = lin_parts(x_ref, slot, span, rows)
            row, col, finish, lower, upper = span_tables(extra)
            within = jnp.exp(jnp.where(lower, col - row, -1e30))
            within_t = jnp.exp(jnp.where(upper, row - col, -1e30))
            low_cot = low_ref[slot, span]
            grad_pair = (nt(low_cot, v) * within).astype(jnp.bfloat16)
            grad_pair_t = (nt(v, low_cot) * within_t).astype(jnp.bfloat16)
            pair_t = (nt(k, q) * within_t).astype(jnp.bfloat16)
            leading = jnp.exp(col)
            trailing = jnp.exp(finish - col)
            low_state = state.astype(jnp.bfloat16)
            carried = states_ref[slot, span].astype(jnp.float32) + jnp.exp(before[span]) * given
            dq = nn(grad_pair, k) + leading * nt(low_cot, carried.astype(jnp.bfloat16))
            dq_ref[slot, span] = dq.astype(jnp.bfloat16)
            made_ref[slot, 0, span] = nn(grad_pair_t, q) + trailing * nt(v, low_state)
            made_ref[slot, 1, span] = nn(pair_t, low_cot) + trailing * nn(k, low_state)
            decayed = (q.astype(jnp.float32) * leading).astype(jnp.bfloat16)
            state = jnp.exp(finish) * state + tn(decayed, low_cot)


def lin_finish_kernel(half, rows, x_ref, dq_ref, made_ref, state_ref, *refs):
    outs, packed = refs[:half], refs[half]
    for slot in range(2):
        state = state_ref[slot]
        after = jnp.where(later(half), -1e30, jnp.zeros((1, 1), jnp.float32))
        for span in reversed(range(half)):
            _, k, v, extra = lin_parts(x_ref, slot, span, rows)
            _, col, finish, _, _ = span_tables(extra)
            trailing = jnp.exp(after + finish - col)
            after = after + finish
            dk = made_ref[slot, 0, span] + trailing * nt(v, state)
            dv = made_ref[slot, 1, span] + trailing * nn(k, state)
            for place, made in enumerate((dq_ref[slot, span], dk, dv)):
                packed[span, pl.ds((slot * 3 + place) * rows, rows), :] = made.astype(
                    jnp.bfloat16
                )
    for step, out in enumerate(outs):
        out[...] = packed[jnp.bitwise_xor(place_in(half), step)]


def call(name, kernel, out_shape, scratch, cost, *args):
    with jax.named_scope(name):
        return pl.pallas_call(
            kernel,
            out_shape=out_shape,
            scratch_shapes=scratch,
            name=name,
            compiler_params=pltpu.CompilerParams(vmem_limit_bytes=VMEM_BYTES[name.startswith("pack_soft")]),
            cost_estimate=pl.CostEstimate(flops=cost, bytes_accessed=1024, transcendentals=0),
        )(*args)


def by_halves(lin_q, lin_k, lin_v, lin_decay, norm_gain, soft_q, soft_k, soft_v, out_grad):
    rows, heads, width = lin_q.shape
    spans = lax.axis_size("ctx")
    half = spans // 2
    tokens = half * rows
    total_width = heads * lax.axis_size("head") * width
    low = lambda *s: jax.ShapeDtypeStruct(s, jnp.bfloat16)
    full = lambda *s: jax.ShapeDtypeStruct(s, jnp.float32)
    held = lambda *s: pltpu.VMEM(s, jnp.float32)
    bind = functools.partial
    tiles, wide = spans // GROUP, GROUP * rows
    after = lax.optimization_barrier

    def moved(x, pairs):
        return lax.ppermute(x, "ctx", pairs)

    def exchanged(parts):
        return [parts[0]] + [
            moved(parts[step], [(i, i ^ step) for i in range(spans)]) for step in range(1, len(parts))
        ]

    both = [(i, i ^ half) for i in range(spans)]
    turned = held(rows * heads, width)
    mine = (low(rows, heads, width),) * 3
    soft_sent = call(
        "pack_soft", bind(pack_soft_kernel, half), (low(4 * rows, width),) * spans, [turned] * 4, 11960000000,
        soft_q, soft_k, soft_v, out_grad,
    )
    soft_got = exchanged(soft_sent)
    lin_sent = call(
        "pack_lin", bind(pack_lin_kernel, half), (low(6 * rows + 2 * PAD, width),) * half,
        [turned] * 3 + [held(6 * heads, width)], 5980000000,
        lin_q, lin_k, lin_v, lin_decay, norm_gain,
    )
    lin_got = exchanged(lin_sent)
    x, lines, dv, own, give = call(
        "soft_forward", bind(soft_forward_kernel, half),
        (
            low(spans, 4 * rows, width),
            full(8, spans * rows),
            low(spans, rows, width),
            full(tokens, width),
            low(tokens, width),
        ),
        [held(tiles, wide, wide), held(tiles, wide, width)], COST, *soft_got,
    )
    far = moved(give, both)
    lin_got[0], own = after((lin_got[0], own))
    lin_x, local_out, states, state = call(
        "lin_local", bind(lin_local_kernel, half, rows),
        (
            low(half, 6 * rows + 2 * PAD, width),
            full(2, half, rows, width),
            low(2, half, width, width),
            low(2, width, width),
        ),
        [], 13340000000, *lin_got,
    )
    state = moved(state, both)
    soft_made = call(
        "soft_backward", soft_backward_kernel, low(spans, 3 * rows, width),
        [held(tiles, wide, width)], 16560000000, x, lines, dv,
    )
    far, soft_made = after((far, soft_made))
    cot, layer_out, sums = call(
        "lin_sums", bind(lin_sums_kernel, half, rows),
        (full(2, half, rows, width),) * 2 + (full(2 * half, rows),), [], COST,
        lin_x, own, far, local_out, state,
    )
    soft_made, sums = after((soft_made, sums))
    soft_back = lax.all_to_all(soft_made, "ctx", 0, 0, tiled=True)
    for axis, reach in (("head", lax.axis_size("head")), ("ctx", half)):
        count = lax.axis_size(axis)
        sums = after(sums)
        sums = sums + sum(
            lax.ppermute(sums, axis, [(i, i ^ step) for i in range(count)])
            for step in range(1, reach)
        )
    low_cot, late_state = call(
        "lin_cot", bind(lin_cot_kernel, half, rows, total_width),
        (low(2, half, rows, width), low(2, width, width)), [], COST,
        lin_x, cot, layer_out, sums,
    )
    late_state = moved(late_state, both)
    lin_dq, lin_made = call(
        "lin_own", bind(lin_own_kernel, half, rows),
        (low(2, half, rows, width), full(2, 2, half, rows, width)), [], COST,
        lin_x, low_cot, states, state,
    )
    lin_made = call(
        "lin_finish", bind(lin_finish_kernel, half, rows), (low(6 * rows, width),) * half,
        [pltpu.VMEM((half, 6 * rows, width), jnp.bfloat16)], COST,
        lin_x, lin_dq, lin_made, late_state,
    )
    lin_back = exchanged(lin_made)
    soft_out = call(
        "unpack_soft", bind(unpack_soft_kernel, half), mine, [turned], 4600000000, soft_back
    )
    soft_out = list(soft_out)
    lin_back[0], soft_out[0] = after((lin_back[0], soft_out[0]))
    lin_out = call("unpack_lin", bind(unpack_lin_kernel, half), mine, [turned], COST, *lin_back)
    return (*lin_out, *soft_out)


def layers(
    lin_q,
    lin_k,
    lin_v,
    lin_decay,
    norm_gain,
    soft_q,
    soft_k,
    soft_v,
    out_grad,
    block_lists,
    block_counts,
):
    spans = lax.axis_size("ctx")
    if (
        lin_q.shape[0] == BLK
        and spans - 1 <= NSEL
        and lin_q.shape[1] == spans
        and spans >= 4
        and spans & (spans - 1) == 0
    ):
        return by_halves(
            lin_q, lin_k, lin_v, lin_decay, norm_gain, soft_q, soft_k, soft_v, out_grad
        )
    return local(
        lin_q,
        lin_k,
        lin_v,
        lin_decay,
        norm_gain,
        soft_q,
        soft_k,
        soft_v,
        out_grad,
        block_lists,
        block_counts,
    )


def solution(mesh):
    in_specs = (
        P("ctx", "head", None),
        P("ctx", "head", None),
        P("ctx", "head", None),
        P("head", "ctx"),
        P("head", None),
        P("ctx", "head", None),
        P("ctx", "head", None),
        P("ctx", "head", None),
        P("ctx", "head", None),
        P("ctx", None),
        P("ctx"),
    )
    out_specs = (
        P("ctx", "head", None),
        P("ctx", "head", None),
        P("ctx", "head", None),
        P("ctx", "head", None),
        P("ctx", "head", None),
        P("ctx", "head", None),
    )
    return jax.shard_map(layers, mesh=mesh, in_specs=in_specs, out_specs=out_specs, check_vma=False)
```

```python
import functools

import jax
import jax.numpy as jnp
from jax import lax
from jax.experimental import pallas as pl
from jax.experimental.pallas import tpu as pltpu
from jax.sharding import PartitionSpec as P

BLK = 128
NSEL = 16
PAD = 16
GROUP = 2
COST = 1024
VMEM_BYTES = (24 * 1024 * 1024, 56 * 1024 * 1024)


epsilon = 1e-05
exact_precision = lax.Precision.HIGHEST


def carried_in(part, axis, combine, identity, reverse):
    count = lax.axis_size(axis)
    place = lax.axis_index(axis)
    ahead = count - 1 - place if reverse else place
    gathered = jax.tree.map(lambda a: lax.all_gather(a, axis), part)
    state = jax.tree.map(lambda a, e: jnp.zeros_like(a) + jnp.asarray(e, a.dtype), part, identity)

    def one(lap, state):
        source = count - 1 - lap if reverse else lap
        return combine(
            state, jax.tree.map(lambda a: lax.dynamic_index_in_dim(a, source, 0, False), gathered)
        )

    return lax.fori_loop(0, ahead, one, state)


def decay_tables(decays):
    running = jnp.cumsum(decays, axis=1)
    finish = running[:, -1]
    length = decays.shape[1]
    below_diag = (jnp.arange(length)[:, None] >= jnp.arange(length)[None, :])[None]
    spread = running[:, :, None] - running[:, None, :]
    within = jnp.where(below_diag, jnp.exp(jnp.where(below_diag, spread, 0.0)), 0.0)
    return (jnp.exp(finish), jnp.exp(finish[:, None] - running), jnp.exp(running), within)


def chain_join(earlier, later):
    return (earlier[0] * later[0], later[0][:, None, None] * earlier[1] + later[1])


def sparse_grads(queries, grads_out, key_rows, value_rows, allowed):
    score_scale = queries.shape[-1] ** (-0.5)
    scores = (
        jnp.einsum("bqhd,bkhd->bhqk", queries, key_rows, preferred_element_type=jnp.float32)
        * score_scale
    )
    key_mask = allowed[:, None]
    scores = jnp.where(key_mask, scores, -1e30)
    row_max = jnp.max(scores, axis=-1, keepdims=True)
    weights = jnp.where(key_mask, jnp.exp(scores - row_max), 0.0)
    softmax_probs = weights / jnp.sum(weights, axis=-1, keepdims=True)
    rounded = softmax_probs.astype(jnp.bfloat16)
    outputs = jnp.einsum("bhqk,bkhd->bqhd", rounded, value_rows, preferred_element_type=jnp.float32)
    row_delta = jnp.sum(grads_out.astype(jnp.float32) * outputs, axis=-1)
    grad_probs = jnp.einsum(
        "bqhd,bkhd->bhqk", grads_out, value_rows, preferred_element_type=jnp.float32
    )
    grad_scores = (
        softmax_probs * (grad_probs - jnp.transpose(row_delta, (0, 2, 1))[..., None])
    ).astype(jnp.bfloat16)
    query_gradient = (
        jnp.einsum("bhqk,bkhd->bqhd", grad_scores, key_rows, preferred_element_type=jnp.float32)
        * score_scale
    )
    key_gradient = (
        jnp.einsum("bhqk,bqhd->bkhd", grad_scores, queries, preferred_element_type=jnp.float32)
        * score_scale
    )
    value_gradient = jnp.einsum(
        "bhqk,bqhd->bkhd", rounded, grads_out, preferred_element_type=jnp.float32
    )
    return (query_gradient, key_gradient, value_gradient)


def local(
    lin_q,
    lin_k,
    lin_v,
    lin_decay,
    norm_gain,
    soft_q,
    soft_k,
    soft_v,
    out_grad,
    block_lists,
    block_counts,
):
    tok_rows, heads_here, head_width = lin_q.shape
    blocks_here = tok_rows // BLK
    span_count = lax.axis_size("ctx")
    own_span = lax.axis_index("ctx")
    total_width = heads_here * lax.axis_size("head") * head_width
    complete_query = lin_q.astype(jnp.float32)
    complete_key = lin_k.astype(jnp.float32)
    complete_value = lin_v.astype(jnp.float32)
    carry_decay, trailing_decay, leading_decay, within = decay_tables(lin_decay)
    state_here = jnp.einsum(
        "boz,bor->ozr",
        complete_key * trailing_decay.T[:, :, None],
        complete_value,
        precision=exact_precision,
    )
    identity = (jnp.ones_like(carry_decay), jnp.zeros_like(state_here))
    incoming_state = carried_in((carry_decay, state_here), "ctx", chain_join, identity, False)[1]
    pair_weights = (
        jnp.einsum("thk,shk->hts", lin_q, lin_k, preferred_element_type=jnp.float32) * within
    )
    layer_out = jnp.einsum("hts,shv->thv", pair_weights, complete_value, precision=exact_precision)
    layer_out = layer_out + leading_decay.T[:, :, None] * jnp.einsum(
        "wfg,fgl->wfl", complete_query, incoming_state, precision=exact_precision
    )
    squares = lax.psum(jnp.sum(layer_out * layer_out, axis=(1, 2)), "head")
    root_mean = jnp.sqrt(squares / total_width + epsilon)
    norm_scale = norm_gain[None]
    all_lists, all_counts = (
        lax.all_gather(block_lists, "ctx", axis=0, tiled=True),
        lax.all_gather(block_counts, "ctx", axis=0, tiled=True),
    )
    entries = blocks_here * NSEL
    every_live = (
        jnp.arange(NSEL)[None, None, :] < all_counts.reshape(span_count, blocks_here)[:, :, None]
    ).reshape(span_count, entries)
    owner_hits = every_live & (all_lists // blocks_here == own_span)
    wanted_here = jnp.max(jnp.where(owner_hits, all_lists % blocks_here, -1), axis=1)
    my_live = jnp.arange(NSEL)[None, :] < block_counts[:, None]
    flat_owner = (block_lists // blocks_here).reshape(entries)
    flat_live = my_live.reshape(entries)
    key_blocks = soft_k.reshape(blocks_here, BLK, heads_here, head_width)
    value_blocks = soft_v.reshape(blocks_here, BLK, heads_here, head_width)
    picked = jnp.clip(wanted_here, 0, blocks_here - 1)
    present = (wanted_here >= 0)[:, None, None, None]
    nothing = jnp.zeros((), jnp.bfloat16)
    send_keys = jnp.where(present, key_blocks[picked], nothing)
    send_values = jnp.where(present, value_blocks[picked], nothing)
    got_keys, got_values = (
        lax.all_to_all(send_keys, "ctx", split_axis=0, concat_axis=0, tiled=True),
        lax.all_to_all(send_values, "ctx", split_axis=0, concat_axis=0, tiled=True),
    )
    listed_keys = jnp.take(got_keys, flat_owner, axis=0).reshape(
        blocks_here, NSEL * BLK, heads_here, head_width
    )
    listed_values = jnp.take(got_values, flat_owner, axis=0).reshape(
        blocks_here, NSEL * BLK, heads_here, head_width
    )
    key_rows = jnp.concatenate([key_blocks, listed_keys], axis=1)
    value_rows = jnp.concatenate([value_blocks, listed_values], axis=1)
    causal = jnp.arange(BLK)[:, None] >= jnp.arange(BLK)[None, :]
    remote_mask = jnp.broadcast_to(
        jnp.repeat(my_live, BLK, axis=1)[:, None, :], (blocks_here, BLK, NSEL * BLK)
    )
    allowed = jnp.concatenate(
        [jnp.broadcast_to(causal, (blocks_here, BLK, BLK)), remote_mask], axis=2
    )
    query_blocks = soft_q.reshape(blocks_here, BLK, heads_here, head_width)
    grad_blocks = out_grad.reshape(blocks_here, BLK, heads_here, head_width)
    query_gradient, key_gradient, value_gradient = sparse_grads(
        query_blocks, grad_blocks, key_rows, value_rows, allowed
    )
    soft_dq = query_gradient.reshape(tok_rows, heads_here, head_width).astype(jnp.bfloat16)
    routing = (
        flat_live[None, :] & (flat_owner[None, :] == jnp.arange(span_count)[:, None])
    ).astype(jnp.float32)
    remote_key = key_gradient[:, BLK:].reshape(entries, BLK, heads_here, head_width)
    remote_value = value_gradient[:, BLK:].reshape(entries, BLK, heads_here, head_width)
    part_key = jnp.einsum("oe,exhd->oxhd", routing, remote_key, precision=exact_precision).astype(
        jnp.bfloat16
    )
    part_value = jnp.einsum(
        "oe,exhd->oxhd", routing, remote_value, precision=exact_precision
    ).astype(jnp.bfloat16)
    back_key, back_value = (
        lax.all_to_all(part_key, "ctx", split_axis=0, concat_axis=0, tiled=True),
        lax.all_to_all(part_value, "ctx", split_axis=0, concat_axis=0, tiled=True),
    )
    placing = (wanted_here[:, None] == jnp.arange(blocks_here)[None, :]).astype(jnp.float32)
    added_key = jnp.einsum(
        "rb,rxhd->bxhd", placing, back_key.astype(jnp.float32), precision=exact_precision
    ).reshape(tok_rows, heads_here, head_width)
    added_value = jnp.einsum(
        "rb,rxhd->bxhd", placing, back_value.astype(jnp.float32), precision=exact_precision
    ).reshape(tok_rows, heads_here, head_width)
    soft_dk = (key_gradient[:, :BLK].reshape(tok_rows, heads_here, head_width) + added_key).astype(
        jnp.bfloat16
    )
    value_total = value_gradient[:, :BLK].reshape(tok_rows, heads_here, head_width) + added_value
    soft_dv = value_total.astype(jnp.bfloat16)
    cotangent = out_grad.astype(jnp.float32) + value_total
    inner_total = lax.psum(jnp.sum(norm_scale * cotangent * layer_out, axis=(1, 2)), "head")
    linear_cotangent = (
        norm_scale * cotangent / root_mean[:, None, None]
        - layer_out * (inner_total / (total_width * root_mean**3))[:, None, None]
    )
    reverse_state = carried_in(
        (
            carry_decay,
            jnp.einsum(
                "boz,bor->ozr",
                complete_query * leading_decay.T[:, :, None],
                linear_cotangent,
                precision=exact_precision,
            ),
        ),
        "ctx",
        chain_join,
        identity,
        True,
    )[1]
    grad_pair = (
        jnp.einsum("thv,shv->hts", linear_cotangent, complete_value, precision=exact_precision)
        * within
    )
    lin_dq = jnp.einsum("hts,shk->thk", grad_pair, complete_key, precision=exact_precision)
    lin_dq = lin_dq + leading_decay.T[:, :, None] * jnp.einsum(
        "fqs,qrs->fqr", linear_cotangent, incoming_state, precision=exact_precision
    )
    lin_dk = jnp.einsum("hts,thk->shk", grad_pair, complete_query, precision=exact_precision)
    lin_dk = lin_dk + trailing_decay.T[:, :, None] * jnp.einsum(
        "fut,ujt->fuj", complete_value, reverse_state, precision=exact_precision
    )
    lin_dv = jnp.einsum("hts,thv->shv", pair_weights, linear_cotangent, precision=exact_precision)
    lin_dv = lin_dv + trailing_decay.T[:, :, None] * jnp.einsum(
        "zpu,pux->zpx", complete_key, reverse_state, precision=exact_precision
    )
    return (
        lin_dq.astype(jnp.bfloat16),
        lin_dk.astype(jnp.bfloat16),
        lin_dv.astype(jnp.bfloat16),
        soft_dq,
        soft_dk,
        soft_dv,
    )


def triple(x):
    top = x.astype(jnp.bfloat16)
    rest = x - top.astype(jnp.float32)
    middle = rest.astype(jnp.bfloat16)
    low = (rest - middle.astype(jnp.float32)).astype(jnp.bfloat16)
    return top, middle, low


def nt(a, b):
    return lax.dot_general(a, b, (((1,), (1,)), ((), ())), preferred_element_type=jnp.float32)


def nn(a, b):
    return lax.dot_general(a, b, (((1,), (0,)), ((), ())), preferred_element_type=jnp.float32)


def tn(a, b):
    return lax.dot_general(a, b, (((0,), (0,)), ((), ())), preferred_element_type=jnp.float32)


def later(half):
    return lax.axis_index("ctx") >= half


def place_in(half):
    return lax.rem(lax.axis_index("ctx"), half)


def spread(source, scratch):
    rows, heads, width = source.shape
    scratch[...] = source[...].astype(jnp.float32).reshape(rows * heads, width)


def head_of(scratch, head, heads):
    return scratch[pl.ds(head, scratch.shape[0] // heads, stride=heads), :]


def put_heads(half, outs, scratch, first, second, rows, heads):
    late, me = later(half), place_in(half)
    for step, out in enumerate(outs):
        head = 2 * jnp.bitwise_xor(me, step)
        even, odd = head_of(scratch, head, heads), head_of(scratch, head + 1, heads)
        out[pl.ds(first * rows, rows), :] = jnp.where(late, odd, even).astype(jnp.bfloat16)
        out[pl.ds(second * rows, rows), :] = jnp.where(late, even, odd).astype(jnp.bfloat16)


def pack_soft_kernel(half, *refs):
    sources, outs, scratches = refs[:4], refs[4 : 4 + half], refs[4 + half :]
    rows, heads, _ = sources[0].shape
    for place, (source, scratch) in enumerate(zip(sources, scratches)):
        spread(source, scratch)
        put_heads(half, outs, scratch, place, 4 + place, rows, heads)


def pack_lin_kernel(half, *refs):
    sources, decay_ref, gain_ref, outs = refs[:3], refs[3], refs[4], refs[5 : 5 + half]
    scratches, parts_scr = refs[5 + half : 8 + half], refs[8 + half]
    late, me = later(half), place_in(half)
    rows, heads, width = sources[0].shape
    for place, (source, scratch) in enumerate(zip(sources, scratches)):
        spread(source, scratch)
        put_heads(half, outs, scratch, place, 3 + place, rows, heads)
    parts = [*triple(decay_ref[...]), *triple(gain_ref[...])]
    for place, part in enumerate(parts):
        parts_scr[pl.ds(place * heads, heads), :] = part.astype(jnp.float32)
    line = lax.broadcasted_iota(jnp.int32, (PAD, width), 0)
    for step, out in enumerate(outs):
        blocks = []
        for head in range(2):
            at = 2 * jnp.bitwise_xor(me, step) + head
            block = jnp.zeros((PAD, width), jnp.float32)
            for place in range(len(parts)):
                block = jnp.where(line == place, parts_scr[pl.ds(place * heads + at, 1), :], block)
            blocks.append(block)
        even, odd = blocks
        out[pl.ds(6 * rows, PAD), :] = jnp.where(late, odd, even).astype(jnp.bfloat16)
        out[pl.ds(6 * rows + PAD, PAD), :] = jnp.where(late, even, odd).astype(jnp.bfloat16)


def unpack_kernel(half, *refs):
    steps, outs, scratch = refs[:half], refs[half:-1], refs[-1]
    late, me = later(half), place_in(half)
    rows, heads, width = outs[0].shape
    for place, out in enumerate(outs):
        for step, ref in enumerate(steps):
            head = 2 * jnp.bitwise_xor(me, step)
            first = ref[pl.ds(place * rows, rows), :].astype(jnp.float32)
            second = ref[pl.ds((3 + place) * rows, rows), :].astype(jnp.float32)
            scratch[pl.ds(head, rows, stride=heads), :] = jnp.where(late, second, first)
            scratch[pl.ds(head + 1, rows, stride=heads), :] = jnp.where(late, first, second)
        out[...] = scratch[...].reshape(rows, heads, width).astype(jnp.bfloat16)


def soft_gather_kernel(half, *refs):
    steps, x_ref, give_ref = refs[:half], refs[half], refs[half + 1]
    late, me = later(half), place_in(half)
    rows = x_ref.shape[1] // 8
    for step, ref in enumerate(steps):
        source = jnp.bitwise_xor(me, step)
        x_ref[source] = ref[...]
        give_ref[source] = jnp.where(
            late, ref[pl.ds(0, rows), :], ref[pl.ds(rows, rows), :]
        )


def soft_blocks(half, x_ref, recv_ref):
    late = later(half)
    rows = x_ref.shape[1] // 8
    width = x_ref.shape[2]

    def own(slot, place):
        def take(tile):
            return x_ref[
                pl.ds(tile * GROUP, GROUP), pl.ds((slot * 4 + place) * rows, rows), :
            ].reshape(GROUP * rows, width)

        return take

    def other(place):
        def take(tile):
            return recv_ref[place][pl.ds(tile * GROUP, GROUP)].reshape(GROUP * rows, width)

        return take

    def either(if_late, if_early):
        return lambda tile: jnp.where(late, if_late(tile), if_early(tile))

    zero = (own(0, 0), own(0, 1), own(0, 2), own(0, 3), True)
    same = (own(1, 0), own(1, 1), own(1, 2), own(1, 3), True)
    rect = (
        either(own(1, 0), other(0)),
        either(other(0), own(1, 1)),
        either(other(1), own(1, 2)),
        either(own(1, 3), other(1)),
        False,
    )
    return zero, same, rect


def tile_scores(block, i, j, wide):
    q, k, _, _, causal = block
    scores = nt(k(i), q(j))
    if not causal or i < j:
        return scores
    key_at = lax.broadcasted_iota(jnp.int32, (wide, wide), 0)
    query_at = lax.broadcasted_iota(jnp.int32, (wide, wide), 1)
    return jnp.where(key_at <= query_at, scores, -1e30)


def tiles_of(block, j, tiles):
    return range(j + 1) if block[4] else range(tiles)


def block_stats(block, scr, tiles, wide, scale):
    tops, totals, dots = [], [], []
    _, _, v, g, _ = block
    for j in range(tiles):
        top = None
        for i in tiles_of(block, j, tiles):
            scores = tile_scores(block, i, j, wide)
            scr[i, j] = scores
            here = jnp.max(scores, axis=0, keepdims=True)
            top = here if top is None else jnp.maximum(top, here)
        total = jnp.zeros_like(top)
        out_t = None
        for i in tiles_of(block, j, tiles):
            weights = jnp.exp((scr[i, j] - top) * scale)
            scr[i, j] = weights
            total = total + jnp.sum(weights, axis=0, keepdims=True)
            part = tn(v(i), weights.astype(jnp.bfloat16))
            out_t = part if out_t is None else out_t + part
        grads_t = jnp.transpose(g(j).astype(jnp.float32))
        tops.append(top)
        totals.append(total)
        dots.append(jnp.sum(grads_t * out_t, axis=0, keepdims=True))
    return tops, totals, dots


def joined(mine, other, use, scale):
    top, total, dot = mine
    top_other, total_other, dot_other = other
    top_other = jnp.where(use, top_other, top)
    both = jnp.maximum(top, top_other)
    here = jnp.exp((top - both) * scale)
    there = jnp.where(use, jnp.exp((top_other - both) * scale), 0.0)
    inverse = 1.0 / (total * here + total_other * there)
    return here * inverse, (dot * here + dot_other * there) * inverse


def block_grads(block, factors, deltas, scr, tiles, scale):
    q, k, v, g, _ = block
    dq, dk, dv = [], [None] * tiles, [None] * tiles
    add = lambda total, part: part if total is None else total + part
    for j in range(tiles):
        dq_t = None
        for i in tiles_of(block, j, tiles):
            probs = scr[i, j] * factors[j]
            dv[i] = add(dv[i], nn(probs.astype(jnp.bfloat16), g(j)))
            grad_probs = nt(v(i), g(j))
            grad_scores = (probs * (grad_probs - deltas[j])).astype(jnp.bfloat16)
            dq_t = add(dq_t, tn(k(i), grad_scores))
            dk[i] = add(dk[i], nn(grad_scores, q(j)))
        dq.append(jnp.transpose(dq_t) * scale)
    return dq, [x * scale for x in dk], dv


def put_lines(ref, first, lines, wide):
    for place, row in enumerate(lines):
        for j, piece in enumerate(row):
            ref[pl.ds(first + place, 1), pl.ds(j * wide, wide)] = piece


def get_lines(ref, first, j, wide):
    return [ref[pl.ds(first + place, 1), pl.ds(j * wide, wide)] for place in range(3)]


def soft_shape(half, x_ref):
    rows, width = x_ref.shape[1] // 8, x_ref.shape[2]
    return half // GROUP, GROUP * rows, width**-0.5


def soft_stats_kernel(half, x_ref, lines_ref, give_ref, scr):
    late, rows = later(half), x_ref.shape[1] // 8
    for span in range(half):
        give_ref[span] = jnp.where(
            late, x_ref[span, pl.ds(3 * rows, rows), :], x_ref[span, pl.ds(2 * rows, rows), :]
        )
    tiles, wide, scale = soft_shape(half, x_ref)
    zero, same, _ = soft_blocks(half, x_ref, None)
    lines_ref[...] = jnp.zeros_like(lines_ref)
    put_lines(lines_ref, 0, block_stats(zero, scr, tiles, wide, scale), wide)
    put_lines(lines_ref, 3, block_stats(same, scr, tiles, wide, scale), wide)


def rect_joined(late, lines_ref, far_ref, lines, j, wide, scale):
    near, far = get_lines(lines_ref, 3, j, wide), get_lines(far_ref, 0, j, wide)
    other = [jnp.where(late, a, b) for a, b in zip(near, far)]
    return joined([line[j] for line in lines], other, True, scale)


def soft_first_kernel(half, x_ref, recv_ref, lines_ref, send_ref, rect_ref, scr):
    late = later(half)
    tiles, wide, scale = soft_shape(half, x_ref)
    _, same, rect = soft_blocks(half, x_ref, (recv_ref, recv_ref))
    grads = same[3]
    tops, totals = [], []
    rect_ref[...] = jnp.zeros_like(rect_ref)
    dv = [None] * tiles
    for j in range(tiles):
        top = None
        for i in range(tiles):
            scores = tile_scores(rect, i, j, wide)
            scr[i, j] = scores
            here = jnp.max(scores, axis=0, keepdims=True)
            top = here if top is None else jnp.maximum(top, here)
        total = jnp.zeros_like(top)
        for i in range(tiles):
            weights = jnp.exp((scr[i, j] - top) * scale)
            scr[i, j] = weights
            total = total + jnp.sum(weights, axis=0, keepdims=True)
        tops.append(top)
        totals.append(total)
        zeros = [jnp.zeros_like(top)] * tiles
        factor, _ = rect_joined(
            late, lines_ref, lines_ref, ([top] * tiles, [total] * tiles, zeros), j, wide, scale
        )
        for i in range(tiles):
            part = nn((scr[i, j] * factor).astype(jnp.bfloat16), grads(j))
            dv[i] = part if dv[i] is None else dv[i] + part
    put_lines(rect_ref, 0, (tops, totals), wide)
    for i in range(tiles):
        send_ref[pl.ds(i * wide, wide), :] = dv[i].astype(jnp.bfloat16)

    @pl.when(jnp.logical_not(late))
    def _():
        width = x_ref.shape[2]
        for place, part in enumerate(triple(rect_ref[...])):
            for piece in range(rect_ref.shape[1] // width):
                send_ref[pl.ds((place * tiles * GROUP + piece) * PAD, PAD), :] = jnp.concatenate(
                    [part[:, piece * width : (piece + 1) * width]] * (PAD // 8), axis=0
                )


def soft_rect_kernel(
    half, x_ref, recv_ref, recv_two_ref, lines_ref, far_ref, made_ref, rect_ref, scr
):
    late = later(half)
    tiles, wide, scale = soft_shape(half, x_ref)
    _, _, rect = soft_blocks(half, x_ref, (recv_ref, recv_two_ref))
    lines = block_stats(rect, scr, tiles, wide, scale)
    rect_ref[...] = jnp.zeros_like(rect_ref)
    put_lines(rect_ref, 0, lines, wide)
    both = [rect_joined(late, lines_ref, far_ref, lines, j, wide, scale) for j in range(tiles)]
    factors, deltas = zip(*both)
    dq, dk, dv = block_grads(rect, factors, deltas, scr, tiles, scale)
    for j in range(tiles):
        at = pl.ds(j * wide, wide)
        for place, made in enumerate((dq[j], dk[j], dv[j])):
            made_ref[place, at, :] = made


def sent_lines(ref, pieces, lines_ref):
    width = ref.shape[1]
    for piece in range(pieces):
        parts = [
            ref[pl.ds((place * pieces + piece) * PAD, PAD), :].astype(jnp.float32)[0:8]
            for place in range(3)
        ]
        lines_ref[:, pl.ds(piece * width, width)] = parts[0] + parts[1] + parts[2]


def causal_grads(half, slot, x_ref, lines_ref, far_ref, scr):
    tiles, wide, scale = soft_shape(half, x_ref)
    block = soft_blocks(half, x_ref, None)[slot]
    factors, deltas = [], []
    for j in range(tiles):
        mine = get_lines(lines_ref, 3 * slot, j, wide)
        factor, delta = joined(mine, get_lines(far_ref, 0, j, wide), later(half), scale)
        factors.append(factor)
        deltas.append(delta)
        for i in range(j + 1):
            scr[i, j] = jnp.exp((tile_scores(block, i, j, wide) - mine[0]) * scale)
    return block_grads(block, factors, deltas, scr, tiles, scale)


def soft_zero_kernel(half, x_ref, lines_ref, far_ref, made_ref, scr):
    tiles, wide, _ = soft_shape(half, x_ref)
    grads = causal_grads(half, 0, x_ref, lines_ref, far_ref, scr)
    for j in range(tiles):
        for place in range(3):
            made_ref[place, pl.ds(j * wide, wide), :] = grads[place][j]


def soft_value_kernel(half, x_ref, lines_ref, sent_ref, dv_ref, far_ref):
    sent_lines(sent_ref, half, far_ref)
    tiles, wide, scale = soft_shape(half, x_ref)
    zero, _, _ = soft_blocks(half, x_ref, None)
    dv = [None] * tiles
    for j in range(tiles):
        mine = get_lines(lines_ref, 0, j, wide)
        factor, _ = joined(mine, get_lines(far_ref, 0, j, wide), later(half), scale)
        for i in range(j + 1):
            weights = jnp.exp((tile_scores(zero, i, j, wide) - mine[0]) * scale)
            part = nn((weights * factor).astype(jnp.bfloat16), zero[3](j))
            dv[i] = part if dv[i] is None else dv[i] + part
    for i in range(tiles):
        dv_ref[pl.ds(i * wide, wide), :] = dv[i]


def soft_same_kernel(half, x_ref, lines_ref, rect_lines_ref, rect_ref, packed, dv_ref, scr):
    late = later(half)
    tiles, wide, _ = soft_shape(half, x_ref)
    rows = wide // GROUP
    grads = causal_grads(half, 1, x_ref, lines_ref, rect_lines_ref, scr)
    for j in range(tiles):
        at = pl.ds(j * wide, wide)
        for place in range(3):
            added = rect_ref[place, at, :]
            made = grads[place][j] + (
                jnp.where(late, added, 0.0) if place == 0 else jnp.where(late, 0.0, added)
            )
            packed[pl.ds(j * GROUP, GROUP), pl.ds(place * rows, rows), :] = made.astype(
                jnp.bfloat16
            ).reshape(GROUP, rows, made.shape[1])
            if place == 2:
                dv_ref[at, :] = made


def decay_lines(half, rows, x_ref):
    firsts = [
        x_ref[span, pl.ds(6 * rows + slot * PAD, PAD), :].astype(jnp.float32)
        for slot in range(2)
        for span in range(half)
    ]
    parts = [
        jnp.concatenate([block[place : place + 1] for block in firsts], axis=0)
        for place in range(3)
    ]
    first = lax.broadcasted_iota(jnp.int32, (rows, rows), 0)
    second = lax.broadcasted_iota(jnp.int32, (rows, rows), 1)
    ones = (first <= second).astype(jnp.float32).astype(jnp.bfloat16)
    sums = nn(jnp.concatenate(parts, axis=0).astype(jnp.bfloat16), ones)
    count = 2 * half
    return sums[:count] + sums[count : 2 * count] + sums[2 * count :]


def tables(lines):
    count, rows = lines.shape
    columns = jnp.transpose(lines)
    return [
        (lines[c : c + 1], columns[:, c : c + 1], lines[c : c + 1, rows - 1 : rows])
        for c in range(count)
    ]


def triangle(rows):
    first = lax.broadcasted_iota(jnp.int32, (rows, rows), 0)
    second = lax.broadcasted_iota(jnp.int32, (rows, rows), 1)
    return first >= second, first <= second


def gain_of(extra):
    wide = extra.astype(jnp.float32)
    return wide[3:4] + wide[4:5] + wide[5:6]


def lin_parts(x_ref, slot, span, rows):
    q, k, v = (
        x_ref[span, pl.ds((slot * 3 + place) * rows, rows), :] for place in range(3)
    )
    return q, k, v, x_ref[span, pl.ds(6 * rows + slot * PAD, PAD), :]


def lin_local_kernel(half, rows, *refs):
    steps, (x_ref, lines_ref, out_ref, states_ref, give_ref) = refs[:half], refs[half + 1 :]
    me = place_in(half)
    for step, ref in enumerate(steps):
        x_ref[jnp.bitwise_xor(me, step)] = ref[...]
    width = x_ref.shape[2]
    lines = decay_lines(half, rows, x_ref)
    lines_ref[...] = lines
    chunks = tables(lines)
    lower, _ = triangle(rows)
    for slot in range(2):
        state = None
        for span in range(half):
            _, k, v, _ = lin_parts(x_ref, slot, span, rows)
            _, col, finish = chunks[slot * half + span]
            decayed = (k.astype(jnp.float32) * jnp.exp(finish - col)).astype(jnp.bfloat16)
            if span:
                states_ref[slot, span] = state.astype(jnp.bfloat16)
                state = jnp.exp(finish) * state + tn(decayed, v)
            else:
                states_ref[slot, span] = jnp.zeros((width, width), jnp.bfloat16)
                state = tn(decayed, v)
        give_ref[1 - slot] = state.astype(jnp.bfloat16)
    for slot in range(2):
        for span in range(half):
            q, k, v, _ = lin_parts(x_ref, slot, span, rows)
            row, col, _ = chunks[slot * half + span]
            within = jnp.exp(jnp.where(lower, col - row, -1e30))
            out = nn((nt(q, k) * within).astype(jnp.bfloat16), v)
            if span:
                out = out + jnp.exp(col) * nn(q, states_ref[slot, span])
            out_ref[slot, span] = out


def lin_sums_kernel(
    half, rows, x_ref, lines_ref, soft_ref, zero_ref, same_ref, dv_ref, local_ref, given_ref,
    cot_ref, out_ref, sums_ref,
):
    late = later(half)
    chunks = tables(lines_ref[...])
    before = [jnp.where(late, jnp.zeros((1, 1), jnp.float32), -1e30)] * 2
    for span in range(half):
        at = pl.ds(span * rows, rows)
        inner, squares = None, None
        for slot in range(2):
            q, _, _, extra = lin_parts(x_ref, slot, span, rows)
            _, col, finish = chunks[slot * half + span]
            out = local_ref[slot, span] + jnp.exp(before[slot] + col) * nn(q, given_ref[slot])
            before[slot] = before[slot] + finish
            out_ref[slot, span] = out
            cot = soft_ref[span, pl.ds((slot * 4 + 3) * rows, rows), :].astype(jnp.float32)
            if slot == 0:
                cot = cot + zero_ref[at, :]
                cot = cot + jnp.where(late, 0.0, dv_ref[at, :].astype(jnp.float32))
            else:
                cot = cot + same_ref[at, :]
            scaled = gain_of(extra) * cot
            cot_ref[slot, span] = scaled
            inner = scaled * out if slot == 0 else inner + scaled * out
            squares = out * out if slot == 0 else squares + out * out
        sums_ref[pl.ds(span, 1), :] = jnp.sum(jnp.transpose(squares), axis=0, keepdims=True)
        sums_ref[pl.ds(half + span, 1), :] = jnp.sum(jnp.transpose(inner), axis=0, keepdims=True)


def lin_cot_kernel(
    half, rows, total_width, x_ref, lines_ref, cot_ref, out_ref, sums_ref, low_ref, state_ref
):
    mean = sums_ref[pl.ds(0, half), :] / total_width + epsilon
    root = jnp.sqrt(mean)
    inner = sums_ref[pl.ds(half, half), :] / (total_width * root * mean)
    scalars = jnp.transpose(jnp.concatenate([1.0 / root, inner], axis=0))
    chunks = tables(lines_ref[...])
    for slot in range(2):
        before = jnp.zeros((1, 1), jnp.float32)
        state = None
        for span in range(half):
            q, _, _, _ = lin_parts(x_ref, slot, span, rows)
            _, col, finish = chunks[slot * half + span]
            cotangent = (
                cot_ref[slot, span] * scalars[:, span : span + 1]
                - out_ref[slot, span] * scalars[:, half + span : half + span + 1]
            )
            low_cot = cotangent.astype(jnp.bfloat16)
            low_ref[slot, span] = low_cot
            decayed = (q.astype(jnp.float32) * jnp.exp(before + col)).astype(jnp.bfloat16)
            before = before + finish
            part = tn(decayed, low_cot)
            state = part if state is None else state + part
        state_ref[1 - slot] = state.astype(jnp.bfloat16)


def lin_own_kernel(half, rows, x_ref, lines_ref, low_ref, states_ref, given_ref, dq_ref, made_ref):
    chunks = tables(lines_ref[...])
    lower, upper = triangle(rows)
    late = later(half)
    for slot in range(2):
        given = jnp.where(late, given_ref[slot].astype(jnp.float32), 0.0)
        before = [jnp.zeros((1, 1), jnp.float32)]
        for span in range(half):
            before.append(before[-1] + chunks[slot * half + span][2])
        state = None
        for span in reversed(range(half)):
            q, k, v, _ = lin_parts(x_ref, slot, span, rows)
            row, col, finish = chunks[slot * half + span]
            within = jnp.exp(jnp.where(lower, col - row, -1e30))
            within_t = jnp.exp(jnp.where(upper, row - col, -1e30))
            low_cot = low_ref[slot, span]
            grad_pair = (nt(low_cot, v) * within).astype(jnp.bfloat16)
            grad_pair_t = (nt(v, low_cot) * within_t).astype(jnp.bfloat16)
            pair_t = (nt(k, q) * within_t).astype(jnp.bfloat16)
            leading = jnp.exp(col)
            trailing = jnp.exp(finish - col)
            carried = states_ref[slot, span].astype(jnp.float32) + jnp.exp(before[span]) * given
            dq = nn(grad_pair, k) + leading * nt(low_cot, carried.astype(jnp.bfloat16))
            dk = nn(grad_pair_t, q)
            dv = nn(pair_t, low_cot)
            decayed = (q.astype(jnp.float32) * leading).astype(jnp.bfloat16)
            part = tn(decayed, low_cot)
            if state is None:
                state = part
            else:
                low_state = state.astype(jnp.bfloat16)
                dk = dk + trailing * nt(v, low_state)
                dv = dv + trailing * nn(k, low_state)
                state = jnp.exp(finish) * state + part
            dq_ref[slot, span] = dq.astype(jnp.bfloat16)
            made_ref[slot, 0, span] = dk
            made_ref[slot, 1, span] = dv


def lin_finish_kernel(half, rows, x_ref, lines_ref, dq_ref, made_ref, state_ref, *refs):
    outs, packed = refs[:half], refs[half]
    chunks = tables(lines_ref[...])
    me = place_in(half)
    for slot in range(2):
        state = state_ref[slot]
        after = jnp.where(later(half), -1e30, jnp.zeros((1, 1), jnp.float32))
        for span in reversed(range(half)):
            _, k, v, _ = lin_parts(x_ref, slot, span, rows)
            _, col, finish = chunks[slot * half + span]
            trailing = jnp.exp(after + finish - col)
            after = after + finish
            dk = made_ref[slot, 0, span] + trailing * nt(v, state)
            dv = made_ref[slot, 1, span] + trailing * nn(k, state)
            packed[span, pl.ds(slot * 3 * rows, rows), :] = dq_ref[slot, span]
            packed[span, pl.ds((slot * 3 + 1) * rows, rows), :] = dk.astype(jnp.bfloat16)
            packed[span, pl.ds((slot * 3 + 2) * rows, rows), :] = dv.astype(jnp.bfloat16)
    for step, out in enumerate(outs):
        out[...] = packed[jnp.bitwise_xor(me, step)]


def pack_give_kernel(half, rect_ref, give_ref):
    give_ref[...] = jnp.where(later(half), rect_ref[1], rect_ref[0]).astype(jnp.bfloat16)


def pack_early_kernel(half, zero_ref, same_ref, dv_ref, given_ref, *outs):
    late, me = later(half), place_in(half)
    rows = same_ref.shape[1] // 3
    for step, out in enumerate(outs):
        span = jnp.bitwise_xor(me, step)
        at = pl.ds(pl.multiple_of(span * rows, rows), rows)
        given = given_ref[at, :].astype(jnp.float32)
        added = (
            jnp.where(late, given, 0.0),
            jnp.where(late, 0.0, given),
            jnp.where(late, 0.0, dv_ref[at, :].astype(jnp.float32)),
        )
        for place in range(3):
            out[pl.ds(place * rows, rows), :] = (zero_ref[place, at, :] + added[place]).astype(
                jnp.bfloat16
            )
        out[pl.ds(3 * rows, 3 * rows), :] = same_ref[span]


def call(name, kernel, out_shape, scratch, cost, *args):
    with jax.named_scope(name):
        return pl.pallas_call(
            kernel,
            out_shape=out_shape,
            scratch_shapes=scratch,
            name=name,
            compiler_params=pltpu.CompilerParams(vmem_limit_bytes=VMEM_BYTES[name == "pack_soft"]),
            cost_estimate=pl.CostEstimate(flops=cost, bytes_accessed=1024, transcendentals=0),
        )(*args)


def by_halves(lin_q, lin_k, lin_v, lin_decay, norm_gain, soft_q, soft_k, soft_v, out_grad):
    rows, heads, width = lin_q.shape
    spans = lax.axis_size("ctx")
    half = spans // 2
    tokens = half * rows
    total_width = heads * lax.axis_size("head") * width
    low = lambda *s: jax.ShapeDtypeStruct(s, jnp.bfloat16)
    full = lambda *s: jax.ShapeDtypeStruct(s, jnp.float32)
    held = lambda *s: pltpu.VMEM(s, jnp.float32)
    bind = functools.partial
    tiles, wide = half // GROUP, GROUP * rows
    after = lax.optimization_barrier
    turned = held(rows * heads, width)
    scores = held(tiles, tiles, wide, wide)
    mine = (low(rows, heads, width),) * 3

    def moved(x, step):
        return lax.ppermute(x, "ctx", [(i, i ^ step) for i in range(spans)])

    def exchanged(parts):
        return [moved(part, step) if step else part for step, part in enumerate(parts)]

    soft_sent = call(
        "pack_soft", bind(pack_soft_kernel, half), (low(8 * rows, width),) * half, [turned] * 4,
        11960000000, soft_q, soft_k, soft_v, out_grad,
    )
    soft_got = exchanged(soft_sent)
    lin_sent = call(
        "pack_lin", bind(pack_lin_kernel, half), (low(6 * rows + 2 * PAD, width),) * half,
        [turned] * 3 + [held(6 * heads, width)], 5980000000,
        lin_q, lin_k, lin_v, lin_decay, norm_gain,
    )
    lin_got = exchanged(lin_sent)
    x, give = call(
        "soft_gather", bind(soft_gather_kernel, half),
        (low(half, 8 * rows, width), low(half, rows, width)), [], COST, *soft_got,
    )
    recv = moved(give, half)
    lines, give = call(
        "soft_stats", bind(soft_stats_kernel, half), (full(8, tokens), low(half, rows, width)),
        [scores], 5520000000, x,
    )
    recv_two = moved(give, half)
    far_lines = moved(lines, half)
    dv_give, first_lines = call(
        "soft_first", bind(soft_first_kernel, half), (low(tokens, width), full(8, tokens)),
        [scores], 13800000000, x, recv, lines,
    )
    dv_given = moved(dv_give, half)
    lin_x, lin_lines, local_out, states, state = call(
        "lin_local", bind(lin_local_kernel, half, rows),
        (
            low(half, 6 * rows + 2 * PAD, width),
            full(2 * half, rows),
            full(2, half, rows, width),
            low(2, half, width, width),
            low(2, width, width),
        ),
        [], 7360000000, *lin_got, first_lines,
    )
    state = moved(state, half)
    rect, rect_lines = call(
        "soft_rect", bind(soft_rect_kernel, half), (full(3, tokens, width), full(8, tokens)),
        [scores], 9200000000, x, recv, recv_two, lines, far_lines,
    )
    far_rect = moved(rect_lines, half)
    same, same_dv = call(
        "soft_same", bind(soft_same_kernel, half),
        (low(half, 3 * rows, width), full(tokens, width)), [scores], 4370000000,
        x, lines, rect_lines, rect,
    )
    zero_dv = call(
        "soft_value", bind(soft_value_kernel, half), full(tokens, width), [held(8, tokens)], COST,
        x, lines, dv_given,
    )
    cot, layer_out, sums = call(
        "lin_sums", bind(lin_sums_kernel, half, rows),
        (full(2, half, rows, width),) * 2 + (full(2 * half, rows),), [], COST,
        lin_x, lin_lines, x, zero_dv, same_dv, dv_given, local_out, state,
    )
    zero = call(
        "soft_zero", bind(soft_zero_kernel, half), full(3, tokens, width), [scores], 3680000000,
        x, lines, far_rect,
    )
    rect_then, sums = after((rect, sums))
    give = call("pack_give", bind(pack_give_kernel, half), low(tokens, width), [], 9200000000, rect_then)
    given = moved(give, half)
    steps = [("ctx", 1 << bit) for bit in range((half - 1).bit_length())]
    steps += [("head", 1 << bit) for bit in reversed(range((lax.axis_size("head") - 1).bit_length()))]
    for place, (axis, step) in enumerate(steps):
        sums = after(sums)
        if place == 3:
            given, sums = after((given, sums))
        count = lax.axis_size(axis)
        sums = sums + lax.ppermute(sums, axis, [(i, i ^ step) for i in range(count)])
    early = call(
        "pack_early", bind(pack_early_kernel, half), (low(6 * rows, width),) * half, [], 9200000000,
        zero, same, dv_given, given,
    )
    early = exchanged(early)
    low_cot, late_state = call(
        "lin_cot", bind(lin_cot_kernel, half, rows, total_width),
        (low(2, half, rows, width), low(2, width, width)), [], COST,
        lin_x, lin_lines, cot, layer_out, sums,
    )
    late_state = moved(late_state, half)
    lin_dq, lin_made = call(
        "lin_own", bind(lin_own_kernel, half, rows),
        (low(2, half, rows, width), full(2, 2, half, rows, width)), [], COST,
        lin_x, lin_lines, low_cot, states, state,
    )
    lin_made = call(
        "lin_finish", bind(lin_finish_kernel, half, rows), (low(6 * rows, width),) * half,
        [pltpu.VMEM((half, 6 * rows, width), jnp.bfloat16)], COST,
        lin_x, lin_lines, lin_dq, lin_made, late_state,
    )
    lin_back = exchanged(lin_made)
    soft_out = list(call("unpack_soft", bind(unpack_kernel, half), mine, [turned], 5060000000, *early))
    lin_back[0], soft_out[0] = after((lin_back[0], soft_out[0]))
    lin_out = call("unpack_lin", bind(unpack_kernel, half), mine, [turned], COST, *lin_back)
    return (*lin_out, *soft_out)


def layers(
    lin_q,
    lin_k,
    lin_v,
    lin_decay,
    norm_gain,
    soft_q,
    soft_k,
    soft_v,
    out_grad,
    block_lists,
    block_counts,
):
    spans = lax.axis_size("ctx")
    if (
        lin_q.shape[0] == BLK
        and spans - 1 <= NSEL
        and lin_q.shape[1] == spans
        and spans >= 4
        and spans & (spans - 1) == 0
    ):
        return by_halves(
            lin_q, lin_k, lin_v, lin_decay, norm_gain, soft_q, soft_k, soft_v, out_grad
        )
    return local(
        lin_q,
        lin_k,
        lin_v,
        lin_decay,
        norm_gain,
        soft_q,
        soft_k,
        soft_v,
        out_grad,
        block_lists,
        block_counts,
    )


def solution(mesh):
    in_specs = (
        P("ctx", "head", None),
        P("ctx", "head", None),
        P("ctx", "head", None),
        P("head", "ctx"),
        P("head", None),
        P("ctx", "head", None),
        P("ctx", "head", None),
        P("ctx", "head", None),
        P("ctx", "head", None),
        P("ctx", None),
        P("ctx"),
    )
    out_specs = (
        P("ctx", "head", None),
        P("ctx", "head", None),
        P("ctx", "head", None),
        P("ctx", "head", None),
        P("ctx", "head", None),
        P("ctx", "head", None),
    )
    return jax.shard_map(layers, mesh=mesh, in_specs=in_specs, out_specs=out_specs, check_vma=False)
```

```python
import functools

import jax
import jax.numpy as jnp
from jax import lax
from jax.experimental import pallas as pl
from jax.experimental.pallas import tpu as pltpu
from jax.sharding import PartitionSpec as P

BLK = 128
NSEL = 16
PAD = 16
GROUP = 2
COST = 1024
VMEM_BYTES = (24 * 1024 * 1024, 56 * 1024 * 1024)


epsilon = 1e-05
exact_precision = lax.Precision.HIGHEST


def carried_in(part, axis, combine, identity, reverse):
    count = lax.axis_size(axis)
    place = lax.axis_index(axis)
    ahead = count - 1 - place if reverse else place
    gathered = jax.tree.map(lambda a: lax.all_gather(a, axis), part)
    state = jax.tree.map(lambda a, e: jnp.zeros_like(a) + jnp.asarray(e, a.dtype), part, identity)

    def one(lap, state):
        source = count - 1 - lap if reverse else lap
        return combine(
            state, jax.tree.map(lambda a: lax.dynamic_index_in_dim(a, source, 0, False), gathered)
        )

    return lax.fori_loop(0, ahead, one, state)


def decay_tables(decays):
    running = jnp.cumsum(decays, axis=1)
    finish = running[:, -1]
    length = decays.shape[1]
    below_diag = (jnp.arange(length)[:, None] >= jnp.arange(length)[None, :])[None]
    spread = running[:, :, None] - running[:, None, :]
    within = jnp.where(below_diag, jnp.exp(jnp.where(below_diag, spread, 0.0)), 0.0)
    return (jnp.exp(finish), jnp.exp(finish[:, None] - running), jnp.exp(running), within)


def chain_join(earlier, later):
    return (earlier[0] * later[0], later[0][:, None, None] * earlier[1] + later[1])


def sparse_grads(queries, grads_out, key_rows, value_rows, allowed):
    score_scale = queries.shape[-1] ** (-0.5)
    scores = (
        jnp.einsum("bqhd,bkhd->bhqk", queries, key_rows, preferred_element_type=jnp.float32)
        * score_scale
    )
    key_mask = allowed[:, None]
    scores = jnp.where(key_mask, scores, -1e30)
    row_max = jnp.max(scores, axis=-1, keepdims=True)
    weights = jnp.where(key_mask, jnp.exp(scores - row_max), 0.0)
    softmax_probs = weights / jnp.sum(weights, axis=-1, keepdims=True)
    rounded = softmax_probs.astype(jnp.bfloat16)
    outputs = jnp.einsum("bhqk,bkhd->bqhd", rounded, value_rows, preferred_element_type=jnp.float32)
    row_delta = jnp.sum(grads_out.astype(jnp.float32) * outputs, axis=-1)
    grad_probs = jnp.einsum(
        "bqhd,bkhd->bhqk", grads_out, value_rows, preferred_element_type=jnp.float32
    )
    grad_scores = (
        softmax_probs * (grad_probs - jnp.transpose(row_delta, (0, 2, 1))[..., None])
    ).astype(jnp.bfloat16)
    query_gradient = (
        jnp.einsum("bhqk,bkhd->bqhd", grad_scores, key_rows, preferred_element_type=jnp.float32)
        * score_scale
    )
    key_gradient = (
        jnp.einsum("bhqk,bqhd->bkhd", grad_scores, queries, preferred_element_type=jnp.float32)
        * score_scale
    )
    value_gradient = jnp.einsum(
        "bhqk,bqhd->bkhd", rounded, grads_out, preferred_element_type=jnp.float32
    )
    return (query_gradient, key_gradient, value_gradient)


def local(
    lin_q,
    lin_k,
    lin_v,
    lin_decay,
    norm_gain,
    soft_q,
    soft_k,
    soft_v,
    out_grad,
    block_lists,
    block_counts,
):
    tok_rows, heads_here, head_width = lin_q.shape
    blocks_here = tok_rows // BLK
    span_count = lax.axis_size("ctx")
    own_span = lax.axis_index("ctx")
    total_width = heads_here * lax.axis_size("head") * head_width
    complete_query = lin_q.astype(jnp.float32)
    complete_key = lin_k.astype(jnp.float32)
    complete_value = lin_v.astype(jnp.float32)
    carry_decay, trailing_decay, leading_decay, within = decay_tables(lin_decay)
    state_here = jnp.einsum(
        "boz,bor->ozr",
        complete_key * trailing_decay.T[:, :, None],
        complete_value,
        precision=exact_precision,
    )
    identity = (jnp.ones_like(carry_decay), jnp.zeros_like(state_here))
    incoming_state = carried_in((carry_decay, state_here), "ctx", chain_join, identity, False)[1]
    pair_weights = (
        jnp.einsum("thk,shk->hts", lin_q, lin_k, preferred_element_type=jnp.float32) * within
    )
    layer_out = jnp.einsum("hts,shv->thv", pair_weights, complete_value, precision=exact_precision)
    layer_out = layer_out + leading_decay.T[:, :, None] * jnp.einsum(
        "wfg,fgl->wfl", complete_query, incoming_state, precision=exact_precision
    )
    squares = lax.psum(jnp.sum(layer_out * layer_out, axis=(1, 2)), "head")
    root_mean = jnp.sqrt(squares / total_width + epsilon)
    norm_scale = norm_gain[None]
    all_lists, all_counts = (
        lax.all_gather(block_lists, "ctx", axis=0, tiled=True),
        lax.all_gather(block_counts, "ctx", axis=0, tiled=True),
    )
    entries = blocks_here * NSEL
    every_live = (
        jnp.arange(NSEL)[None, None, :] < all_counts.reshape(span_count, blocks_here)[:, :, None]
    ).reshape(span_count, entries)
    owner_hits = every_live & (all_lists // blocks_here == own_span)
    wanted_here = jnp.max(jnp.where(owner_hits, all_lists % blocks_here, -1), axis=1)
    my_live = jnp.arange(NSEL)[None, :] < block_counts[:, None]
    flat_owner = (block_lists // blocks_here).reshape(entries)
    flat_live = my_live.reshape(entries)
    key_blocks = soft_k.reshape(blocks_here, BLK, heads_here, head_width)
    value_blocks = soft_v.reshape(blocks_here, BLK, heads_here, head_width)
    picked = jnp.clip(wanted_here, 0, blocks_here - 1)
    present = (wanted_here >= 0)[:, None, None, None]
    nothing = jnp.zeros((), jnp.bfloat16)
    send_keys = jnp.where(present, key_blocks[picked], nothing)
    send_values = jnp.where(present, value_blocks[picked], nothing)
    got_keys, got_values = (
        lax.all_to_all(send_keys, "ctx", split_axis=0, concat_axis=0, tiled=True),
        lax.all_to_all(send_values, "ctx", split_axis=0, concat_axis=0, tiled=True),
    )
    listed_keys = jnp.take(got_keys, flat_owner, axis=0).reshape(
        blocks_here, NSEL * BLK, heads_here, head_width
    )
    listed_values = jnp.take(got_values, flat_owner, axis=0).reshape(
        blocks_here, NSEL * BLK, heads_here, head_width
    )
    key_rows = jnp.concatenate([key_blocks, listed_keys], axis=1)
    value_rows = jnp.concatenate([value_blocks, listed_values], axis=1)
    causal = jnp.arange(BLK)[:, None] >= jnp.arange(BLK)[None, :]
    remote_mask = jnp.broadcast_to(
        jnp.repeat(my_live, BLK, axis=1)[:, None, :], (blocks_here, BLK, NSEL * BLK)
    )
    allowed = jnp.concatenate(
        [jnp.broadcast_to(causal, (blocks_here, BLK, BLK)), remote_mask], axis=2
    )
    query_blocks = soft_q.reshape(blocks_here, BLK, heads_here, head_width)
    grad_blocks = out_grad.reshape(blocks_here, BLK, heads_here, head_width)
    query_gradient, key_gradient, value_gradient = sparse_grads(
        query_blocks, grad_blocks, key_rows, value_rows, allowed
    )
    soft_dq = query_gradient.reshape(tok_rows, heads_here, head_width).astype(jnp.bfloat16)
    routing = (
        flat_live[None, :] & (flat_owner[None, :] == jnp.arange(span_count)[:, None])
    ).astype(jnp.float32)
    remote_key = key_gradient[:, BLK:].reshape(entries, BLK, heads_here, head_width)
    remote_value = value_gradient[:, BLK:].reshape(entries, BLK, heads_here, head_width)
    part_key = jnp.einsum("oe,exhd->oxhd", routing, remote_key, precision=exact_precision).astype(
        jnp.bfloat16
    )
    part_value = jnp.einsum(
        "oe,exhd->oxhd", routing, remote_value, precision=exact_precision
    ).astype(jnp.bfloat16)
    back_key, back_value = (
        lax.all_to_all(part_key, "ctx", split_axis=0, concat_axis=0, tiled=True),
        lax.all_to_all(part_value, "ctx", split_axis=0, concat_axis=0, tiled=True),
    )
    placing = (wanted_here[:, None] == jnp.arange(blocks_here)[None, :]).astype(jnp.float32)
    added_key = jnp.einsum(
        "rb,rxhd->bxhd", placing, back_key.astype(jnp.float32), precision=exact_precision
    ).reshape(tok_rows, heads_here, head_width)
    added_value = jnp.einsum(
        "rb,rxhd->bxhd", placing, back_value.astype(jnp.float32), precision=exact_precision
    ).reshape(tok_rows, heads_here, head_width)
    soft_dk = (key_gradient[:, :BLK].reshape(tok_rows, heads_here, head_width) + added_key).astype(
        jnp.bfloat16
    )
    value_total = value_gradient[:, :BLK].reshape(tok_rows, heads_here, head_width) + added_value
    soft_dv = value_total.astype(jnp.bfloat16)
    cotangent = out_grad.astype(jnp.float32) + value_total
    inner_total = lax.psum(jnp.sum(norm_scale * cotangent * layer_out, axis=(1, 2)), "head")
    linear_cotangent = (
        norm_scale * cotangent / root_mean[:, None, None]
        - layer_out * (inner_total / (total_width * root_mean**3))[:, None, None]
    )
    reverse_state = carried_in(
        (
            carry_decay,
            jnp.einsum(
                "boz,bor->ozr",
                complete_query * leading_decay.T[:, :, None],
                linear_cotangent,
                precision=exact_precision,
            ),
        ),
        "ctx",
        chain_join,
        identity,
        True,
    )[1]
    grad_pair = (
        jnp.einsum("thv,shv->hts", linear_cotangent, complete_value, precision=exact_precision)
        * within
    )
    lin_dq = jnp.einsum("hts,shk->thk", grad_pair, complete_key, precision=exact_precision)
    lin_dq = lin_dq + leading_decay.T[:, :, None] * jnp.einsum(
        "fqs,qrs->fqr", linear_cotangent, incoming_state, precision=exact_precision
    )
    lin_dk = jnp.einsum("hts,thk->shk", grad_pair, complete_query, precision=exact_precision)
    lin_dk = lin_dk + trailing_decay.T[:, :, None] * jnp.einsum(
        "fut,ujt->fuj", complete_value, reverse_state, precision=exact_precision
    )
    lin_dv = jnp.einsum("hts,thv->shv", pair_weights, linear_cotangent, precision=exact_precision)
    lin_dv = lin_dv + trailing_decay.T[:, :, None] * jnp.einsum(
        "zpu,pux->zpx", complete_key, reverse_state, precision=exact_precision
    )
    return (
        lin_dq.astype(jnp.bfloat16),
        lin_dk.astype(jnp.bfloat16),
        lin_dv.astype(jnp.bfloat16),
        soft_dq,
        soft_dk,
        soft_dv,
    )


def triple(x):
    top = x.astype(jnp.bfloat16)
    rest = x - top.astype(jnp.float32)
    middle = rest.astype(jnp.bfloat16)
    low = (rest - middle.astype(jnp.float32)).astype(jnp.bfloat16)
    return top, middle, low


def nt(a, b):
    return lax.dot_general(a, b, (((1,), (1,)), ((), ())), preferred_element_type=jnp.float32)


def nn(a, b):
    return lax.dot_general(a, b, (((1,), (0,)), ((), ())), preferred_element_type=jnp.float32)


def tn(a, b):
    return lax.dot_general(a, b, (((0,), (0,)), ((), ())), preferred_element_type=jnp.float32)


def later(half):
    return lax.axis_index("ctx") >= half


def place_in(half):
    return lax.rem(lax.axis_index("ctx"), half)


def spread(source, scratch):
    rows, heads, width = source.shape
    scratch[...] = source[...].astype(jnp.float32).reshape(rows * heads, width)


def head_of(scratch, head, heads):
    return scratch[pl.ds(head, scratch.shape[0] // heads, stride=heads), :]


def put_heads(half, outs, scratch, first, second, rows, heads):
    late, me = later(half), place_in(half)
    for step, out in enumerate(outs):
        head = 2 * jnp.bitwise_xor(me, step)
        even, odd = head_of(scratch, head, heads), head_of(scratch, head + 1, heads)
        out[pl.ds(first * rows, rows), :] = jnp.where(late, odd, even).astype(jnp.bfloat16)
        out[pl.ds(second * rows, rows), :] = jnp.where(late, even, odd).astype(jnp.bfloat16)


def pack_soft_kernel(half, *refs):
    sources, outs, scratches = refs[:4], refs[4 : 4 + half], refs[4 + half :]
    rows, heads, _ = sources[0].shape
    for place, (source, scratch) in enumerate(zip(sources, scratches)):
        spread(source, scratch)
        put_heads(half, outs, scratch, place, 4 + place, rows, heads)


def pack_lin_kernel(half, *refs):
    sources, decay_ref, gain_ref, outs = refs[:3], refs[3], refs[4], refs[5 : 5 + half]
    scratches, parts_scr = refs[5 + half : 8 + half], refs[8 + half]
    late, me = later(half), place_in(half)
    rows, heads, width = sources[0].shape
    for place, (source, scratch) in enumerate(zip(sources, scratches)):
        spread(source, scratch)
        put_heads(half, outs, scratch, place, 3 + place, rows, heads)
    parts = [*triple(decay_ref[...]), *triple(gain_ref[...])]
    for place, part in enumerate(parts):
        parts_scr[pl.ds(place * heads, heads), :] = part.astype(jnp.float32)
    line = lax.broadcasted_iota(jnp.int32, (PAD, width), 0)
    for step, out in enumerate(outs):
        blocks = []
        for head in range(2):
            at = 2 * jnp.bitwise_xor(me, step) + head
            block = jnp.zeros((PAD, width), jnp.float32)
            for place in range(len(parts)):
                block = jnp.where(line == place, parts_scr[pl.ds(place * heads + at, 1), :], block)
            blocks.append(block)
        even, odd = blocks
        out[pl.ds(6 * rows, PAD), :] = jnp.where(late, odd, even).astype(jnp.bfloat16)
        out[pl.ds(6 * rows + PAD, PAD), :] = jnp.where(late, even, odd).astype(jnp.bfloat16)


def unpack_kernel(half, *refs):
    steps, outs, scratch = refs[:half], refs[half:-1], refs[-1]
    late, me = later(half), place_in(half)
    rows, heads, width = outs[0].shape
    for place, out in enumerate(outs):
        for step, ref in enumerate(steps):
            head = 2 * jnp.bitwise_xor(me, step)
            first = ref[pl.ds(place * rows, rows), :].astype(jnp.float32)
            second = ref[pl.ds((3 + place) * rows, rows), :].astype(jnp.float32)
            scratch[pl.ds(head, rows, stride=heads), :] = jnp.where(late, second, first)
            scratch[pl.ds(head + 1, rows, stride=heads), :] = jnp.where(late, first, second)
        out[...] = scratch[...].reshape(rows, heads, width).astype(jnp.bfloat16)


def soft_gather_kernel(half, *refs):
    steps, x_ref, give_ref = refs[:half], refs[half], refs[half + 1]
    late, me = later(half), place_in(half)
    rows = x_ref.shape[1] // 8
    for step, ref in enumerate(steps):
        source = jnp.bitwise_xor(me, step)
        x_ref[source] = ref[...]
        give_ref[source] = jnp.where(
            late, ref[pl.ds(0, rows), :], ref[pl.ds(rows, rows), :]
        )


def soft_blocks(half, x_ref, recv_ref):
    late = later(half)
    rows = x_ref.shape[1] // 8
    width = x_ref.shape[2]

    def own(slot, place):
        def take(tile):
            return x_ref[
                pl.ds(tile * GROUP, GROUP), pl.ds((slot * 4 + place) * rows, rows), :
            ].reshape(GROUP * rows, width)

        return take

    def other(place):
        def take(tile):
            return recv_ref[place][pl.ds(tile * GROUP, GROUP)].reshape(GROUP * rows, width)

        return take

    def either(if_late, if_early):
        return lambda tile: jnp.where(late, if_late(tile), if_early(tile))

    zero = (own(0, 0), own(0, 1), own(0, 2), own(0, 3), True)
    same = (own(1, 0), own(1, 1), own(1, 2), own(1, 3), True)
    rect = (
        either(own(1, 0), other(0)),
        either(other(0), own(1, 1)),
        either(other(1), own(1, 2)),
        either(own(1, 3), other(1)),
        False,
    )
    return zero, same, rect


def tile_scores(block, i, j, wide):
    q, k, _, _, causal = block
    scores = nt(k(i), q(j))
    if not causal or i < j:
        return scores
    key_at = lax.broadcasted_iota(jnp.int32, (wide, wide), 0)
    query_at = lax.broadcasted_iota(jnp.int32, (wide, wide), 1)
    return jnp.where(key_at <= query_at, scores, -1e30)


def tiles_of(block, j, tiles):
    return range(j + 1) if block[4] else range(tiles)


def block_stats(block, scr, tiles, wide, scale):
    tops, totals, dots = [], [], []
    _, _, v, g, _ = block
    for j in range(tiles):
        top = None
        for i in tiles_of(block, j, tiles):
            scores = tile_scores(block, i, j, wide)
            scr[i, j] = scores
            here = jnp.max(scores, axis=0, keepdims=True)
            top = here if top is None else jnp.maximum(top, here)
        total = jnp.zeros_like(top)
        out_t = None
        for i in tiles_of(block, j, tiles):
            weights = jnp.exp((scr[i, j] - top) * scale)
            scr[i, j] = weights
            total = total + jnp.sum(weights, axis=0, keepdims=True)
            part = tn(v(i), weights.astype(jnp.bfloat16))
            out_t = part if out_t is None else out_t + part
        grads_t = jnp.transpose(g(j).astype(jnp.float32))
        tops.append(top)
        totals.append(total)
        dots.append(jnp.sum(grads_t * out_t, axis=0, keepdims=True))
    return tops, totals, dots


def joined(mine, other, use, scale):
    top, total, dot = mine
    top_other, total_other, dot_other = other
    top_other = jnp.where(use, top_other, top)
    both = jnp.maximum(top, top_other)
    here = jnp.exp((top - both) * scale)
    there = jnp.where(use, jnp.exp((top_other - both) * scale), 0.0)
    inverse = 1.0 / (total * here + total_other * there)
    return here * inverse, (dot * here + dot_other * there) * inverse


def block_grads(block, factors, deltas, scr, tiles, scale):
    q, k, v, g, _ = block
    dq, dk, dv = [], [None] * tiles, [None] * tiles
    add = lambda total, part: part if total is None else total + part
    for j in range(tiles):
        dq_t = None
        for i in tiles_of(block, j, tiles):
            probs = scr[i, j] * factors[j]
            dv[i] = add(dv[i], nn(probs.astype(jnp.bfloat16), g(j)))
            grad_probs = nt(v(i), g(j))
            grad_scores = (probs * (grad_probs - deltas[j])).astype(jnp.bfloat16)
            dq_t = add(dq_t, tn(k(i), grad_scores))
            dk[i] = add(dk[i], nn(grad_scores, q(j)))
        dq.append(jnp.transpose(dq_t) * scale)
    return dq, [x * scale for x in dk], dv


def put_lines(ref, first, lines, wide):
    for place, row in enumerate(lines):
        for j, piece in enumerate(row):
            ref[pl.ds(first + place, 1), pl.ds(j * wide, wide)] = piece


def get_lines(ref, first, j, wide):
    return [ref[pl.ds(first + place, 1), pl.ds(j * wide, wide)] for place in range(3)]


def soft_shape(half, x_ref):
    rows, width = x_ref.shape[1] // 8, x_ref.shape[2]
    return half // GROUP, GROUP * rows, width**-0.5


def soft_stats_kernel(half, x_ref, lines_ref, give_ref, scr):
    late, rows = later(half), x_ref.shape[1] // 8
    for span in range(half):
        give_ref[span] = jnp.where(
            late, x_ref[span, pl.ds(3 * rows, rows), :], x_ref[span, pl.ds(2 * rows, rows), :]
        )
    tiles, wide, scale = soft_shape(half, x_ref)
    zero, same, _ = soft_blocks(half, x_ref, None)
    lines_ref[...] = jnp.zeros_like(lines_ref)
    put_lines(lines_ref, 0, block_stats(zero, scr, tiles, wide, scale), wide)
    put_lines(lines_ref, 3, block_stats(same, scr, tiles, wide, scale), wide)


def rect_joined(late, lines_ref, far_ref, lines, j, wide, scale):
    near, far = get_lines(lines_ref, 3, j, wide), get_lines(far_ref, 0, j, wide)
    other = [jnp.where(late, a, b) for a, b in zip(near, far)]
    return joined([line[j] for line in lines], other, True, scale)


def soft_first_kernel(half, x_ref, recv_ref, lines_ref, far_ref, send_ref, rect_ref, scr):
    late = later(half)
    tiles, wide, scale = soft_shape(half, x_ref)
    _, same, rect = soft_blocks(half, x_ref, (recv_ref, recv_ref))
    grads = same[3]
    tops, totals = [], []
    rect_ref[...] = jnp.zeros_like(rect_ref)
    dv = [None] * tiles
    for j in range(tiles):
        top = None
        for i in range(tiles):
            scores = tile_scores(rect, i, j, wide)
            scr[i, j] = scores
            here = jnp.max(scores, axis=0, keepdims=True)
            top = here if top is None else jnp.maximum(top, here)
        total = jnp.zeros_like(top)
        for i in range(tiles):
            weights = jnp.exp((scr[i, j] - top) * scale)
            scr[i, j] = weights
            total = total + jnp.sum(weights, axis=0, keepdims=True)
        tops.append(top)
        totals.append(total)
        zeros = [jnp.zeros_like(top)] * tiles
        factor, _ = rect_joined(
            late, lines_ref, far_ref, ([top] * tiles, [total] * tiles, zeros), j, wide, scale
        )
        for i in range(tiles):
            part = nn((scr[i, j] * factor).astype(jnp.bfloat16), grads(j))
            dv[i] = part if dv[i] is None else dv[i] + part
    put_lines(rect_ref, 0, (tops, totals), wide)
    for i in range(tiles):
        send_ref[pl.ds(i * wide, wide), :] = dv[i].astype(jnp.bfloat16)

    @pl.when(jnp.logical_not(late))
    def _():
        width = x_ref.shape[2]
        for place, part in enumerate(triple(rect_ref[...])):
            for piece in range(rect_ref.shape[1] // width):
                send_ref[pl.ds((place * tiles * GROUP + piece) * PAD, PAD), :] = jnp.concatenate(
                    [part[:, piece * width : (piece + 1) * width]] * (PAD // 8), axis=0
                )


def soft_rect_kernel(
    half, x_ref, recv_ref, recv_two_ref, lines_ref, far_ref, made_ref, rect_ref, scr
):
    late = later(half)
    tiles, wide, scale = soft_shape(half, x_ref)
    _, _, rect = soft_blocks(half, x_ref, (recv_ref, recv_two_ref))
    lines = block_stats(rect, scr, tiles, wide, scale)
    rect_ref[...] = jnp.zeros_like(rect_ref)
    put_lines(rect_ref, 0, lines, wide)
    both = [rect_joined(late, lines_ref, far_ref, lines, j, wide, scale) for j in range(tiles)]
    factors, deltas = zip(*both)
    dq, dk, dv = block_grads(rect, factors, deltas, scr, tiles, scale)
    for j in range(tiles):
        at = pl.ds(j * wide, wide)
        for place, made in enumerate((dq[j], dk[j], dv[j])):
            made_ref[place, at, :] = made


def sent_lines(ref, pieces, lines_ref):
    width = ref.shape[1]
    for piece in range(pieces):
        parts = [
            ref[pl.ds((place * pieces + piece) * PAD, PAD), :].astype(jnp.float32)[0:8]
            for place in range(3)
        ]
        lines_ref[:, pl.ds(piece * width, width)] = parts[0] + parts[1] + parts[2]


def causal_grads(half, slot, x_ref, lines_ref, far_ref, scr):
    tiles, wide, scale = soft_shape(half, x_ref)
    block = soft_blocks(half, x_ref, None)[slot]
    factors, deltas = [], []
    for j in range(tiles):
        mine = get_lines(lines_ref, 3 * slot, j, wide)
        factor, delta = joined(mine, get_lines(far_ref, 0, j, wide), later(half), scale)
        factors.append(factor)
        deltas.append(delta)
        for i in range(j + 1):
            scr[i, j] = jnp.exp((tile_scores(block, i, j, wide) - mine[0]) * scale)
    return block_grads(block, factors, deltas, scr, tiles, scale)


def soft_zero_kernel(half, x_ref, lines_ref, far_ref, made_ref, scr):
    tiles, wide, _ = soft_shape(half, x_ref)
    grads = causal_grads(half, 0, x_ref, lines_ref, far_ref, scr)
    for j in range(tiles):
        for place in range(3):
            made_ref[place, pl.ds(j * wide, wide), :] = grads[place][j]


def soft_value_kernel(half, x_ref, lines_ref, sent_ref, dv_ref, far_ref):
    sent_lines(sent_ref, half, far_ref)
    tiles, wide, scale = soft_shape(half, x_ref)
    zero, _, _ = soft_blocks(half, x_ref, None)
    dv = [None] * tiles
    for j in range(tiles):
        mine = get_lines(lines_ref, 0, j, wide)
        factor, _ = joined(mine, get_lines(far_ref, 0, j, wide), later(half), scale)
        for i in range(j + 1):
            weights = jnp.exp((tile_scores(zero, i, j, wide) - mine[0]) * scale)
            part = nn((weights * factor).astype(jnp.bfloat16), zero[3](j))
            dv[i] = part if dv[i] is None else dv[i] + part
    for i in range(tiles):
        dv_ref[pl.ds(i * wide, wide), :] = dv[i]


def soft_same_kernel(half, x_ref, lines_ref, rect_lines_ref, rect_ref, packed, dv_ref, scr):
    late = later(half)
    tiles, wide, _ = soft_shape(half, x_ref)
    rows = wide // GROUP
    grads = causal_grads(half, 1, x_ref, lines_ref, rect_lines_ref, scr)
    for j in range(tiles):
        at = pl.ds(j * wide, wide)
        for place in range(3):
            added = rect_ref[place, at, :]
            made = grads[place][j] + (
                jnp.where(late, added, 0.0) if place == 0 else jnp.where(late, 0.0, added)
            )
            packed[pl.ds(j * GROUP, GROUP), pl.ds(place * rows, rows), :] = made.astype(
                jnp.bfloat16
            ).reshape(GROUP, rows, made.shape[1])
            if place == 2:
                dv_ref[at, :] = made


def decay_lines(half, rows, x_ref):
    firsts = [
        x_ref[span, pl.ds(6 * rows + slot * PAD, PAD), :].astype(jnp.float32)
        for slot in range(2)
        for span in range(half)
    ]
    parts = [
        jnp.concatenate([block[place : place + 1] for block in firsts], axis=0)
        for place in range(3)
    ]
    first = lax.broadcasted_iota(jnp.int32, (rows, rows), 0)
    second = lax.broadcasted_iota(jnp.int32, (rows, rows), 1)
    ones = (first <= second).astype(jnp.float32).astype(jnp.bfloat16)
    sums = nn(jnp.concatenate(parts, axis=0).astype(jnp.bfloat16), ones)
    count = 2 * half
    return sums[:count] + sums[count : 2 * count] + sums[2 * count :]


def tables(lines):
    count, rows = lines.shape
    columns = jnp.transpose(lines)
    return [
        (lines[c : c + 1], columns[:, c : c + 1], lines[c : c + 1, rows - 1 : rows])
        for c in range(count)
    ]


def triangle(rows):
    first = lax.broadcasted_iota(jnp.int32, (rows, rows), 0)
    second = lax.broadcasted_iota(jnp.int32, (rows, rows), 1)
    return first >= second, first <= second


def gain_of(extra):
    wide = extra.astype(jnp.float32)
    return wide[3:4] + wide[4:5] + wide[5:6]


def lin_parts(x_ref, slot, span, rows):
    q, k, v = (
        x_ref[span, pl.ds((slot * 3 + place) * rows, rows), :] for place in range(3)
    )
    return q, k, v, x_ref[span, pl.ds(6 * rows + slot * PAD, PAD), :]


def lin_local_kernel(half, rows, *refs):
    steps, (x_ref, lines_ref, out_ref, states_ref, give_ref) = refs[:half], refs[half:]
    me = place_in(half)
    for step, ref in enumerate(steps):
        x_ref[jnp.bitwise_xor(me, step)] = ref[...]
    width = x_ref.shape[2]
    lines = decay_lines(half, rows, x_ref)
    lines_ref[...] = lines
    chunks = tables(lines)
    lower, _ = triangle(rows)
    for slot in range(2):
        state = None
        for span in range(half):
            _, k, v, _ = lin_parts(x_ref, slot, span, rows)
            _, col, finish = chunks[slot * half + span]
            decayed = (k.astype(jnp.float32) * jnp.exp(finish - col)).astype(jnp.bfloat16)
            if span:
                states_ref[slot, span] = state.astype(jnp.bfloat16)
                state = jnp.exp(finish) * state + tn(decayed, v)
            else:
                states_ref[slot, span] = jnp.zeros((width, width), jnp.bfloat16)
                state = tn(decayed, v)
        give_ref[1 - slot] = state.astype(jnp.bfloat16)
    for slot in range(2):
        for span in range(half):
            q, k, v, _ = lin_parts(x_ref, slot, span, rows)
            row, col, _ = chunks[slot * half + span]
            within = jnp.exp(jnp.where(lower, col - row, -1e30))
            out = nn((nt(q, k) * within).astype(jnp.bfloat16), v)
            if span:
                out = out + jnp.exp(col) * nn(q, states_ref[slot, span])
            out_ref[slot, span] = out


def lin_sums_kernel(
    half, rows, x_ref, lines_ref, soft_ref, zero_ref, same_ref, dv_ref, local_ref, given_ref,
    cot_ref, out_ref, sums_ref,
):
    late = later(half)
    chunks = tables(lines_ref[...])
    before = [jnp.where(late, jnp.zeros((1, 1), jnp.float32), -1e30)] * 2
    for span in range(half):
        at = pl.ds(span * rows, rows)
        inner, squares = None, None
        for slot in range(2):
            q, _, _, extra = lin_parts(x_ref, slot, span, rows)
            _, col, finish = chunks[slot * half + span]
            out = local_ref[slot, span] + jnp.exp(before[slot] + col) * nn(q, given_ref[slot])
            before[slot] = before[slot] + finish
            out_ref[slot, span] = out
            cot = soft_ref[span, pl.ds((slot * 4 + 3) * rows, rows), :].astype(jnp.float32)
            if slot == 0:
                cot = cot + zero_ref[at, :]
                cot = cot + jnp.where(late, 0.0, dv_ref[at, :].astype(jnp.float32))
            else:
                cot = cot + same_ref[at, :]
            scaled = gain_of(extra) * cot
            cot_ref[slot, span] = scaled
            inner = scaled * out if slot == 0 else inner + scaled * out
            squares = out * out if slot == 0 else squares + out * out
        sums_ref[pl.ds(span, 1), :] = jnp.sum(jnp.transpose(squares), axis=0, keepdims=True)
        sums_ref[pl.ds(half + span, 1), :] = jnp.sum(jnp.transpose(inner), axis=0, keepdims=True)


def lin_cot_kernel(
    half, rows, total_width, x_ref, lines_ref, cot_ref, out_ref, sums_ref, low_ref, state_ref
):
    mean = sums_ref[pl.ds(0, half), :] / total_width + epsilon
    root = jnp.sqrt(mean)
    inner = sums_ref[pl.ds(half, half), :] / (total_width * root * mean)
    scalars = jnp.transpose(jnp.concatenate([1.0 / root, inner], axis=0))
    chunks = tables(lines_ref[...])
    for slot in range(2):
        before = jnp.zeros((1, 1), jnp.float32)
        state = None
        for span in range(half):
            q, _, _, _ = lin_parts(x_ref, slot, span, rows)
            _, col, finish = chunks[slot * half + span]
            cotangent = (
                cot_ref[slot, span] * scalars[:, span : span + 1]
                - out_ref[slot, span] * scalars[:, half + span : half + span + 1]
            )
            low_cot = cotangent.astype(jnp.bfloat16)
            low_ref[slot, span] = low_cot
            decayed = (q.astype(jnp.float32) * jnp.exp(before + col)).astype(jnp.bfloat16)
            before = before + finish
            part = tn(decayed, low_cot)
            state = part if state is None else state + part
        state_ref[1 - slot] = state.astype(jnp.bfloat16)


def lin_own_kernel(half, rows, x_ref, lines_ref, low_ref, states_ref, given_ref, dq_ref, made_ref):
    chunks = tables(lines_ref[...])
    lower, upper = triangle(rows)
    late = later(half)
    for slot in range(2):
        given = jnp.where(late, given_ref[slot].astype(jnp.float32), 0.0)
        before = [jnp.zeros((1, 1), jnp.float32)]
        for span in range(half):
            before.append(before[-1] + chunks[slot * half + span][2])
        state = None
        for span in reversed(range(half)):
            q, k, v, _ = lin_parts(x_ref, slot, span, rows)
            row, col, finish = chunks[slot * half + span]
            within = jnp.exp(jnp.where(lower, col - row, -1e30))
            within_t = jnp.exp(jnp.where(upper, row - col, -1e30))
            low_cot = low_ref[slot, span]
            grad_pair = (nt(low_cot, v) * within).astype(jnp.bfloat16)
            grad_pair_t = (nt(v, low_cot) * within_t).astype(jnp.bfloat16)
            pair_t = (nt(k, q) * within_t).astype(jnp.bfloat16)
            leading = jnp.exp(col)
            trailing = jnp.exp(finish - col)
            carried = states_ref[slot, span].astype(jnp.float32) + jnp.exp(before[span]) * given
            dq = nn(grad_pair, k) + leading * nt(low_cot, carried.astype(jnp.bfloat16))
            dk = nn(grad_pair_t, q)
            dv = nn(pair_t, low_cot)
            decayed = (q.astype(jnp.float32) * leading).astype(jnp.bfloat16)
            part = tn(decayed, low_cot)
            if state is None:
                state = part
            else:
                low_state = state.astype(jnp.bfloat16)
                dk = dk + trailing * nt(v, low_state)
                dv = dv + trailing * nn(k, low_state)
                state = jnp.exp(finish) * state + part
            dq_ref[slot, span] = dq.astype(jnp.bfloat16)
            made_ref[slot, 0, span] = dk
            made_ref[slot, 1, span] = dv


def lin_finish_kernel(half, rows, x_ref, lines_ref, dq_ref, made_ref, state_ref, *refs):
    outs, packed = refs[:half], refs[half]
    chunks = tables(lines_ref[...])
    me = place_in(half)
    for slot in range(2):
        state = state_ref[slot]
        after = jnp.where(later(half), -1e30, jnp.zeros((1, 1), jnp.float32))
        for span in reversed(range(half)):
            _, k, v, _ = lin_parts(x_ref, slot, span, rows)
            _, col, finish = chunks[slot * half + span]
            trailing = jnp.exp(after + finish - col)
            after = after + finish
            dk = made_ref[slot, 0, span] + trailing * nt(v, state)
            dv = made_ref[slot, 1, span] + trailing * nn(k, state)
            packed[span, pl.ds(slot * 3 * rows, rows), :] = dq_ref[slot, span]
            packed[span, pl.ds((slot * 3 + 1) * rows, rows), :] = dk.astype(jnp.bfloat16)
            packed[span, pl.ds((slot * 3 + 2) * rows, rows), :] = dv.astype(jnp.bfloat16)
    for step, out in enumerate(outs):
        out[...] = packed[jnp.bitwise_xor(me, step)]


def pack_give_kernel(half, rect_ref, give_ref):
    give_ref[...] = jnp.where(later(half), rect_ref[1], rect_ref[0]).astype(jnp.bfloat16)


def pack_early_kernel(half, zero_ref, same_ref, dv_ref, given_ref, *outs):
    late, me = later(half), place_in(half)
    rows = same_ref.shape[1] // 3
    for step, out in enumerate(outs):
        span = jnp.bitwise_xor(me, step)
        at = pl.ds(pl.multiple_of(span * rows, rows), rows)
        given = given_ref[at, :].astype(jnp.float32)
        added = (
            jnp.where(late, given, 0.0),
            jnp.where(late, 0.0, given),
            jnp.where(late, 0.0, dv_ref[at, :].astype(jnp.float32)),
        )
        for place in range(3):
            out[pl.ds(place * rows, rows), :] = (zero_ref[place, at, :] + added[place]).astype(
                jnp.bfloat16
            )
        out[pl.ds(3 * rows, 3 * rows), :] = same_ref[span]


def call(name, kernel, out_shape, scratch, cost, *args, waits=()):
    count = len(args)
    places = {}
    if waits:
        places["in_specs"] = [pl.BlockSpec(memory_space=pltpu.VMEM)] * count + [
            pl.BlockSpec(memory_space=pl.ANY)
        ] * len(waits)

    def body(*refs):
        kernel(*refs[:count], *refs[count + len(waits) :])

    with jax.named_scope(name):
        return pl.pallas_call(
            body,
            out_shape=out_shape,
            scratch_shapes=scratch,
            name=name,
            compiler_params=pltpu.CompilerParams(vmem_limit_bytes=VMEM_BYTES[name == "pack_soft"]),
            cost_estimate=pl.CostEstimate(flops=cost, bytes_accessed=1024, transcendentals=0),
            **places,
        )(*args, *waits)


def by_halves(lin_q, lin_k, lin_v, lin_decay, norm_gain, soft_q, soft_k, soft_v, out_grad):
    rows, heads, width = lin_q.shape
    spans = lax.axis_size("ctx")
    half = spans // 2
    tokens = half * rows
    total_width = heads * lax.axis_size("head") * width
    low = lambda *s: jax.ShapeDtypeStruct(s, jnp.bfloat16)
    full = lambda *s: jax.ShapeDtypeStruct(s, jnp.float32)
    held = lambda *s: pltpu.VMEM(s, jnp.float32)
    bind = functools.partial
    tiles, wide = half // GROUP, GROUP * rows
    after = lax.optimization_barrier
    turned = held(rows * heads, width)
    scores = held(tiles, tiles, wide, wide)
    mine = (low(rows, heads, width),) * 3

    def moved(x, step):
        return lax.ppermute(x, "ctx", [(i, i ^ step) for i in range(spans)])

    def exchanged(parts):
        return [moved(part, step) if step else part for step, part in enumerate(parts)]

    soft_sent = call(
        "pack_soft", bind(pack_soft_kernel, half), (low(8 * rows, width),) * half, [turned] * 4,
        11960000000, soft_q, soft_k, soft_v, out_grad,
    )
    soft_got = exchanged(soft_sent)
    lin_sent = call(
        "pack_lin", bind(pack_lin_kernel, half), (low(6 * rows + 2 * PAD, width),) * half,
        [turned] * 3 + [held(6 * heads, width)], 5980000000,
        lin_q, lin_k, lin_v, lin_decay, norm_gain,
    )
    lin_got = exchanged(lin_sent)
    x, give = call(
        "soft_gather", bind(soft_gather_kernel, half),
        (low(half, 8 * rows, width), low(half, rows, width)), [], COST, *soft_got,
    )
    recv = moved(give, half)
    lines, give = call(
        "soft_stats", bind(soft_stats_kernel, half), (full(8, tokens), low(half, rows, width)),
        [scores], 5520000000, x,
    )
    recv_two = moved(give, half)
    far_lines = moved(lines, half)
    dv_give, first_lines = call(
        "soft_first", bind(soft_first_kernel, half), (low(tokens, width), full(8, tokens)),
        [scores], 13800000000, x, recv, lines, far_lines, waits=lin_got[1:3],
    )
    dv_given = moved(dv_give, half)
    lin_x, lin_lines, local_out, states, state = call(
        "lin_local", bind(lin_local_kernel, half, rows),
        (
            low(half, 6 * rows + 2 * PAD, width),
            full(2 * half, rows),
            full(2, half, rows, width),
            low(2, half, width, width),
            low(2, width, width),
        ),
        [], 7360000000, *lin_got, waits=(first_lines,),
    )
    state = moved(state, half)
    rect, rect_lines = call(
        "soft_rect", bind(soft_rect_kernel, half), (full(3, tokens, width), full(8, tokens)),
        [scores], 9200000000, x, recv, recv_two, lines, far_lines,
    )
    far_rect = moved(rect_lines, half)
    same, same_dv = call(
        "soft_same", bind(soft_same_kernel, half),
        (low(half, 3 * rows, width), full(tokens, width)), [scores], 4370000000,
        x, lines, rect_lines, rect,
    )
    zero_dv = call(
        "soft_value", bind(soft_value_kernel, half), full(tokens, width), [held(8, tokens)], COST,
        x, lines, dv_given,
    )
    cot, layer_out, sums = call(
        "lin_sums", bind(lin_sums_kernel, half, rows),
        (full(2, half, rows, width),) * 2 + (full(2 * half, rows),), [], COST,
        lin_x, lin_lines, x, zero_dv, same_dv, dv_given, local_out, state,
    )
    zero = call(
        "soft_zero", bind(soft_zero_kernel, half), full(3, tokens, width), [scores], 3680000000,
        x, lines, far_rect,
    )
    rect_then, sums = after((rect, sums))
    give = call("pack_give", bind(pack_give_kernel, half), low(tokens, width), [], 9200000000, rect_then)
    given = moved(give, half)
    steps = [("ctx", 1 << bit) for bit in range((half - 1).bit_length())]
    steps += [("head", 1 << bit) for bit in reversed(range((lax.axis_size("head") - 1).bit_length()))]
    for place, (axis, step) in enumerate(steps):
        sums = after(sums)
        if place == 3:
            given, sums = after((given, sums))
        count = lax.axis_size(axis)
        sums = sums + lax.ppermute(sums, axis, [(i, i ^ step) for i in range(count)])
    early = call(
        "pack_early", bind(pack_early_kernel, half), (low(6 * rows, width),) * half, [], 9200000000,
        zero, same, dv_given, given,
    )
    early = exchanged(early)
    low_cot, late_state = call(
        "lin_cot", bind(lin_cot_kernel, half, rows, total_width),
        (low(2, half, rows, width), low(2, width, width)), [], COST,
        lin_x, lin_lines, cot, layer_out, sums,
    )
    late_state = moved(late_state, half)
    lin_dq, lin_made = call(
        "lin_own", bind(lin_own_kernel, half, rows),
        (low(2, half, rows, width), full(2, 2, half, rows, width)), [], COST,
        lin_x, lin_lines, low_cot, states, state,
    )
    lin_made = call(
        "lin_finish", bind(lin_finish_kernel, half, rows), (low(6 * rows, width),) * half,
        [pltpu.VMEM((half, 6 * rows, width), jnp.bfloat16)], COST,
        lin_x, lin_lines, lin_dq, lin_made, late_state,
    )
    lin_back = exchanged(lin_made)
    soft_out = list(call("unpack_soft", bind(unpack_kernel, half), mine, [turned], 5060000000, *early))
    lin_back[0], soft_out[0] = after((lin_back[0], soft_out[0]))
    lin_out = call("unpack_lin", bind(unpack_kernel, half), mine, [turned], COST, *lin_back)
    return (*lin_out, *soft_out)


def layers(
    lin_q,
    lin_k,
    lin_v,
    lin_decay,
    norm_gain,
    soft_q,
    soft_k,
    soft_v,
    out_grad,
    block_lists,
    block_counts,
):
    spans = lax.axis_size("ctx")
    if (
        lin_q.shape[0] == BLK
        and spans - 1 <= NSEL
        and lin_q.shape[1] == spans
        and spans >= 4
        and spans & (spans - 1) == 0
    ):
        return by_halves(
            lin_q, lin_k, lin_v, lin_decay, norm_gain, soft_q, soft_k, soft_v, out_grad
        )
    return local(
        lin_q,
        lin_k,
        lin_v,
        lin_decay,
        norm_gain,
        soft_q,
        soft_k,
        soft_v,
        out_grad,
        block_lists,
        block_counts,
    )


def solution(mesh):
    in_specs = (
        P("ctx", "head", None),
        P("ctx", "head", None),
        P("ctx", "head", None),
        P("head", "ctx"),
        P("head", None),
        P("ctx", "head", None),
        P("ctx", "head", None),
        P("ctx", "head", None),
        P("ctx", "head", None),
        P("ctx", None),
        P("ctx"),
    )
    out_specs = (
        P("ctx", "head", None),
        P("ctx", "head", None),
        P("ctx", "head", None),
        P("ctx", "head", None),
        P("ctx", "head", None),
        P("ctx", "head", None),
    )
    return jax.shard_map(layers, mesh=mesh, in_specs=in_specs, out_specs=out_specs, check_vma=False)
```

```python
import functools

import jax
import jax.numpy as jnp
from jax import lax
from jax.experimental import pallas as pl
from jax.experimental.pallas import tpu as pltpu
from jax.sharding import PartitionSpec as P

BLK = 128
NSEL = 16
PAD = 16
GROUP = 2
COST = 1024
VMEM_BYTES = (24 * 1024 * 1024, 56 * 1024 * 1024)


epsilon = 1e-05
exact_precision = lax.Precision.HIGHEST


def carried_in(part, axis, combine, identity, reverse):
    count = lax.axis_size(axis)
    place = lax.axis_index(axis)
    ahead = count - 1 - place if reverse else place
    gathered = jax.tree.map(lambda a: lax.all_gather(a, axis), part)
    state = jax.tree.map(lambda a, e: jnp.zeros_like(a) + jnp.asarray(e, a.dtype), part, identity)

    def one(lap, state):
        source = count - 1 - lap if reverse else lap
        return combine(
            state, jax.tree.map(lambda a: lax.dynamic_index_in_dim(a, source, 0, False), gathered)
        )

    return lax.fori_loop(0, ahead, one, state)


def decay_tables(decays):
    running = jnp.cumsum(decays, axis=1)
    finish = running[:, -1]
    length = decays.shape[1]
    below_diag = (jnp.arange(length)[:, None] >= jnp.arange(length)[None, :])[None]
    spread = running[:, :, None] - running[:, None, :]
    within = jnp.where(below_diag, jnp.exp(jnp.where(below_diag, spread, 0.0)), 0.0)
    return (jnp.exp(finish), jnp.exp(finish[:, None] - running), jnp.exp(running), within)


def chain_join(earlier, later):
    return (earlier[0] * later[0], later[0][:, None, None] * earlier[1] + later[1])


def sparse_grads(queries, grads_out, key_rows, value_rows, allowed):
    score_scale = queries.shape[-1] ** (-0.5)
    scores = (
        jnp.einsum("bqhd,bkhd->bhqk", queries, key_rows, preferred_element_type=jnp.float32)
        * score_scale
    )
    key_mask = allowed[:, None]
    scores = jnp.where(key_mask, scores, -1e30)
    row_max = jnp.max(scores, axis=-1, keepdims=True)
    weights = jnp.where(key_mask, jnp.exp(scores - row_max), 0.0)
    softmax_probs = weights / jnp.sum(weights, axis=-1, keepdims=True)
    rounded = softmax_probs.astype(jnp.bfloat16)
    outputs = jnp.einsum("bhqk,bkhd->bqhd", rounded, value_rows, preferred_element_type=jnp.float32)
    row_delta = jnp.sum(grads_out.astype(jnp.float32) * outputs, axis=-1)
    grad_probs = jnp.einsum(
        "bqhd,bkhd->bhqk", grads_out, value_rows, preferred_element_type=jnp.float32
    )
    grad_scores = (
        softmax_probs * (grad_probs - jnp.transpose(row_delta, (0, 2, 1))[..., None])
    ).astype(jnp.bfloat16)
    query_gradient = (
        jnp.einsum("bhqk,bkhd->bqhd", grad_scores, key_rows, preferred_element_type=jnp.float32)
        * score_scale
    )
    key_gradient = (
        jnp.einsum("bhqk,bqhd->bkhd", grad_scores, queries, preferred_element_type=jnp.float32)
        * score_scale
    )
    value_gradient = jnp.einsum(
        "bhqk,bqhd->bkhd", rounded, grads_out, preferred_element_type=jnp.float32
    )
    return (query_gradient, key_gradient, value_gradient)


def local(
    lin_q,
    lin_k,
    lin_v,
    lin_decay,
    norm_gain,
    soft_q,
    soft_k,
    soft_v,
    out_grad,
    block_lists,
    block_counts,
):
    tok_rows, heads_here, head_width = lin_q.shape
    blocks_here = tok_rows // BLK
    span_count = lax.axis_size("ctx")
    own_span = lax.axis_index("ctx")
    total_width = heads_here * lax.axis_size("head") * head_width
    complete_query = lin_q.astype(jnp.float32)
    complete_key = lin_k.astype(jnp.float32)
    complete_value = lin_v.astype(jnp.float32)
    carry_decay, trailing_decay, leading_decay, within = decay_tables(lin_decay)
    state_here = jnp.einsum(
        "boz,bor->ozr",
        complete_key * trailing_decay.T[:, :, None],
        complete_value,
        precision=exact_precision,
    )
    identity = (jnp.ones_like(carry_decay), jnp.zeros_like(state_here))
    incoming_state = carried_in((carry_decay, state_here), "ctx", chain_join, identity, False)[1]
    pair_weights = (
        jnp.einsum("thk,shk->hts", lin_q, lin_k, preferred_element_type=jnp.float32) * within
    )
    layer_out = jnp.einsum("hts,shv->thv", pair_weights, complete_value, precision=exact_precision)
    layer_out = layer_out + leading_decay.T[:, :, None] * jnp.einsum(
        "wfg,fgl->wfl", complete_query, incoming_state, precision=exact_precision
    )
    squares = lax.psum(jnp.sum(layer_out * layer_out, axis=(1, 2)), "head")
    root_mean = jnp.sqrt(squares / total_width + epsilon)
    norm_scale = norm_gain[None]
    all_lists, all_counts = (
        lax.all_gather(block_lists, "ctx", axis=0, tiled=True),
        lax.all_gather(block_counts, "ctx", axis=0, tiled=True),
    )
    entries = blocks_here * NSEL
    every_live = (
        jnp.arange(NSEL)[None, None, :] < all_counts.reshape(span_count, blocks_here)[:, :, None]
    ).reshape(span_count, entries)
    owner_hits = every_live & (all_lists // blocks_here == own_span)
    wanted_here = jnp.max(jnp.where(owner_hits, all_lists % blocks_here, -1), axis=1)
    my_live = jnp.arange(NSEL)[None, :] < block_counts[:, None]
    flat_owner = (block_lists // blocks_here).reshape(entries)
    flat_live = my_live.reshape(entries)
    key_blocks = soft_k.reshape(blocks_here, BLK, heads_here, head_width)
    value_blocks = soft_v.reshape(blocks_here, BLK, heads_here, head_width)
    picked = jnp.clip(wanted_here, 0, blocks_here - 1)
    present = (wanted_here >= 0)[:, None, None, None]
    nothing = jnp.zeros((), jnp.bfloat16)
    send_keys = jnp.where(present, key_blocks[picked], nothing)
    send_values = jnp.where(present, value_blocks[picked], nothing)
    got_keys, got_values = (
        lax.all_to_all(send_keys, "ctx", split_axis=0, concat_axis=0, tiled=True),
        lax.all_to_all(send_values, "ctx", split_axis=0, concat_axis=0, tiled=True),
    )
    listed_keys = jnp.take(got_keys, flat_owner, axis=0).reshape(
        blocks_here, NSEL * BLK, heads_here, head_width
    )
    listed_values = jnp.take(got_values, flat_owner, axis=0).reshape(
        blocks_here, NSEL * BLK, heads_here, head_width
    )
    key_rows = jnp.concatenate([key_blocks, listed_keys], axis=1)
    value_rows = jnp.concatenate([value_blocks, listed_values], axis=1)
    causal = jnp.arange(BLK)[:, None] >= jnp.arange(BLK)[None, :]
    remote_mask = jnp.broadcast_to(
        jnp.repeat(my_live, BLK, axis=1)[:, None, :], (blocks_here, BLK, NSEL * BLK)
    )
    allowed = jnp.concatenate(
        [jnp.broadcast_to(causal, (blocks_here, BLK, BLK)), remote_mask], axis=2
    )
    query_blocks = soft_q.reshape(blocks_here, BLK, heads_here, head_width)
    grad_blocks = out_grad.reshape(blocks_here, BLK, heads_here, head_width)
    query_gradient, key_gradient, value_gradient = sparse_grads(
        query_blocks, grad_blocks, key_rows, value_rows, allowed
    )
    soft_dq = query_gradient.reshape(tok_rows, heads_here, head_width).astype(jnp.bfloat16)
    routing = (
        flat_live[None, :] & (flat_owner[None, :] == jnp.arange(span_count)[:, None])
    ).astype(jnp.float32)
    remote_key = key_gradient[:, BLK:].reshape(entries, BLK, heads_here, head_width)
    remote_value = value_gradient[:, BLK:].reshape(entries, BLK, heads_here, head_width)
    part_key = jnp.einsum("oe,exhd->oxhd", routing, remote_key, precision=exact_precision).astype(
        jnp.bfloat16
    )
    part_value = jnp.einsum(
        "oe,exhd->oxhd", routing, remote_value, precision=exact_precision
    ).astype(jnp.bfloat16)
    back_key, back_value = (
        lax.all_to_all(part_key, "ctx", split_axis=0, concat_axis=0, tiled=True),
        lax.all_to_all(part_value, "ctx", split_axis=0, concat_axis=0, tiled=True),
    )
    placing = (wanted_here[:, None] == jnp.arange(blocks_here)[None, :]).astype(jnp.float32)
    added_key = jnp.einsum(
        "rb,rxhd->bxhd", placing, back_key.astype(jnp.float32), precision=exact_precision
    ).reshape(tok_rows, heads_here, head_width)
    added_value = jnp.einsum(
        "rb,rxhd->bxhd", placing, back_value.astype(jnp.float32), precision=exact_precision
    ).reshape(tok_rows, heads_here, head_width)
    soft_dk = (key_gradient[:, :BLK].reshape(tok_rows, heads_here, head_width) + added_key).astype(
        jnp.bfloat16
    )
    value_total = value_gradient[:, :BLK].reshape(tok_rows, heads_here, head_width) + added_value
    soft_dv = value_total.astype(jnp.bfloat16)
    cotangent = out_grad.astype(jnp.float32) + value_total
    inner_total = lax.psum(jnp.sum(norm_scale * cotangent * layer_out, axis=(1, 2)), "head")
    linear_cotangent = (
        norm_scale * cotangent / root_mean[:, None, None]
        - layer_out * (inner_total / (total_width * root_mean**3))[:, None, None]
    )
    reverse_state = carried_in(
        (
            carry_decay,
            jnp.einsum(
                "boz,bor->ozr",
                complete_query * leading_decay.T[:, :, None],
                linear_cotangent,
                precision=exact_precision,
            ),
        ),
        "ctx",
        chain_join,
        identity,
        True,
    )[1]
    grad_pair = (
        jnp.einsum("thv,shv->hts", linear_cotangent, complete_value, precision=exact_precision)
        * within
    )
    lin_dq = jnp.einsum("hts,shk->thk", grad_pair, complete_key, precision=exact_precision)
    lin_dq = lin_dq + leading_decay.T[:, :, None] * jnp.einsum(
        "fqs,qrs->fqr", linear_cotangent, incoming_state, precision=exact_precision
    )
    lin_dk = jnp.einsum("hts,thk->shk", grad_pair, complete_query, precision=exact_precision)
    lin_dk = lin_dk + trailing_decay.T[:, :, None] * jnp.einsum(
        "fut,ujt->fuj", complete_value, reverse_state, precision=exact_precision
    )
    lin_dv = jnp.einsum("hts,thv->shv", pair_weights, linear_cotangent, precision=exact_precision)
    lin_dv = lin_dv + trailing_decay.T[:, :, None] * jnp.einsum(
        "zpu,pux->zpx", complete_key, reverse_state, precision=exact_precision
    )
    return (
        lin_dq.astype(jnp.bfloat16),
        lin_dk.astype(jnp.bfloat16),
        lin_dv.astype(jnp.bfloat16),
        soft_dq,
        soft_dk,
        soft_dv,
    )


def triple(x):
    top = x.astype(jnp.bfloat16)
    rest = x - top.astype(jnp.float32)
    middle = rest.astype(jnp.bfloat16)
    low = (rest - middle.astype(jnp.float32)).astype(jnp.bfloat16)
    return top, middle, low


def nt(a, b):
    return lax.dot_general(a, b, (((1,), (1,)), ((), ())), preferred_element_type=jnp.float32)


def nn(a, b):
    return lax.dot_general(a, b, (((1,), (0,)), ((), ())), preferred_element_type=jnp.float32)


def tn(a, b):
    return lax.dot_general(a, b, (((0,), (0,)), ((), ())), preferred_element_type=jnp.float32)


def later(half):
    return lax.axis_index("ctx") >= half


def place_in(half):
    return lax.rem(lax.axis_index("ctx"), half)


def spread(source, scratch):
    rows, heads, width = source.shape
    scratch[...] = source[...].astype(jnp.float32).reshape(rows * heads, width)


def head_of(scratch, head, heads):
    return scratch[pl.ds(head, scratch.shape[0] // heads, stride=heads), :]


def put_heads(half, outs, scratch, first, second, rows, heads):
    late, me = later(half), place_in(half)
    for step, out in enumerate(outs):
        head = 2 * jnp.bitwise_xor(me, step)
        even, odd = head_of(scratch, head, heads), head_of(scratch, head + 1, heads)
        out[pl.ds(first * rows, rows), :] = jnp.where(late, odd, even).astype(jnp.bfloat16)
        out[pl.ds(second * rows, rows), :] = jnp.where(late, even, odd).astype(jnp.bfloat16)


def pack_soft_kernel(half, *refs):
    sources, outs, scratches = refs[:4], refs[4 : 4 + half], refs[4 + half :]
    rows, heads, _ = sources[0].shape
    for place, (source, scratch) in enumerate(zip(sources, scratches)):
        spread(source, scratch)
        put_heads(half, outs, scratch, place, 4 + place, rows, heads)


def pack_lin_kernel(half, *refs):
    sources, decay_ref, gain_ref, outs = refs[:3], refs[3], refs[4], refs[5 : 5 + half]
    scratches, parts_scr = refs[5 + half : 8 + half], refs[8 + half]
    late, me = later(half), place_in(half)
    rows, heads, width = sources[0].shape
    for place, (source, scratch) in enumerate(zip(sources, scratches)):
        spread(source, scratch)
        put_heads(half, outs, scratch, place, 3 + place, rows, heads)
    parts = [*triple(decay_ref[...]), *triple(gain_ref[...])]
    for place, part in enumerate(parts):
        parts_scr[pl.ds(place * heads, heads), :] = part.astype(jnp.float32)
    line = lax.broadcasted_iota(jnp.int32, (PAD, width), 0)
    for step, out in enumerate(outs):
        blocks = []
        for head in range(2):
            at = 2 * jnp.bitwise_xor(me, step) + head
            block = jnp.zeros((PAD, width), jnp.float32)
            for place in range(len(parts)):
                block = jnp.where(line == place, parts_scr[pl.ds(place * heads + at, 1), :], block)
            blocks.append(block)
        even, odd = blocks
        out[pl.ds(6 * rows, PAD), :] = jnp.where(late, odd, even).astype(jnp.bfloat16)
        out[pl.ds(6 * rows + PAD, PAD), :] = jnp.where(late, even, odd).astype(jnp.bfloat16)


def unpack_kernel(half, *refs):
    steps, outs, scratch = refs[:half][::-1], refs[half:-1], refs[-1]
    late, me = later(half), place_in(half)
    rows, heads, width = outs[0].shape
    for place, out in enumerate(outs):
        for step, ref in enumerate(steps):
            head = 2 * jnp.bitwise_xor(me, step)
            first = ref[pl.ds(place * rows, rows), :].astype(jnp.float32)
            second = ref[pl.ds((3 + place) * rows, rows), :].astype(jnp.float32)
            scratch[pl.ds(head, rows, stride=heads), :] = jnp.where(late, second, first)
            scratch[pl.ds(head + 1, rows, stride=heads), :] = jnp.where(late, first, second)
        out[...] = scratch[...].reshape(rows, heads, width).astype(jnp.bfloat16)


def soft_gather_kernel(half, *refs):
    steps, x_ref, give_ref = refs[:half], refs[half], refs[half + 1]
    late, me = later(half), place_in(half)
    rows = x_ref.shape[1] // 8
    for step, ref in enumerate(steps):
        source = jnp.bitwise_xor(me, step)
        x_ref[source] = ref[...]
        give_ref[source] = jnp.where(
            late, ref[pl.ds(0, rows), :], ref[pl.ds(rows, rows), :]
        )


def soft_blocks(half, x_ref, recv_ref):
    late = later(half)
    rows = x_ref.shape[1] // 8
    width = x_ref.shape[2]

    def own(slot, place):
        def take(tile):
            return x_ref[
                pl.ds(tile * GROUP, GROUP), pl.ds((slot * 4 + place) * rows, rows), :
            ].reshape(GROUP * rows, width)

        return take

    def other(place):
        def take(tile):
            return recv_ref[place][pl.ds(tile * GROUP, GROUP)].reshape(GROUP * rows, width)

        return take

    def either(if_late, if_early):
        return lambda tile: jnp.where(late, if_late(tile), if_early(tile))

    zero = (own(0, 0), own(0, 1), own(0, 2), own(0, 3), True)
    same = (own(1, 0), own(1, 1), own(1, 2), own(1, 3), True)
    rect = (
        either(own(1, 0), other(0)),
        either(other(0), own(1, 1)),
        either(other(1), own(1, 2)),
        either(own(1, 3), other(1)),
        False,
    )
    return zero, same, rect


def tile_scores(block, i, j, wide):
    q, k, _, _, causal = block
    scores = nt(k(i), q(j))
    if not causal or i < j:
        return scores
    key_at = lax.broadcasted_iota(jnp.int32, (wide, wide), 0)
    query_at = lax.broadcasted_iota(jnp.int32, (wide, wide), 1)
    return jnp.where(key_at <= query_at, scores, -1e30)


def tiles_of(block, j, tiles):
    return range(j + 1) if block[4] else range(tiles)


def block_stats(block, scr, tiles, wide, scale):
    tops, totals, dots = [], [], []
    _, _, v, g, _ = block
    for j in range(tiles):
        top = None
        for i in tiles_of(block, j, tiles):
            scores = tile_scores(block, i, j, wide)
            scr[i, j] = scores
            here = jnp.max(scores, axis=0, keepdims=True)
            top = here if top is None else jnp.maximum(top, here)
        total = jnp.zeros_like(top)
        out_t = None
        for i in tiles_of(block, j, tiles):
            weights = jnp.exp((scr[i, j] - top) * scale)
            scr[i, j] = weights
            total = total + jnp.sum(weights, axis=0, keepdims=True)
            part = tn(v(i), weights.astype(jnp.bfloat16))
            out_t = part if out_t is None else out_t + part
        grads_t = jnp.transpose(g(j).astype(jnp.float32))
        tops.append(top)
        totals.append(total)
        dots.append(jnp.sum(grads_t * out_t, axis=0, keepdims=True))
    return tops, totals, dots


def joined(mine, other, use, scale):
    top, total, dot = mine
    top_other, total_other, dot_other = other
    top_other = jnp.where(use, top_other, top)
    both = jnp.maximum(top, top_other)
    here = jnp.exp((top - both) * scale)
    there = jnp.where(use, jnp.exp((top_other - both) * scale), 0.0)
    inverse = 1.0 / (total * here + total_other * there)
    return here * inverse, (dot * here + dot_other * there) * inverse


def block_grads(block, factors, deltas, scr, tiles, scale):
    q, k, v, g, _ = block
    dq, dk, dv = [], [None] * tiles, [None] * tiles
    add = lambda total, part: part if total is None else total + part
    for j in range(tiles):
        dq_t = None
        for i in tiles_of(block, j, tiles):
            probs = scr[i, j] * factors[j]
            dv[i] = add(dv[i], nn(probs.astype(jnp.bfloat16), g(j)))
            grad_probs = nt(v(i), g(j))
            grad_scores = (probs * (grad_probs - deltas[j])).astype(jnp.bfloat16)
            dq_t = add(dq_t, tn(k(i), grad_scores))
            dk[i] = add(dk[i], nn(grad_scores, q(j)))
        dq.append(jnp.transpose(dq_t) * scale)
    return dq, [x * scale for x in dk], dv


def put_lines(ref, first, lines, wide):
    for place, row in enumerate(lines):
        for j, piece in enumerate(row):
            ref[pl.ds(first + place, 1), pl.ds(j * wide, wide)] = piece


def get_lines(ref, first, j, wide):
    return [ref[pl.ds(first + place, 1), pl.ds(j * wide, wide)] for place in range(3)]


def soft_shape(half, x_ref):
    rows, width = x_ref.shape[1] // 8, x_ref.shape[2]
    return half // GROUP, GROUP * rows, width**-0.5


def soft_stats_kernel(half, x_ref, lines_ref, give_ref, scr):
    late, rows = later(half), x_ref.shape[1] // 8
    for span in range(half):
        give_ref[span] = jnp.where(
            late, x_ref[span, pl.ds(3 * rows, rows), :], x_ref[span, pl.ds(2 * rows, rows), :]
        )
    tiles, wide, scale = soft_shape(half, x_ref)
    zero, same, _ = soft_blocks(half, x_ref, None)
    lines_ref[...] = jnp.zeros_like(lines_ref)
    put_lines(lines_ref, 0, block_stats(zero, scr, tiles, wide, scale), wide)
    put_lines(lines_ref, 3, block_stats(same, scr, tiles, wide, scale), wide)


def rect_joined(late, lines_ref, far_ref, lines, j, wide, scale):
    near, far = get_lines(lines_ref, 3, j, wide), get_lines(far_ref, 0, j, wide)
    other = [jnp.where(late, a, b) for a, b in zip(near, far)]
    return joined([line[j] for line in lines], other, True, scale)


def soft_first_kernel(half, x_ref, recv_ref, lines_ref, far_ref, send_ref, rect_ref, scr):
    late = later(half)
    tiles, wide, scale = soft_shape(half, x_ref)
    _, same, rect = soft_blocks(half, x_ref, (recv_ref, recv_ref))
    grads = same[3]
    tops, totals = [], []
    rect_ref[...] = jnp.zeros_like(rect_ref)
    dv = [None] * tiles
    for j in range(tiles):
        top = None
        for i in range(tiles):
            scores = tile_scores(rect, i, j, wide)
            scr[i, j] = scores
            here = jnp.max(scores, axis=0, keepdims=True)
            top = here if top is None else jnp.maximum(top, here)
        total = jnp.zeros_like(top)
        for i in range(tiles):
            weights = jnp.exp((scr[i, j] - top) * scale)
            scr[i, j] = weights
            total = total + jnp.sum(weights, axis=0, keepdims=True)
        tops.append(top)
        totals.append(total)
        zeros = [jnp.zeros_like(top)] * tiles
        factor, _ = rect_joined(
            late, lines_ref, far_ref, ([top] * tiles, [total] * tiles, zeros), j, wide, scale
        )
        for i in range(tiles):
            part = nn((scr[i, j] * factor).astype(jnp.bfloat16), grads(j))
            dv[i] = part if dv[i] is None else dv[i] + part
    put_lines(rect_ref, 0, (tops, totals), wide)
    for i in range(tiles):
        send_ref[pl.ds(i * wide, wide), :] = dv[i].astype(jnp.bfloat16)

    @pl.when(jnp.logical_not(late))
    def _():
        width = x_ref.shape[2]
        for place, part in enumerate(triple(rect_ref[...])):
            for piece in range(rect_ref.shape[1] // width):
                send_ref[pl.ds((place * tiles * GROUP + piece) * PAD, PAD), :] = jnp.concatenate(
                    [part[:, piece * width : (piece + 1) * width]] * (PAD // 8), axis=0
                )


def soft_rect_kernel(
    half, x_ref, recv_ref, recv_two_ref, lines_ref, far_ref, made_ref, rect_ref, scr
):
    late = later(half)
    tiles, wide, scale = soft_shape(half, x_ref)
    _, _, rect = soft_blocks(half, x_ref, (recv_ref, recv_two_ref))
    lines = block_stats(rect, scr, tiles, wide, scale)
    rect_ref[...] = jnp.zeros_like(rect_ref)
    put_lines(rect_ref, 0, lines, wide)
    both = [rect_joined(late, lines_ref, far_ref, lines, j, wide, scale) for j in range(tiles)]
    factors, deltas = zip(*both)
    dq, dk, dv = block_grads(rect, factors, deltas, scr, tiles, scale)
    for j in range(tiles):
        at = pl.ds(j * wide, wide)
        for place, made in enumerate((dq[j], dk[j], dv[j])):
            made_ref[place, at, :] = made


def sent_lines(ref, pieces, lines_ref):
    width = ref.shape[1]
    for piece in range(pieces):
        parts = [
            ref[pl.ds((place * pieces + piece) * PAD, PAD), :].astype(jnp.float32)[0:8]
            for place in range(3)
        ]
        lines_ref[:, pl.ds(piece * width, width)] = parts[0] + parts[1] + parts[2]


def causal_grads(half, slot, x_ref, lines_ref, far_ref, scr):
    tiles, wide, scale = soft_shape(half, x_ref)
    block = soft_blocks(half, x_ref, None)[slot]
    factors, deltas = [], []
    for j in range(tiles):
        mine = get_lines(lines_ref, 3 * slot, j, wide)
        factor, delta = joined(mine, get_lines(far_ref, 0, j, wide), later(half), scale)
        factors.append(factor)
        deltas.append(delta)
        for i in range(j + 1):
            scr[i, j] = jnp.exp((tile_scores(block, i, j, wide) - mine[0]) * scale)
    return block_grads(block, factors, deltas, scr, tiles, scale)


def soft_zero_kernel(half, x_ref, lines_ref, far_ref, made_ref, scr):
    tiles, wide, _ = soft_shape(half, x_ref)
    grads = causal_grads(half, 0, x_ref, lines_ref, far_ref, scr)
    for j in range(tiles):
        for place in range(3):
            made_ref[place, pl.ds(j * wide, wide), :] = grads[place][j]


def soft_value_kernel(half, x_ref, lines_ref, sent_ref, dv_ref, far_ref):
    sent_lines(sent_ref, half, far_ref)
    tiles, wide, scale = soft_shape(half, x_ref)
    zero, _, _ = soft_blocks(half, x_ref, None)
    dv = [None] * tiles
    for j in range(tiles):
        mine = get_lines(lines_ref, 0, j, wide)
        factor, _ = joined(mine, get_lines(far_ref, 0, j, wide), later(half), scale)
        for i in range(j + 1):
            weights = jnp.exp((tile_scores(zero, i, j, wide) - mine[0]) * scale)
            part = nn((weights * factor).astype(jnp.bfloat16), zero[3](j))
            dv[i] = part if dv[i] is None else dv[i] + part
    for i in range(tiles):
        dv_ref[pl.ds(i * wide, wide), :] = dv[i]


def soft_same_kernel(half, x_ref, lines_ref, rect_lines_ref, rect_ref, packed, dv_ref, scr):
    late = later(half)
    tiles, wide, _ = soft_shape(half, x_ref)
    rows = wide // GROUP
    grads = causal_grads(half, 1, x_ref, lines_ref, rect_lines_ref, scr)
    for j in range(tiles):
        at = pl.ds(j * wide, wide)
        for place in range(3):
            added = rect_ref[place, at, :]
            made = grads[place][j] + (
                jnp.where(late, added, 0.0) if place == 0 else jnp.where(late, 0.0, added)
            )
            packed[pl.ds(j * GROUP, GROUP), pl.ds(place * rows, rows), :] = made.astype(
                jnp.bfloat16
            ).reshape(GROUP, rows, made.shape[1])
            if place == 2:
                dv_ref[at, :] = made


def decay_lines(half, rows, x_ref):
    firsts = [
        x_ref[span, pl.ds(6 * rows + slot * PAD, PAD), :].astype(jnp.float32)
        for slot in range(2)
        for span in range(half)
    ]
    parts = [
        jnp.concatenate([block[place : place + 1] for block in firsts], axis=0)
        for place in range(3)
    ]
    first = lax.broadcasted_iota(jnp.int32, (rows, rows), 0)
    second = lax.broadcasted_iota(jnp.int32, (rows, rows), 1)
    ones = (first <= second).astype(jnp.float32).astype(jnp.bfloat16)
    sums = nn(jnp.concatenate(parts, axis=0).astype(jnp.bfloat16), ones)
    count = 2 * half
    return sums[:count] + sums[count : 2 * count] + sums[2 * count :]


def tables(lines):
    count, rows = lines.shape
    columns = jnp.transpose(lines)
    return [
        (lines[c : c + 1], columns[:, c : c + 1], lines[c : c + 1, rows - 1 : rows])
        for c in range(count)
    ]


def triangle(rows):
    first = lax.broadcasted_iota(jnp.int32, (rows, rows), 0)
    second = lax.broadcasted_iota(jnp.int32, (rows, rows), 1)
    return first >= second, first <= second


def gain_of(extra):
    wide = extra.astype(jnp.float32)
    return wide[3:4] + wide[4:5] + wide[5:6]


def lin_parts(x_ref, slot, span, rows):
    q, k, v = (
        x_ref[span, pl.ds((slot * 3 + place) * rows, rows), :] for place in range(3)
    )
    return q, k, v, x_ref[span, pl.ds(6 * rows + slot * PAD, PAD), :]


def lin_local_kernel(half, rows, *refs):
    steps, (x_ref, lines_ref, out_ref, states_ref, give_ref) = refs[:half], refs[half:]
    me = place_in(half)
    for step, ref in enumerate(steps):
        x_ref[jnp.bitwise_xor(me, step)] = ref[...]
    width = x_ref.shape[2]
    lines = decay_lines(half, rows, x_ref)
    lines_ref[...] = lines
    chunks = tables(lines)
    lower, _ = triangle(rows)
    for slot in range(2):
        state = None
        for span in range(half):
            _, k, v, _ = lin_parts(x_ref, slot, span, rows)
            _, col, finish = chunks[slot * half + span]
            decayed = (k.astype(jnp.float32) * jnp.exp(finish - col)).astype(jnp.bfloat16)
            if span:
                states_ref[slot, span] = state.astype(jnp.bfloat16)
                state = jnp.exp(finish) * state + tn(decayed, v)
            else:
                states_ref[slot, span] = jnp.zeros((width, width), jnp.bfloat16)
                state = tn(decayed, v)
        give_ref[1 - slot] = state.astype(jnp.bfloat16)
    for slot in range(2):
        for span in range(half):
            q, k, v, _ = lin_parts(x_ref, slot, span, rows)
            row, col, _ = chunks[slot * half + span]
            within = jnp.exp(jnp.where(lower, col - row, -1e30))
            out = nn((nt(q, k) * within).astype(jnp.bfloat16), v)
            if span:
                out = out + jnp.exp(col) * nn(q, states_ref[slot, span])
            out_ref[slot, span] = out


def lin_sums_kernel(
    half, rows, x_ref, lines_ref, soft_ref, zero_ref, same_ref, dv_ref, local_ref, given_ref,
    cot_ref, out_ref, sums_ref,
):
    late = later(half)
    chunks = tables(lines_ref[...])
    before = [jnp.where(late, jnp.zeros((1, 1), jnp.float32), -1e30)] * 2
    for span in range(half):
        at = pl.ds(span * rows, rows)
        inner, squares = None, None
        for slot in range(2):
            q, _, _, extra = lin_parts(x_ref, slot, span, rows)
            _, col, finish = chunks[slot * half + span]
            out = local_ref[slot, span] + jnp.exp(before[slot] + col) * nn(q, given_ref[slot])
            before[slot] = before[slot] + finish
            out_ref[slot, span] = out
            cot = soft_ref[span, pl.ds((slot * 4 + 3) * rows, rows), :].astype(jnp.float32)
            if slot == 0:
                cot = cot + zero_ref[at, :]
                cot = cot + jnp.where(late, 0.0, dv_ref[at, :].astype(jnp.float32))
            else:
                cot = cot + same_ref[at, :]
            scaled = gain_of(extra) * cot
            cot_ref[slot, span] = scaled
            inner = scaled * out if slot == 0 else inner + scaled * out
            squares = out * out if slot == 0 else squares + out * out
        sums_ref[pl.ds(span, 1), :] = jnp.sum(jnp.transpose(squares), axis=0, keepdims=True)
        sums_ref[pl.ds(half + span, 1), :] = jnp.sum(jnp.transpose(inner), axis=0, keepdims=True)


def lin_cot_kernel(
    half, rows, total_width, x_ref, lines_ref, cot_ref, out_ref, sums_ref, low_ref, state_ref
):
    mean = sums_ref[pl.ds(0, half), :] / total_width + epsilon
    root = jnp.sqrt(mean)
    inner = sums_ref[pl.ds(half, half), :] / (total_width * root * mean)
    scalars = jnp.transpose(jnp.concatenate([1.0 / root, inner], axis=0))
    chunks = tables(lines_ref[...])
    for slot in range(2):
        before = jnp.zeros((1, 1), jnp.float32)
        state = None
        for span in range(half):
            q, _, _, _ = lin_parts(x_ref, slot, span, rows)
            _, col, finish = chunks[slot * half + span]
            cotangent = (
                cot_ref[slot, span] * scalars[:, span : span + 1]
                - out_ref[slot, span] * scalars[:, half + span : half + span + 1]
            )
            low_cot = cotangent.astype(jnp.bfloat16)
            low_ref[slot, span] = low_cot
            decayed = (q.astype(jnp.float32) * jnp.exp(before + col)).astype(jnp.bfloat16)
            before = before + finish
            part = tn(decayed, low_cot)
            state = part if state is None else state + part
        state_ref[1 - slot] = state.astype(jnp.bfloat16)


def lin_own_kernel(half, rows, x_ref, lines_ref, low_ref, states_ref, given_ref, dq_ref, made_ref):
    chunks = tables(lines_ref[...])
    lower, upper = triangle(rows)
    late = later(half)
    for slot in range(2):
        given = jnp.where(late, given_ref[slot].astype(jnp.float32), 0.0)
        before = [jnp.zeros((1, 1), jnp.float32)]
        for span in range(half):
            before.append(before[-1] + chunks[slot * half + span][2])
        state = None
        for span in reversed(range(half)):
            q, k, v, _ = lin_parts(x_ref, slot, span, rows)
            row, col, finish = chunks[slot * half + span]
            within = jnp.exp(jnp.where(lower, col - row, -1e30))
            within_t = jnp.exp(jnp.where(upper, row - col, -1e30))
            low_cot = low_ref[slot, span]
            grad_pair = (nt(low_cot, v) * within).astype(jnp.bfloat16)
            grad_pair_t = (nt(v, low_cot) * within_t).astype(jnp.bfloat16)
            pair_t = (nt(k, q) * within_t).astype(jnp.bfloat16)
            leading = jnp.exp(col)
            trailing = jnp.exp(finish - col)
            carried = states_ref[slot, span].astype(jnp.float32) + jnp.exp(before[span]) * given
            dq = nn(grad_pair, k) + leading * nt(low_cot, carried.astype(jnp.bfloat16))
            dk = nn(grad_pair_t, q)
            dv = nn(pair_t, low_cot)
            decayed = (q.astype(jnp.float32) * leading).astype(jnp.bfloat16)
            part = tn(decayed, low_cot)
            if state is None:
                state = part
            else:
                low_state = state.astype(jnp.bfloat16)
                dk = dk + trailing * nt(v, low_state)
                dv = dv + trailing * nn(k, low_state)
                state = jnp.exp(finish) * state + part
            dq_ref[slot, span] = dq.astype(jnp.bfloat16)
            made_ref[slot, 0, span] = dk
            made_ref[slot, 1, span] = dv


def lin_finish_kernel(half, rows, x_ref, lines_ref, dq_ref, made_ref, state_ref, *refs):
    outs, packed = refs[:half], refs[half]
    chunks = tables(lines_ref[...])
    me = place_in(half)
    for slot in range(2):
        state = state_ref[slot]
        after = jnp.where(later(half), -1e30, jnp.zeros((1, 1), jnp.float32))
        for span in reversed(range(half)):
            _, k, v, _ = lin_parts(x_ref, slot, span, rows)
            _, col, finish = chunks[slot * half + span]
            trailing = jnp.exp(after + finish - col)
            after = after + finish
            dk = made_ref[slot, 0, span] + trailing * nt(v, state)
            dv = made_ref[slot, 1, span] + trailing * nn(k, state)
            packed[span, pl.ds(slot * 3 * rows, rows), :] = dq_ref[slot, span]
            packed[span, pl.ds((slot * 3 + 1) * rows, rows), :] = dk.astype(jnp.bfloat16)
            packed[span, pl.ds((slot * 3 + 2) * rows, rows), :] = dv.astype(jnp.bfloat16)
    for step, out in enumerate(outs):
        out[...] = packed[jnp.bitwise_xor(me, step)]


def pack_give_kernel(half, rect_ref, give_ref):
    give_ref[...] = jnp.where(later(half), rect_ref[1], rect_ref[0]).astype(jnp.bfloat16)


def pack_early_kernel(half, zero_ref, same_ref, dv_ref, given_ref, *outs):
    late, me = later(half), place_in(half)
    rows = same_ref.shape[1] // 3
    for step, out in enumerate(outs):
        span = jnp.bitwise_xor(me, step)
        at = pl.ds(pl.multiple_of(span * rows, rows), rows)
        given = given_ref[at, :].astype(jnp.float32)
        added = (
            jnp.where(late, given, 0.0),
            jnp.where(late, 0.0, given),
            jnp.where(late, 0.0, dv_ref[at, :].astype(jnp.float32)),
        )
        for place in range(3):
            out[pl.ds(place * rows, rows), :] = (zero_ref[place, at, :] + added[place]).astype(
                jnp.bfloat16
            )
        out[pl.ds(3 * rows, 3 * rows), :] = same_ref[span]


def call(name, kernel, out_shape, scratch, cost, *args, waits=()):
    count = len(args)
    places = {}
    if waits:
        places["in_specs"] = [pl.BlockSpec(memory_space=pltpu.VMEM)] * count + [
            pl.BlockSpec(memory_space=pl.ANY)
        ] * len(waits)

    def body(*refs):
        kernel(*refs[:count], *refs[count + len(waits) :])

    with jax.named_scope(name):
        return pl.pallas_call(
            body,
            out_shape=out_shape,
            scratch_shapes=scratch,
            name=name,
            compiler_params=pltpu.CompilerParams(vmem_limit_bytes=VMEM_BYTES[name == "pack_soft"]),
            cost_estimate=pl.CostEstimate(flops=cost, bytes_accessed=1024, transcendentals=0),
            **places,
        )(*args, *waits)


def by_halves(lin_q, lin_k, lin_v, lin_decay, norm_gain, soft_q, soft_k, soft_v, out_grad):
    rows, heads, width = lin_q.shape
    spans = lax.axis_size("ctx")
    half = spans // 2
    tokens = half * rows
    total_width = heads * lax.axis_size("head") * width
    low = lambda *s: jax.ShapeDtypeStruct(s, jnp.bfloat16)
    full = lambda *s: jax.ShapeDtypeStruct(s, jnp.float32)
    held = lambda *s: pltpu.VMEM(s, jnp.float32)
    bind = functools.partial
    tiles, wide = half // GROUP, GROUP * rows
    after = lax.optimization_barrier
    turned = held(rows * heads, width)
    scores = held(tiles, tiles, wide, wide)
    mine = (low(rows, heads, width),) * 3

    def moved(x, step):
        return lax.ppermute(x, "ctx", [(i, i ^ step) for i in range(spans)])

    def exchanged(parts):
        return [moved(part, step) if step else part for step, part in enumerate(parts)]

    soft_sent = call(
        "pack_soft", bind(pack_soft_kernel, half), (low(8 * rows, width),) * half, [turned] * 4,
        11960000000, soft_q, soft_k, soft_v, out_grad,
    )
    soft_got = exchanged(soft_sent)
    lin_sent = call(
        "pack_lin", bind(pack_lin_kernel, half), (low(6 * rows + 2 * PAD, width),) * half,
        [turned] * 3 + [held(6 * heads, width)], 5980000000,
        lin_q, lin_k, lin_v, lin_decay, norm_gain,
    )
    lin_got = exchanged(lin_sent)
    x, give = call(
        "soft_gather", bind(soft_gather_kernel, half),
        (low(half, 8 * rows, width), low(half, rows, width)), [], COST, *soft_got,
    )
    recv = moved(give, half)
    lines, give = call(
        "soft_stats", bind(soft_stats_kernel, half), (full(8, tokens), low(half, rows, width)),
        [scores], 5520000000, x,
    )
    recv_two = moved(give, half)
    far_lines = moved(lines, half)
    dv_give, first_lines = call(
        "soft_first", bind(soft_first_kernel, half), (low(tokens, width), full(8, tokens)),
        [scores], 13800000000, x, recv, lines, far_lines, waits=lin_got[1:3],
    )
    dv_given = moved(dv_give, half)
    lin_x, lin_lines, local_out, states, state = call(
        "lin_local", bind(lin_local_kernel, half, rows),
        (
            low(half, 6 * rows + 2 * PAD, width),
            full(2 * half, rows),
            full(2, half, rows, width),
            low(2, half, width, width),
            low(2, width, width),
        ),
        [], 7360000000, *lin_got, waits=(first_lines,),
    )
    state = moved(state, half)
    rect, rect_lines = call(
        "soft_rect", bind(soft_rect_kernel, half), (full(3, tokens, width), full(8, tokens)),
        [scores], 9200000000, x, recv, recv_two, lines, far_lines,
    )
    far_rect = moved(rect_lines, half)
    same, same_dv = call(
        "soft_same", bind(soft_same_kernel, half),
        (low(half, 3 * rows, width), full(tokens, width)), [scores], 4370000000,
        x, lines, rect_lines, rect,
    )
    zero_dv = call(
        "soft_value", bind(soft_value_kernel, half), full(tokens, width), [held(8, tokens)], COST,
        x, lines, dv_given,
    )
    cot, layer_out, sums = call(
        "lin_sums", bind(lin_sums_kernel, half, rows),
        (full(2, half, rows, width),) * 2 + (full(2 * half, rows),), [], COST,
        lin_x, lin_lines, x, zero_dv, same_dv, dv_given, local_out, state,
    )
    zero = call(
        "soft_zero", bind(soft_zero_kernel, half), full(3, tokens, width), [scores], 3680000000,
        x, lines, far_rect,
    )
    rect_then, sums = after((rect, sums))
    give = call("pack_give", bind(pack_give_kernel, half), low(tokens, width), [], 9200000000, rect_then)
    given = moved(give, half)
    steps = [("ctx", 1 << bit) for bit in range((half - 1).bit_length())]
    steps += [("head", 1 << bit) for bit in reversed(range((lax.axis_size("head") - 1).bit_length()))]
    for place, (axis, step) in enumerate(steps):
        sums = after(sums)
        if place == 3:
            given, sums = after((given, sums))
        count = lax.axis_size(axis)
        sums = sums + lax.ppermute(sums, axis, [(i, i ^ step) for i in range(count)])
    early = call(
        "pack_early", bind(pack_early_kernel, half), (low(6 * rows, width),) * half, [], 9200000000,
        zero, same, dv_given, given,
    )
    early = exchanged(early)
    low_cot, late_state = call(
        "lin_cot", bind(lin_cot_kernel, half, rows, total_width),
        (low(2, half, rows, width), low(2, width, width)), [], COST,
        lin_x, lin_lines, cot, layer_out, sums,
    )
    late_state = moved(late_state, half)
    lin_dq, lin_made = call(
        "lin_own", bind(lin_own_kernel, half, rows),
        (low(2, half, rows, width), full(2, 2, half, rows, width)), [], COST,
        lin_x, lin_lines, low_cot, states, state,
    )
    lin_made = call(
        "lin_finish", bind(lin_finish_kernel, half, rows), (low(6 * rows, width),) * half,
        [pltpu.VMEM((half, 6 * rows, width), jnp.bfloat16)], COST,
        lin_x, lin_lines, lin_dq, lin_made, late_state,
    )
    lin_back = exchanged(lin_made)
    soft_out = list(call("unpack_soft", bind(unpack_kernel, half), mine, [turned], 5060000000, *early[::-1]))
    lin_back[0], soft_out[0] = after((lin_back[0], soft_out[0]))
    lin_out = call("unpack_lin", bind(unpack_kernel, half), mine, [turned], COST, *lin_back[::-1])
    return (*lin_out, *soft_out)


def layers(
    lin_q,
    lin_k,
    lin_v,
    lin_decay,
    norm_gain,
    soft_q,
    soft_k,
    soft_v,
    out_grad,
    block_lists,
    block_counts,
):
    spans = lax.axis_size("ctx")
    if (
        lin_q.shape[0] == BLK
        and spans - 1 <= NSEL
        and lin_q.shape[1] == spans
        and spans >= 4
        and spans & (spans - 1) == 0
    ):
        return by_halves(
            lin_q, lin_k, lin_v, lin_decay, norm_gain, soft_q, soft_k, soft_v, out_grad
        )
    return local(
        lin_q,
        lin_k,
        lin_v,
        lin_decay,
        norm_gain,
        soft_q,
        soft_k,
        soft_v,
        out_grad,
        block_lists,
        block_counts,
    )


def solution(mesh):
    in_specs = (
        P("ctx", "head", None),
        P("ctx", "head", None),
        P("ctx", "head", None),
        P("head", "ctx"),
        P("head", None),
        P("ctx", "head", None),
        P("ctx", "head", None),
        P("ctx", "head", None),
        P("ctx", "head", None),
        P("ctx", None),
        P("ctx"),
    )
    out_specs = (
        P("ctx", "head", None),
        P("ctx", "head", None),
        P("ctx", "head", None),
        P("ctx", "head", None),
        P("ctx", "head", None),
        P("ctx", "head", None),
    )
    return jax.shard_map(layers, mesh=mesh, in_specs=in_specs, out_specs=out_specs, check_vma=False)
```

```python
import functools

import jax
import jax.numpy as jnp
from jax import lax
from jax.experimental import pallas as pl
from jax.experimental.pallas import tpu as pltpu
from jax.sharding import PartitionSpec as P

BLK = 128
NSEL = 16
PAD = 16
GROUP = 2
COST = 1024
VMEM_BYTES = (24 * 1024 * 1024, 56 * 1024 * 1024)


epsilon = 1e-05
exact_precision = lax.Precision.HIGHEST


def carried_in(part, axis, combine, identity, reverse):
    count = lax.axis_size(axis)
    place = lax.axis_index(axis)
    ahead = count - 1 - place if reverse else place
    gathered = jax.tree.map(lambda a: lax.all_gather(a, axis), part)
    state = jax.tree.map(lambda a, e: jnp.zeros_like(a) + jnp.asarray(e, a.dtype), part, identity)

    def one(lap, state):
        source = count - 1 - lap if reverse else lap
        return combine(
            state, jax.tree.map(lambda a: lax.dynamic_index_in_dim(a, source, 0, False), gathered)
        )

    return lax.fori_loop(0, ahead, one, state)


def decay_tables(decays):
    running = jnp.cumsum(decays, axis=1)
    finish = running[:, -1]
    length = decays.shape[1]
    below_diag = (jnp.arange(length)[:, None] >= jnp.arange(length)[None, :])[None]
    spread = running[:, :, None] - running[:, None, :]
    within = jnp.where(below_diag, jnp.exp(jnp.where(below_diag, spread, 0.0)), 0.0)
    return (jnp.exp(finish), jnp.exp(finish[:, None] - running), jnp.exp(running), within)


def chain_join(earlier, later):
    return (earlier[0] * later[0], later[0][:, None, None] * earlier[1] + later[1])


def sparse_grads(queries, grads_out, key_rows, value_rows, allowed):
    score_scale = queries.shape[-1] ** (-0.5)
    scores = (
        jnp.einsum("bqhd,bkhd->bhqk", queries, key_rows, preferred_element_type=jnp.float32)
        * score_scale
    )
    key_mask = allowed[:, None]
    scores = jnp.where(key_mask, scores, -1e30)
    row_max = jnp.max(scores, axis=-1, keepdims=True)
    weights = jnp.where(key_mask, jnp.exp(scores - row_max), 0.0)
    softmax_probs = weights / jnp.sum(weights, axis=-1, keepdims=True)
    rounded = softmax_probs.astype(jnp.bfloat16)
    outputs = jnp.einsum("bhqk,bkhd->bqhd", rounded, value_rows, preferred_element_type=jnp.float32)
    row_delta = jnp.sum(grads_out.astype(jnp.float32) * outputs, axis=-1)
    grad_probs = jnp.einsum(
        "bqhd,bkhd->bhqk", grads_out, value_rows, preferred_element_type=jnp.float32
    )
    grad_scores = (
        softmax_probs * (grad_probs - jnp.transpose(row_delta, (0, 2, 1))[..., None])
    ).astype(jnp.bfloat16)
    query_gradient = (
        jnp.einsum("bhqk,bkhd->bqhd", grad_scores, key_rows, preferred_element_type=jnp.float32)
        * score_scale
    )
    key_gradient = (
        jnp.einsum("bhqk,bqhd->bkhd", grad_scores, queries, preferred_element_type=jnp.float32)
        * score_scale
    )
    value_gradient = jnp.einsum(
        "bhqk,bqhd->bkhd", rounded, grads_out, preferred_element_type=jnp.float32
    )
    return (query_gradient, key_gradient, value_gradient)


def local(
    lin_q,
    lin_k,
    lin_v,
    lin_decay,
    norm_gain,
    soft_q,
    soft_k,
    soft_v,
    out_grad,
    block_lists,
    block_counts,
):
    tok_rows, heads_here, head_width = lin_q.shape
    blocks_here = tok_rows // BLK
    span_count = lax.axis_size("ctx")
    own_span = lax.axis_index("ctx")
    total_width = heads_here * lax.axis_size("head") * head_width
    complete_query = lin_q.astype(jnp.float32)
    complete_key = lin_k.astype(jnp.float32)
    complete_value = lin_v.astype(jnp.float32)
    carry_decay, trailing_decay, leading_decay, within = decay_tables(lin_decay)
    state_here = jnp.einsum(
        "boz,bor->ozr",
        complete_key * trailing_decay.T[:, :, None],
        complete_value,
        precision=exact_precision,
    )
    identity = (jnp.ones_like(carry_decay), jnp.zeros_like(state_here))
    incoming_state = carried_in((carry_decay, state_here), "ctx", chain_join, identity, False)[1]
    pair_weights = (
        jnp.einsum("thk,shk->hts", lin_q, lin_k, preferred_element_type=jnp.float32) * within
    )
    layer_out = jnp.einsum("hts,shv->thv", pair_weights, complete_value, precision=exact_precision)
    layer_out = layer_out + leading_decay.T[:, :, None] * jnp.einsum(
        "wfg,fgl->wfl", complete_query, incoming_state, precision=exact_precision
    )
    squares = lax.psum(jnp.sum(layer_out * layer_out, axis=(1, 2)), "head")
    root_mean = jnp.sqrt(squares / total_width + epsilon)
    norm_scale = norm_gain[None]
    all_lists, all_counts = (
        lax.all_gather(block_lists, "ctx", axis=0, tiled=True),
        lax.all_gather(block_counts, "ctx", axis=0, tiled=True),
    )
    entries = blocks_here * NSEL
    every_live = (
        jnp.arange(NSEL)[None, None, :] < all_counts.reshape(span_count, blocks_here)[:, :, None]
    ).reshape(span_count, entries)
    owner_hits = every_live & (all_lists // blocks_here == own_span)
    wanted_here = jnp.max(jnp.where(owner_hits, all_lists % blocks_here, -1), axis=1)
    my_live = jnp.arange(NSEL)[None, :] < block_counts[:, None]
    flat_owner = (block_lists // blocks_here).reshape(entries)
    flat_live = my_live.reshape(entries)
    key_blocks = soft_k.reshape(blocks_here, BLK, heads_here, head_width)
    value_blocks = soft_v.reshape(blocks_here, BLK, heads_here, head_width)
    picked = jnp.clip(wanted_here, 0, blocks_here - 1)
    present = (wanted_here >= 0)[:, None, None, None]
    nothing = jnp.zeros((), jnp.bfloat16)
    send_keys = jnp.where(present, key_blocks[picked], nothing)
    send_values = jnp.where(present, value_blocks[picked], nothing)
    got_keys, got_values = (
        lax.all_to_all(send_keys, "ctx", split_axis=0, concat_axis=0, tiled=True),
        lax.all_to_all(send_values, "ctx", split_axis=0, concat_axis=0, tiled=True),
    )
    listed_keys = jnp.take(got_keys, flat_owner, axis=0).reshape(
        blocks_here, NSEL * BLK, heads_here, head_width
    )
    listed_values = jnp.take(got_values, flat_owner, axis=0).reshape(
        blocks_here, NSEL * BLK, heads_here, head_width
    )
    key_rows = jnp.concatenate([key_blocks, listed_keys], axis=1)
    value_rows = jnp.concatenate([value_blocks, listed_values], axis=1)
    causal = jnp.arange(BLK)[:, None] >= jnp.arange(BLK)[None, :]
    remote_mask = jnp.broadcast_to(
        jnp.repeat(my_live, BLK, axis=1)[:, None, :], (blocks_here, BLK, NSEL * BLK)
    )
    allowed = jnp.concatenate(
        [jnp.broadcast_to(causal, (blocks_here, BLK, BLK)), remote_mask], axis=2
    )
    query_blocks = soft_q.reshape(blocks_here, BLK, heads_here, head_width)
    grad_blocks = out_grad.reshape(blocks_here, BLK, heads_here, head_width)
    query_gradient, key_gradient, value_gradient = sparse_grads(
        query_blocks, grad_blocks, key_rows, value_rows, allowed
    )
    soft_dq = query_gradient.reshape(tok_rows, heads_here, head_width).astype(jnp.bfloat16)
    routing = (
        flat_live[None, :] & (flat_owner[None, :] == jnp.arange(span_count)[:, None])
    ).astype(jnp.float32)
    remote_key = key_gradient[:, BLK:].reshape(entries, BLK, heads_here, head_width)
    remote_value = value_gradient[:, BLK:].reshape(entries, BLK, heads_here, head_width)
    part_key = jnp.einsum("oe,exhd->oxhd", routing, remote_key, precision=exact_precision).astype(
        jnp.bfloat16
    )
    part_value = jnp.einsum(
        "oe,exhd->oxhd", routing, remote_value, precision=exact_precision
    ).astype(jnp.bfloat16)
    back_key, back_value = (
        lax.all_to_all(part_key, "ctx", split_axis=0, concat_axis=0, tiled=True),
        lax.all_to_all(part_value, "ctx", split_axis=0, concat_axis=0, tiled=True),
    )
    placing = (wanted_here[:, None] == jnp.arange(blocks_here)[None, :]).astype(jnp.float32)
    added_key = jnp.einsum(
        "rb,rxhd->bxhd", placing, back_key.astype(jnp.float32), precision=exact_precision
    ).reshape(tok_rows, heads_here, head_width)
    added_value = jnp.einsum(
        "rb,rxhd->bxhd", placing, back_value.astype(jnp.float32), precision=exact_precision
    ).reshape(tok_rows, heads_here, head_width)
    soft_dk = (key_gradient[:, :BLK].reshape(tok_rows, heads_here, head_width) + added_key).astype(
        jnp.bfloat16
    )
    value_total = value_gradient[:, :BLK].reshape(tok_rows, heads_here, head_width) + added_value
    soft_dv = value_total.astype(jnp.bfloat16)
    cotangent = out_grad.astype(jnp.float32) + value_total
    inner_total = lax.psum(jnp.sum(norm_scale * cotangent * layer_out, axis=(1, 2)), "head")
    linear_cotangent = (
        norm_scale * cotangent / root_mean[:, None, None]
        - layer_out * (inner_total / (total_width * root_mean**3))[:, None, None]
    )
    reverse_state = carried_in(
        (
            carry_decay,
            jnp.einsum(
                "boz,bor->ozr",
                complete_query * leading_decay.T[:, :, None],
                linear_cotangent,
                precision=exact_precision,
            ),
        ),
        "ctx",
        chain_join,
        identity,
        True,
    )[1]
    grad_pair = (
        jnp.einsum("thv,shv->hts", linear_cotangent, complete_value, precision=exact_precision)
        * within
    )
    lin_dq = jnp.einsum("hts,shk->thk", grad_pair, complete_key, precision=exact_precision)
    lin_dq = lin_dq + leading_decay.T[:, :, None] * jnp.einsum(
        "fqs,qrs->fqr", linear_cotangent, incoming_state, precision=exact_precision
    )
    lin_dk = jnp.einsum("hts,thk->shk", grad_pair, complete_query, precision=exact_precision)
    lin_dk = lin_dk + trailing_decay.T[:, :, None] * jnp.einsum(
        "fut,ujt->fuj", complete_value, reverse_state, precision=exact_precision
    )
    lin_dv = jnp.einsum("hts,thv->shv", pair_weights, linear_cotangent, precision=exact_precision)
    lin_dv = lin_dv + trailing_decay.T[:, :, None] * jnp.einsum(
        "zpu,pux->zpx", complete_key, reverse_state, precision=exact_precision
    )
    return (
        lin_dq.astype(jnp.bfloat16),
        lin_dk.astype(jnp.bfloat16),
        lin_dv.astype(jnp.bfloat16),
        soft_dq,
        soft_dk,
        soft_dv,
    )


def triple(x):
    top = x.astype(jnp.bfloat16)
    rest = x - top.astype(jnp.float32)
    middle = rest.astype(jnp.bfloat16)
    low = (rest - middle.astype(jnp.float32)).astype(jnp.bfloat16)
    return top, middle, low


def nt(a, b):
    return lax.dot_general(a, b, (((1,), (1,)), ((), ())), preferred_element_type=jnp.float32)


def nn(a, b):
    return lax.dot_general(a, b, (((1,), (0,)), ((), ())), preferred_element_type=jnp.float32)


def tn(a, b):
    return lax.dot_general(a, b, (((0,), (0,)), ((), ())), preferred_element_type=jnp.float32)


def later(half):
    return lax.axis_index("ctx") >= half


def place_in(half):
    return lax.rem(lax.axis_index("ctx"), half)


def spread(source, scratch):
    rows, heads, width = source.shape
    scratch[...] = source[...].astype(jnp.float32).reshape(rows * heads, width)


def head_of(scratch, head, heads):
    return scratch[pl.ds(head, scratch.shape[0] // heads, stride=heads), :]


def put_heads(half, outs, scratch, first, second, rows, heads):
    late, me = later(half), place_in(half)
    for step, out in enumerate(outs):
        head = 2 * jnp.bitwise_xor(me, step)
        even, odd = head_of(scratch, head, heads), head_of(scratch, head + 1, heads)
        out[pl.ds(first * rows, rows), :] = jnp.where(late, odd, even).astype(jnp.bfloat16)
        out[pl.ds(second * rows, rows), :] = jnp.where(late, even, odd).astype(jnp.bfloat16)


def pack_soft_kernel(half, *refs):
    sources, outs, scratches = refs[:4], refs[4 : 4 + half], refs[4 + half :]
    rows, heads, _ = sources[0].shape
    for place, (source, scratch) in enumerate(zip(sources, scratches)):
        spread(source, scratch)
        put_heads(half, outs, scratch, place, 4 + place, rows, heads)


def pack_lin_kernel(half, *refs):
    sources, decay_ref, gain_ref, outs = refs[:3], refs[3], refs[4], refs[5 : 5 + half]
    scratches, parts_scr = refs[5 + half : 8 + half], refs[8 + half]
    late, me = later(half), place_in(half)
    rows, heads, width = sources[0].shape
    for place, (source, scratch) in enumerate(zip(sources, scratches)):
        spread(source, scratch)
        put_heads(half, outs, scratch, place, 3 + place, rows, heads)
    parts = [*triple(decay_ref[...]), *triple(gain_ref[...])]
    for place, part in enumerate(parts):
        parts_scr[pl.ds(place * heads, heads), :] = part.astype(jnp.float32)
    line = lax.broadcasted_iota(jnp.int32, (PAD, width), 0)
    for step, out in enumerate(outs):
        blocks = []
        for head in range(2):
            at = 2 * jnp.bitwise_xor(me, step) + head
            block = jnp.zeros((PAD, width), jnp.float32)
            for place in range(len(parts)):
                block = jnp.where(line == place, parts_scr[pl.ds(place * heads + at, 1), :], block)
            blocks.append(block)
        even, odd = blocks
        out[pl.ds(6 * rows, PAD), :] = jnp.where(late, odd, even).astype(jnp.bfloat16)
        out[pl.ds(6 * rows + PAD, PAD), :] = jnp.where(late, even, odd).astype(jnp.bfloat16)


def unpack_kernel(half, *refs):
    steps, outs, scratch = refs[:half][::-1], refs[half:-1], refs[-1]
    late, me = later(half), place_in(half)
    rows, heads, width = outs[0].shape
    for place, out in enumerate(outs):
        for step, ref in enumerate(steps):
            head = 2 * jnp.bitwise_xor(me, step)
            first = ref[pl.ds(place * rows, rows), :].astype(jnp.float32)
            second = ref[pl.ds((3 + place) * rows, rows), :].astype(jnp.float32)
            scratch[pl.ds(head, rows, stride=heads), :] = jnp.where(late, second, first)
            scratch[pl.ds(head + 1, rows, stride=heads), :] = jnp.where(late, first, second)
        out[...] = scratch[...].reshape(rows, heads, width).astype(jnp.bfloat16)


def soft_gather_kernel(half, *refs):
    steps, x_ref, give_ref = refs[:half], refs[half], refs[half + 1]
    late, me = later(half), place_in(half)
    rows = x_ref.shape[1] // 8
    for step, ref in enumerate(steps):
        source = jnp.bitwise_xor(me, step)
        x_ref[source] = ref[...]
        give_ref[source] = jnp.where(
            late, ref[pl.ds(0, rows), :], ref[pl.ds(rows, rows), :]
        )


def soft_blocks(half, x_ref, recv_ref):
    late = later(half)
    rows = x_ref.shape[1] // 8
    width = x_ref.shape[2]

    def own(slot, place):
        def take(tile):
            return x_ref[
                pl.ds(tile * GROUP, GROUP), pl.ds((slot * 4 + place) * rows, rows), :
            ].reshape(GROUP * rows, width)

        return take

    def other(place):
        def take(tile):
            return recv_ref[place][pl.ds(tile * GROUP, GROUP)].reshape(GROUP * rows, width)

        return take

    def either(if_late, if_early):
        return lambda tile: jnp.where(late, if_late(tile), if_early(tile))

    zero = (own(0, 0), own(0, 1), own(0, 2), own(0, 3), True)
    same = (own(1, 0), own(1, 1), own(1, 2), own(1, 3), True)
    rect = (
        either(own(1, 0), other(0)),
        either(other(0), own(1, 1)),
        either(other(1), own(1, 2)),
        either(own(1, 3), other(1)),
        False,
    )
    return zero, same, rect


def tile_scores(block, i, j, wide):
    q, k, _, _, causal = block
    scores = nt(k(i), q(j))
    if not causal or i < j:
        return scores
    key_at = lax.broadcasted_iota(jnp.int32, (wide, wide), 0)
    query_at = lax.broadcasted_iota(jnp.int32, (wide, wide), 1)
    return jnp.where(key_at <= query_at, scores, -1e30)


def tiles_of(block, j, tiles):
    return range(j + 1) if block[4] else range(tiles)


def block_stats(block, scr, tiles, wide, scale):
    tops, totals, dots = [], [], []
    _, _, v, g, _ = block
    for j in range(tiles):
        top = None
        for i in tiles_of(block, j, tiles):
            scores = tile_scores(block, i, j, wide)
            scr[i, j] = scores
            here = jnp.max(scores, axis=0, keepdims=True)
            top = here if top is None else jnp.maximum(top, here)
        total = jnp.zeros_like(top)
        out_t = None
        for i in tiles_of(block, j, tiles):
            weights = jnp.exp((scr[i, j] - top) * scale)
            scr[i, j] = weights
            total = total + jnp.sum(weights, axis=0, keepdims=True)
            part = tn(v(i), weights.astype(jnp.bfloat16))
            out_t = part if out_t is None else out_t + part
        grads_t = jnp.transpose(g(j).astype(jnp.float32))
        tops.append(top)
        totals.append(total)
        dots.append(jnp.sum(grads_t * out_t, axis=0, keepdims=True))
    return tops, totals, dots


def joined(mine, other, use, scale):
    top, total, dot = mine
    top_other, total_other, dot_other = other
    top_other = jnp.where(use, top_other, top)
    both = jnp.maximum(top, top_other)
    here = jnp.exp((top - both) * scale)
    there = jnp.where(use, jnp.exp((top_other - both) * scale), 0.0)
    inverse = 1.0 / (total * here + total_other * there)
    return here * inverse, (dot * here + dot_other * there) * inverse


def block_grads(block, factors, deltas, scr, tiles, scale):
    q, k, v, g, _ = block
    dq, dk, dv = [], [None] * tiles, [None] * tiles
    add = lambda total, part: part if total is None else total + part
    for j in range(tiles):
        dq_t = None
        for i in tiles_of(block, j, tiles):
            probs = scr[i, j] * factors[j]
            dv[i] = add(dv[i], nn(probs.astype(jnp.bfloat16), g(j)))
            grad_probs = nt(v(i), g(j))
            grad_scores = (probs * (grad_probs - deltas[j])).astype(jnp.bfloat16)
            dq_t = add(dq_t, tn(k(i), grad_scores))
            dk[i] = add(dk[i], nn(grad_scores, q(j)))
        dq.append(jnp.transpose(dq_t) * scale)
    return dq, [x * scale for x in dk], dv


def put_lines(ref, first, lines, wide):
    for place, row in enumerate(lines):
        for j, piece in enumerate(row):
            ref[pl.ds(first + place, 1), pl.ds(j * wide, wide)] = piece


def get_lines(ref, first, j, wide):
    return [ref[pl.ds(first + place, 1), pl.ds(j * wide, wide)] for place in range(3)]


def soft_shape(half, x_ref):
    rows, width = x_ref.shape[1] // 8, x_ref.shape[2]
    return half // GROUP, GROUP * rows, width**-0.5


def soft_stats_kernel(half, x_ref, lines_ref, give_ref, scr):
    late, rows = later(half), x_ref.shape[1] // 8
    for span in range(half):
        give_ref[span] = jnp.where(
            late, x_ref[span, pl.ds(3 * rows, rows), :], x_ref[span, pl.ds(2 * rows, rows), :]
        )
    tiles, wide, scale = soft_shape(half, x_ref)
    zero, same, _ = soft_blocks(half, x_ref, None)
    lines_ref[...] = jnp.zeros_like(lines_ref)
    put_lines(lines_ref, 0, block_stats(zero, scr, tiles, wide, scale), wide)
    put_lines(lines_ref, 3, block_stats(same, scr, tiles, wide, scale), wide)


def rect_joined(late, lines_ref, far_ref, lines, j, wide, scale):
    near, far = get_lines(lines_ref, 3, j, wide), get_lines(far_ref, 0, j, wide)
    other = [jnp.where(late, a, b) for a, b in zip(near, far)]
    return joined([line[j] for line in lines], other, True, scale)


def soft_first_kernel(half, x_ref, recv_ref, lines_ref, far_ref, send_ref, rect_ref, scr):
    late = later(half)
    tiles, wide, scale = soft_shape(half, x_ref)
    _, same, rect = soft_blocks(half, x_ref, (recv_ref, recv_ref))
    grads = same[3]
    tops, totals = [], []
    rect_ref[...] = jnp.zeros_like(rect_ref)
    dv = [None] * tiles
    for j in range(tiles):
        top = None
        for i in range(tiles):
            scores = tile_scores(rect, i, j, wide)
            scr[i, j] = scores
            here = jnp.max(scores, axis=0, keepdims=True)
            top = here if top is None else jnp.maximum(top, here)
        total = jnp.zeros_like(top)
        for i in range(tiles):
            weights = jnp.exp((scr[i, j] - top) * scale)
            scr[i, j] = weights
            total = total + jnp.sum(weights, axis=0, keepdims=True)
        tops.append(top)
        totals.append(total)
        zeros = [jnp.zeros_like(top)] * tiles
        factor, _ = rect_joined(
            late, lines_ref, far_ref, ([top] * tiles, [total] * tiles, zeros), j, wide, scale
        )
        for i in range(tiles):
            part = nn((scr[i, j] * factor).astype(jnp.bfloat16), grads(j))
            dv[i] = part if dv[i] is None else dv[i] + part
    put_lines(rect_ref, 0, (tops, totals), wide)
    for i in range(tiles):
        send_ref[pl.ds(i * wide, wide), :] = dv[i].astype(jnp.bfloat16)

    @pl.when(jnp.logical_not(late))
    def _():
        width = x_ref.shape[2]
        for place, part in enumerate(triple(rect_ref[...])):
            for piece in range(rect_ref.shape[1] // width):
                send_ref[pl.ds((place * tiles * GROUP + piece) * PAD, PAD), :] = jnp.concatenate(
                    [part[:, piece * width : (piece + 1) * width]] * (PAD // 8), axis=0
                )


def soft_rect_kernel(
    half, x_ref, recv_ref, recv_two_ref, lines_ref, far_ref, made_ref, rect_ref, scr
):
    late = later(half)
    tiles, wide, scale = soft_shape(half, x_ref)
    _, _, rect = soft_blocks(half, x_ref, (recv_ref, recv_two_ref))
    lines = block_stats(rect, scr, tiles, wide, scale)
    rect_ref[...] = jnp.zeros_like(rect_ref)
    put_lines(rect_ref, 0, lines, wide)
    both = [rect_joined(late, lines_ref, far_ref, lines, j, wide, scale) for j in range(tiles)]
    factors, deltas = zip(*both)
    dq, dk, dv = block_grads(rect, factors, deltas, scr, tiles, scale)
    for j in range(tiles):
        at = pl.ds(j * wide, wide)
        for place, made in enumerate((dq[j], dk[j], dv[j])):
            made_ref[place, at, :] = made


def sent_lines(ref, pieces, lines_ref):
    width = ref.shape[1]
    for piece in range(pieces):
        parts = [
            ref[pl.ds((place * pieces + piece) * PAD, PAD), :].astype(jnp.float32)[0:8]
            for place in range(3)
        ]
        lines_ref[:, pl.ds(piece * width, width)] = parts[0] + parts[1] + parts[2]


def causal_grads(half, slot, x_ref, lines_ref, far_ref, scr):
    tiles, wide, scale = soft_shape(half, x_ref)
    block = soft_blocks(half, x_ref, None)[slot]
    factors, deltas = [], []
    for j in range(tiles):
        mine = get_lines(lines_ref, 3 * slot, j, wide)
        factor, delta = joined(mine, get_lines(far_ref, 0, j, wide), later(half), scale)
        factors.append(factor)
        deltas.append(delta)
        for i in range(j + 1):
            scr[i, j] = jnp.exp((tile_scores(block, i, j, wide) - mine[0]) * scale)
    return block_grads(block, factors, deltas, scr, tiles, scale)


def soft_zero_kernel(half, x_ref, lines_ref, far_ref, made_ref, scr):
    tiles, wide, _ = soft_shape(half, x_ref)
    grads = causal_grads(half, 0, x_ref, lines_ref, far_ref, scr)
    for j in range(tiles):
        for place in range(3):
            made_ref[place, pl.ds(j * wide, wide), :] = grads[place][j]


def soft_value_kernel(half, x_ref, lines_ref, sent_ref, dv_ref, far_ref):
    sent_lines(sent_ref, half, far_ref)
    tiles, wide, scale = soft_shape(half, x_ref)
    zero, _, _ = soft_blocks(half, x_ref, None)
    dv = [None] * tiles
    for j in range(tiles):
        mine = get_lines(lines_ref, 0, j, wide)
        factor, _ = joined(mine, get_lines(far_ref, 0, j, wide), later(half), scale)
        for i in range(j + 1):
            weights = jnp.exp((tile_scores(zero, i, j, wide) - mine[0]) * scale)
            part = nn((weights * factor).astype(jnp.bfloat16), zero[3](j))
            dv[i] = part if dv[i] is None else dv[i] + part
    for i in range(tiles):
        dv_ref[pl.ds(i * wide, wide), :] = dv[i]


def soft_same_kernel(half, x_ref, lines_ref, rect_lines_ref, rect_ref, packed, dv_ref, scr):
    late = later(half)
    tiles, wide, _ = soft_shape(half, x_ref)
    rows = wide // GROUP
    grads = causal_grads(half, 1, x_ref, lines_ref, rect_lines_ref, scr)
    for j in range(tiles):
        at = pl.ds(j * wide, wide)
        for place in range(3):
            added = rect_ref[place, at, :]
            made = grads[place][j] + (
                jnp.where(late, added, 0.0) if place == 0 else jnp.where(late, 0.0, added)
            )
            packed[pl.ds(j * GROUP, GROUP), pl.ds(place * rows, rows), :] = made.astype(
                jnp.bfloat16
            ).reshape(GROUP, rows, made.shape[1])
            if place == 2:
                dv_ref[at, :] = made


def decay_lines(half, rows, x_ref):
    firsts = [
        x_ref[span, pl.ds(6 * rows + slot * PAD, PAD), :].astype(jnp.float32)
        for slot in range(2)
        for span in range(half)
    ]
    parts = [
        jnp.concatenate([block[place : place + 1] for block in firsts], axis=0)
        for place in range(3)
    ]
    first = lax.broadcasted_iota(jnp.int32, (rows, rows), 0)
    second = lax.broadcasted_iota(jnp.int32, (rows, rows), 1)
    ones = (first <= second).astype(jnp.float32).astype(jnp.bfloat16)
    sums = nn(jnp.concatenate(parts, axis=0).astype(jnp.bfloat16), ones)
    count = 2 * half
    return sums[:count] + sums[count : 2 * count] + sums[2 * count :]


def tables(lines):
    count, rows = lines.shape
    columns = jnp.transpose(lines)
    return [
        (lines[c : c + 1], columns[:, c : c + 1], lines[c : c + 1, rows - 1 : rows])
        for c in range(count)
    ]


def triangle(rows):
    first = lax.broadcasted_iota(jnp.int32, (rows, rows), 0)
    second = lax.broadcasted_iota(jnp.int32, (rows, rows), 1)
    return first >= second, first <= second


def gain_of(extra):
    wide = extra.astype(jnp.float32)
    return wide[3:4] + wide[4:5] + wide[5:6]


def lin_parts(x_ref, slot, span, rows):
    q, k, v = (
        x_ref[span, pl.ds((slot * 3 + place) * rows, rows), :] for place in range(3)
    )
    return q, k, v, x_ref[span, pl.ds(6 * rows + slot * PAD, PAD), :]


def lin_local_kernel(half, rows, *refs):
    steps, (x_ref, lines_ref, out_ref, states_ref, give_ref) = refs[:half], refs[half:]
    me = place_in(half)
    for step, ref in enumerate(steps):
        x_ref[jnp.bitwise_xor(me, step)] = ref[...]
    width = x_ref.shape[2]
    lines = decay_lines(half, rows, x_ref)
    lines_ref[...] = lines
    chunks = tables(lines)
    lower, _ = triangle(rows)
    for slot in range(2):
        state = None
        for span in range(half):
            _, k, v, _ = lin_parts(x_ref, slot, span, rows)
            _, col, finish = chunks[slot * half + span]
            decayed = (k.astype(jnp.float32) * jnp.exp(finish - col)).astype(jnp.bfloat16)
            if span:
                states_ref[slot, span] = state.astype(jnp.bfloat16)
                state = jnp.exp(finish) * state + tn(decayed, v)
            else:
                states_ref[slot, span] = jnp.zeros((width, width), jnp.bfloat16)
                state = tn(decayed, v)
        give_ref[1 - slot] = state.astype(jnp.bfloat16)
    for slot in range(2):
        for span in range(half):
            q, k, v, _ = lin_parts(x_ref, slot, span, rows)
            row, col, _ = chunks[slot * half + span]
            within = jnp.exp(jnp.where(lower, col - row, -1e30))
            out = nn((nt(q, k) * within).astype(jnp.bfloat16), v)
            if span:
                out = out + jnp.exp(col) * nn(q, states_ref[slot, span])
            out_ref[slot, span] = out


def lin_sums_kernel(
    half, rows, x_ref, lines_ref, soft_ref, zero_ref, same_ref, dv_ref, local_ref, given_ref,
    cot_ref, out_ref, sums_ref,
):
    late = later(half)
    chunks = tables(lines_ref[...])
    before = [jnp.where(late, jnp.zeros((1, 1), jnp.float32), -1e30)] * 2
    for span in range(half):
        at = pl.ds(span * rows, rows)
        inner, squares = None, None
        for slot in range(2):
            q, _, _, extra = lin_parts(x_ref, slot, span, rows)
            _, col, finish = chunks[slot * half + span]
            out = local_ref[slot, span] + jnp.exp(before[slot] + col) * nn(q, given_ref[slot])
            before[slot] = before[slot] + finish
            out_ref[slot, span] = out
            cot = soft_ref[span, pl.ds((slot * 4 + 3) * rows, rows), :].astype(jnp.float32)
            if slot == 0:
                cot = cot + zero_ref[at, :]
                cot = cot + jnp.where(late, 0.0, dv_ref[at, :].astype(jnp.float32))
            else:
                cot = cot + same_ref[at, :]
            scaled = gain_of(extra) * cot
            cot_ref[slot, span] = scaled
            inner = scaled * out if slot == 0 else inner + scaled * out
            squares = out * out if slot == 0 else squares + out * out
        sums_ref[pl.ds(span, 1), :] = jnp.sum(jnp.transpose(squares), axis=0, keepdims=True)
        sums_ref[pl.ds(half + span, 1), :] = jnp.sum(jnp.transpose(inner), axis=0, keepdims=True)


def lin_cot_kernel(
    half, rows, total_width, x_ref, lines_ref, cot_ref, out_ref, sums_ref, low_ref, state_ref
):
    mean = sums_ref[pl.ds(0, half), :] / total_width + epsilon
    root = jnp.sqrt(mean)
    inner = sums_ref[pl.ds(half, half), :] / (total_width * root * mean)
    scalars = jnp.transpose(jnp.concatenate([1.0 / root, inner], axis=0))
    chunks = tables(lines_ref[...])
    for slot in range(2):
        before = jnp.zeros((1, 1), jnp.float32)
        state = None
        for span in range(half):
            q, _, _, _ = lin_parts(x_ref, slot, span, rows)
            _, col, finish = chunks[slot * half + span]
            cotangent = (
                cot_ref[slot, span] * scalars[:, span : span + 1]
                - out_ref[slot, span] * scalars[:, half + span : half + span + 1]
            )
            low_cot = cotangent.astype(jnp.bfloat16)
            low_ref[slot, span] = low_cot
            decayed = (q.astype(jnp.float32) * jnp.exp(before + col)).astype(jnp.bfloat16)
            before = before + finish
            part = tn(decayed, low_cot)
            state = part if state is None else state + part
        state_ref[1 - slot] = state.astype(jnp.bfloat16)


def lin_own_kernel(half, rows, x_ref, lines_ref, low_ref, states_ref, given_ref, dq_ref, made_ref):
    chunks = tables(lines_ref[...])
    lower, upper = triangle(rows)
    late = later(half)
    for slot in range(2):
        given = jnp.where(late, given_ref[slot].astype(jnp.float32), 0.0)
        before = [jnp.zeros((1, 1), jnp.float32)]
        for span in range(half):
            before.append(before[-1] + chunks[slot * half + span][2])
        state = None
        for span in reversed(range(half)):
            q, k, v, _ = lin_parts(x_ref, slot, span, rows)
            row, col, finish = chunks[slot * half + span]
            within = jnp.exp(jnp.where(lower, col - row, -1e30))
            within_t = jnp.exp(jnp.where(upper, row - col, -1e30))
            low_cot = low_ref[slot, span]
            grad_pair = (nt(low_cot, v) * within).astype(jnp.bfloat16)
            grad_pair_t = (nt(v, low_cot) * within_t).astype(jnp.bfloat16)
            pair_t = (nt(k, q) * within_t).astype(jnp.bfloat16)
            leading = jnp.exp(col)
            trailing = jnp.exp(finish - col)
            carried = states_ref[slot, span].astype(jnp.float32) + jnp.exp(before[span]) * given
            dq = nn(grad_pair, k) + leading * nt(low_cot, carried.astype(jnp.bfloat16))
            dk = nn(grad_pair_t, q)
            dv = nn(pair_t, low_cot)
            decayed = (q.astype(jnp.float32) * leading).astype(jnp.bfloat16)
            part = tn(decayed, low_cot)
            if state is None:
                state = part
            else:
                low_state = state.astype(jnp.bfloat16)
                dk = dk + trailing * nt(v, low_state)
                dv = dv + trailing * nn(k, low_state)
                state = jnp.exp(finish) * state + part
            dq_ref[slot, span] = dq.astype(jnp.bfloat16)
            made_ref[slot, 0, span] = dk
            made_ref[slot, 1, span] = dv


def lin_finish_kernel(half, rows, x_ref, lines_ref, dq_ref, made_ref, state_ref, *refs):
    outs, packed = refs[:half], refs[half]
    chunks = tables(lines_ref[...])
    me = place_in(half)
    for slot in range(2):
        state = state_ref[slot]
        after = jnp.where(later(half), -1e30, jnp.zeros((1, 1), jnp.float32))
        for span in reversed(range(half)):
            _, k, v, _ = lin_parts(x_ref, slot, span, rows)
            _, col, finish = chunks[slot * half + span]
            trailing = jnp.exp(after + finish - col)
            after = after + finish
            dk = made_ref[slot, 0, span] + trailing * nt(v, state)
            dv = made_ref[slot, 1, span] + trailing * nn(k, state)
            packed[span, pl.ds(slot * 3 * rows, rows), :] = dq_ref[slot, span]
            packed[span, pl.ds((slot * 3 + 1) * rows, rows), :] = dk.astype(jnp.bfloat16)
            packed[span, pl.ds((slot * 3 + 2) * rows, rows), :] = dv.astype(jnp.bfloat16)
    for step, out in enumerate(outs):
        out[...] = packed[jnp.bitwise_xor(me, step)]


def pack_give_kernel(half, rect_ref, give_ref):
    give_ref[...] = jnp.where(later(half), rect_ref[1], rect_ref[0]).astype(jnp.bfloat16)


def pack_early_kernel(half, zero_ref, same_ref, dv_ref, given_ref, *outs):
    late, me = later(half), place_in(half)
    rows = same_ref.shape[1] // 3
    for step, out in enumerate(outs):
        span = jnp.bitwise_xor(me, step)
        at = pl.ds(pl.multiple_of(span * rows, rows), rows)
        given = given_ref[at, :].astype(jnp.float32)
        added = (
            jnp.where(late, given, 0.0),
            jnp.where(late, 0.0, given),
            jnp.where(late, 0.0, dv_ref[at, :].astype(jnp.float32)),
        )
        for place in range(3):
            out[pl.ds(place * rows, rows), :] = (zero_ref[place, at, :] + added[place]).astype(
                jnp.bfloat16
            )
        out[pl.ds(3 * rows, 3 * rows), :] = same_ref[span]


def call(name, kernel, out_shape, scratch, cost, *args, waits=()):
    count = len(args)
    places = {}
    if waits:
        places["in_specs"] = [pl.BlockSpec(memory_space=pltpu.VMEM)] * count + [
            pl.BlockSpec(memory_space=pl.ANY)
        ] * len(waits)

    def body(*refs):
        kernel(*refs[:count], *refs[count + len(waits) :])

    with jax.named_scope(name):
        return pl.pallas_call(
            body,
            out_shape=out_shape,
            scratch_shapes=scratch,
            name=name,
            compiler_params=pltpu.CompilerParams(vmem_limit_bytes=VMEM_BYTES[name == "pack_soft"]),
            cost_estimate=pl.CostEstimate(flops=cost, bytes_accessed=1024, transcendentals=0),
            **places,
        )(*args, *waits)


def by_halves(lin_q, lin_k, lin_v, lin_decay, norm_gain, soft_q, soft_k, soft_v, out_grad):
    rows, heads, width = lin_q.shape
    spans = lax.axis_size("ctx")
    half = spans // 2
    tokens = half * rows
    total_width = heads * lax.axis_size("head") * width
    low = lambda *s: jax.ShapeDtypeStruct(s, jnp.bfloat16)
    full = lambda *s: jax.ShapeDtypeStruct(s, jnp.float32)
    held = lambda *s: pltpu.VMEM(s, jnp.float32)
    bind = functools.partial
    tiles, wide = half // GROUP, GROUP * rows
    after = lax.optimization_barrier
    turned = held(rows * heads, width)
    scores = held(tiles, tiles, wide, wide)
    mine = (low(rows, heads, width),) * 3

    def moved(x, step):
        return lax.ppermute(x, "ctx", [(i, i ^ step) for i in range(spans)])

    def exchanged(parts):
        return [moved(part, step) if step else part for step, part in enumerate(parts)]

    soft_sent = call(
        "pack_soft", bind(pack_soft_kernel, half), (low(8 * rows, width),) * half, [turned] * 4,
        11960000000, soft_q, soft_k, soft_v, out_grad,
    )
    soft_got = exchanged(soft_sent)
    lin_sent = call(
        "pack_lin", bind(pack_lin_kernel, half), (low(6 * rows + 2 * PAD, width),) * half,
        [turned] * 3 + [held(6 * heads, width)], 5980000000,
        lin_q, lin_k, lin_v, lin_decay, norm_gain,
    )
    lin_got = exchanged(lin_sent)
    x, give = call(
        "soft_gather", bind(soft_gather_kernel, half),
        (low(half, 8 * rows, width), low(half, rows, width)), [], COST, *soft_got,
    )
    recv = moved(give, half)
    lines, give = call(
        "soft_stats", bind(soft_stats_kernel, half), (full(8, tokens), low(half, rows, width)),
        [scores], 5520000000, x,
    )
    recv_two = moved(give, half)
    far_lines = moved(lines, half)
    dv_give, first_lines = call(
        "soft_first", bind(soft_first_kernel, half), (low(tokens, width), full(8, tokens)),
        [scores], 13800000000, x, recv, lines, far_lines, waits=lin_got[1:3],
    )
    dv_given = moved(dv_give, half)
    lin_x, lin_lines, local_out, states, state = call(
        "lin_local", bind(lin_local_kernel, half, rows),
        (
            low(half, 6 * rows + 2 * PAD, width),
            full(2 * half, rows),
            full(2, half, rows, width),
            low(2, half, width, width),
            low(2, width, width),
        ),
        [], 7360000000, *lin_got, waits=(first_lines,),
    )
    state = moved(state, half)
    rect, rect_lines = call(
        "soft_rect", bind(soft_rect_kernel, half), (full(3, tokens, width), full(8, tokens)),
        [scores], 9200000000, x, recv, recv_two, lines, far_lines,
    )
    far_rect = moved(rect_lines, half)
    same, same_dv = call(
        "soft_same", bind(soft_same_kernel, half),
        (low(half, 3 * rows, width), full(tokens, width)), [scores], 4370000000,
        x, lines, rect_lines, rect,
    )
    zero_dv = call(
        "soft_value", bind(soft_value_kernel, half), full(tokens, width), [held(8, tokens)], COST,
        x, lines, dv_given,
    )
    cot, layer_out, sums = call(
        "lin_sums", bind(lin_sums_kernel, half, rows),
        (full(2, half, rows, width),) * 2 + (full(2 * half, rows),), [], COST,
        lin_x, lin_lines, x, zero_dv, same_dv, dv_given, local_out, state,
    )
    zero = call(
        "soft_zero", bind(soft_zero_kernel, half), full(3, tokens, width), [scores], 3680000000,
        x, lines, far_rect,
    )
    rect_then, sums = after((rect, sums))
    give = call("pack_give", bind(pack_give_kernel, half), low(tokens, width), [], 9200000000, rect_then)
    given = moved(give, half)
    steps = [("ctx", 1 << bit) for bit in range((half - 1).bit_length())]
    steps += [("head", 1 << bit) for bit in reversed(range((lax.axis_size("head") - 1).bit_length()))]
    for place, (axis, step) in enumerate(steps):
        sums = after(sums)
        if place == 2:
            given, sums = after((given, sums))
        count = lax.axis_size(axis)
        sums = sums + lax.ppermute(sums, axis, [(i, i ^ step) for i in range(count)])
    early = call(
        "pack_early", bind(pack_early_kernel, half), (low(6 * rows, width),) * half, [], 9200000000,
        zero, same, dv_given, given,
    )
    early = exchanged(early)
    low_cot, late_state = call(
        "lin_cot", bind(lin_cot_kernel, half, rows, total_width),
        (low(2, half, rows, width), low(2, width, width)), [], COST,
        lin_x, lin_lines, cot, layer_out, sums,
    )
    late_state = moved(late_state, half)
    lin_dq, lin_made = call(
        "lin_own", bind(lin_own_kernel, half, rows),
        (low(2, half, rows, width), full(2, 2, half, rows, width)), [], COST,
        lin_x, lin_lines, low_cot, states, state,
    )
    lin_made = call(
        "lin_finish", bind(lin_finish_kernel, half, rows), (low(6 * rows, width),) * half,
        [pltpu.VMEM((half, 6 * rows, width), jnp.bfloat16)], COST,
        lin_x, lin_lines, lin_dq, lin_made, late_state,
    )
    lin_back = exchanged(lin_made)
    soft_out = list(call("unpack_soft", bind(unpack_kernel, half), mine, [turned], 5060000000, *early[::-1]))
    lin_back[0], soft_out[0] = after((lin_back[0], soft_out[0]))
    lin_out = call("unpack_lin", bind(unpack_kernel, half), mine, [turned], COST, *lin_back[::-1])
    return (*lin_out, *soft_out)


def layers(
    lin_q,
    lin_k,
    lin_v,
    lin_decay,
    norm_gain,
    soft_q,
    soft_k,
    soft_v,
    out_grad,
    block_lists,
    block_counts,
):
    spans = lax.axis_size("ctx")
    if (
        lin_q.shape[0] == BLK
        and spans - 1 <= NSEL
        and lin_q.shape[1] == spans
        and spans >= 4
        and spans & (spans - 1) == 0
    ):
        return by_halves(
            lin_q, lin_k, lin_v, lin_decay, norm_gain, soft_q, soft_k, soft_v, out_grad
        )
    return local(
        lin_q,
        lin_k,
        lin_v,
        lin_decay,
        norm_gain,
        soft_q,
        soft_k,
        soft_v,
        out_grad,
        block_lists,
        block_counts,
    )


def solution(mesh):
    in_specs = (
        P("ctx", "head", None),
        P("ctx", "head", None),
        P("ctx", "head", None),
        P("head", "ctx"),
        P("head", None),
        P("ctx", "head", None),
        P("ctx", "head", None),
        P("ctx", "head", None),
        P("ctx", "head", None),
        P("ctx", None),
        P("ctx"),
    )
    out_specs = (
        P("ctx", "head", None),
        P("ctx", "head", None),
        P("ctx", "head", None),
        P("ctx", "head", None),
        P("ctx", "head", None),
        P("ctx", "head", None),
    )
    return jax.shard_map(layers, mesh=mesh, in_specs=in_specs, out_specs=out_specs, check_vma=False)
```
